512 devices in a mesh: gx: 16 (over z, core), yz: 32 (over x, y).
Axes of the slice: x: 4, y: 8, z: 8, core: 2. Of those that a mesh axis runs over, the one named last changes fastest.
Arguments:
- vorticity: bfloat16 [3, 512, 256, 512], P(None, 'gx', 'yz'), may hold values from -6 to 6
- velocity: bfloat16 [3, 512, 256, 512], P(None, 'gx', 'yz'), may hold values from -6 to 6
- blocks: int32 [512, 128], P(('gx', 'yz')), may hold values from 0 to 127, as said below
- counts: int32 [512], P(('gx', 'yz')), may hold values from 32 to 128, as said below
Outputs:
- lamb_vector: bfloat16 [3, 512, 256, 512], P(None, 'gx', 'yz')
The draws below stay inside these ranges and needn't reach their ends.
Inputs may be any that keep to these rules, and one draw needn't show every extreme that they name: `blocks`: the first counts[x] entries of row x are different block numbers. `counts`: some x plane uses all 128 entries.
All inputs are finite; a program needn't handle non-finite values.
Results may differ from the reference program's by a relative error of at most 0.001.
Values sent between devices are 32-bit elements; how exact they have to be, the bound alone decides.
No kernel may reach another device: no remote copies, remote signals or barrier semaphores. Data moves between devices by JAX's collectives and lax.ppermute only.
A program may use at most 128 MiB of HBM per device.

```python
import jax
import jax.numpy as jnp
from jax import lax

NZ = 512
BY = 8
BZ = 128
MAXB = 128
NX = 512
NY = 256
NBLK = 128


def draw_blocks(key, part):
    key = jax.random.fold_in(key, 11)
    row_keys = jax.random.split(key, NX)
    shuffled = jax.vmap(lambda row_key: jax.random.permutation(row_key, NBLK))(row_keys)
    return shuffled[:, :MAXB].astype(jnp.int32)


def draw_counts(key, part):
    key = jax.random.fold_in(key, 12)
    count_key, row_key = jax.random.split(key)
    drawn = jax.random.randint(count_key, (NX,), MAXB // 4, MAXB + 1)
    fullest = jax.random.randint(row_key, (), 0, NX)
    return jnp.where(jnp.arange(NX) == fullest, MAXB, drawn).astype(jnp.int32)


def shard_levels(stream_key, extent, pieces, least, top_value):
    factor_of = 1.0
    for position, parts in pieces:
        heights = jax.random.uniform(jax.random.fold_in(jax.random.fold_in(stream_key, 6), position), (parts,), jnp.float32, least / len(pieces), top_value / len(pieces))
        factor_of = factor_of * jnp.repeat(jnp.exp(heights), extent[position] // parts).reshape((-1,) + (1,) * (len(extent) - 1 - position))
    return factor_of


def bell_draw(rng, shape, scale, reach, pieces=(), kind=jnp.bfloat16):
    array = scale * jax.random.normal(rng, shape, jnp.float32)
    if pieces:
        array = array * shard_levels(rng, shape, pieces, -0.22, 0.18)
    return jnp.clip(array, -reach, reach).astype(kind)


def setup_inputs(seed: int = 0) -> dict:
    keys = jax.random.split(jax.random.key(seed), 5)
    return {
        "vorticity": bell_draw(keys[0], (3, NX, NY, NZ), 1.0, 6.0, ((1, 16), (2, 32))),
        "velocity": bell_draw(keys[1], (3, NX, NY, NZ), 1.0, 6.0, ((1, 16), (2, 32))),
        "blocks": draw_blocks(jax.random.fold_in(keys[4], 71), 0),
        "counts": draw_counts(jax.random.fold_in(keys[4], 71), 0),
    }


root_half = 0.7071067811865476


def haar_forward(values, dimension):
    length = values.shape[dimension]
    if length == 1:
        return values
    new_shape = values.shape[:dimension] + (length // 2, 2) + values.shape[dimension + 1:]
    paired = values.reshape(new_shape)
    even_part = lax.index_in_dim(paired, 0, dimension + 1, keepdims=False)
    odd_part = lax.index_in_dim(paired, 1, dimension + 1, keepdims=False)
    coarse_part = haar_forward((even_part + odd_part) * root_half, dimension)
    detail_part = (even_part - odd_part) * root_half
    return jnp.stack([coarse_part, detail_part], axis=dimension + 1).reshape(values.shape)


def haar_inverse(values, dimension):
    length = values.shape[dimension]
    if length == 1:
        return values
    new_shape = values.shape[:dimension] + (length // 2, 2) + values.shape[dimension + 1:]
    paired = values.reshape(new_shape)
    coarse_part = lax.index_in_dim(paired, 0, dimension + 1, keepdims=False)
    detail_part = lax.index_in_dim(paired, 1, dimension + 1, keepdims=False)
    coarse_part = haar_inverse(coarse_part, dimension)
    even_part = (coarse_part + detail_part) * root_half
    odd_part = (coarse_part - detail_part) * root_half
    return jnp.stack([even_part, odd_part], axis=dimension + 1).reshape(values.shape)


def kept_blocks(block_rows, lengths, nblocks):
    in_use = jnp.arange(block_rows.shape[1], dtype=jnp.int32)[None, :] < lengths[:, None]
    matches = (block_rows[:, :, None] == jnp.arange(nblocks, dtype=jnp.int32)[None, None, :]) & in_use[:, :, None]
    return jnp.any(matches, axis=1).astype(jnp.float32)


def spread_blocks(kept, tall, wide):
    rows_count, across, down = kept.shape
    grown = jnp.broadcast_to(kept[:, :, None, :, None], (rows_count, across, tall, down, wide))
    return grown.reshape(rows_count, across * tall, down * wide)


def cross_product(left, right):
    return jnp.stack([left[1] * right[2] - left[2] * right[1],
                      left[2] * right[0] - left[0] * right[2],
                      left[0] * right[1] - left[1] * right[0]])


def reference(vorticity, velocity, blocks, counts):
    kept = kept_blocks(blocks, counts, NBLK).reshape(NX, NY // BY, NZ // BZ)
    mask = spread_blocks(kept, BY, BZ)

    def coherent(component):
        coeff = component.astype(jnp.float32)
        for dimension in range(3):
            coeff = haar_forward(coeff, dimension)
        coeff = coeff * mask
        for dimension in (2, 1, 0):
            coeff = haar_inverse(coeff, dimension)
        return coeff

    smooth = lax.map(coherent, vorticity)
    return cross_product(smooth, velocity.astype(jnp.float32)).astype(jnp.bfloat16)
```

```python
import jax
import jax.numpy as jnp
from jax import lax
from jax.experimental import pallas as pl
from jax.experimental.pallas import tpu as pltpu
from jax.sharding import PartitionSpec as P


BY = 8
BZ = 128
ZB = 4
CHUNKS = 12
ROWS = 13
EXTRA = 12
CORNER = 48
SLICE = 16
HALF = 64
OWN_KEPT = 48
ALL_KEPT = 64
LINE_KEPT = 52
PACKED = 16
F32 = jnp.float32
BF16 = jnp.bfloat16


def iota(shape, dimension):
    return lax.broadcasted_iota(jnp.int32, shape, dimension)


def sign_of(place, cell, length):
    span = jnp.where(place == 0, length, 2 * (place & -place))
    sign = jnp.where((cell < place) | (place == 0), 1.0, -1.0)
    return jnp.where((cell ^ place) < span, sign, 0.0)


def weight_of(place, cell, length):
    span = jnp.where(place == 0, length, 2 * (place & -place))
    return sign_of(place, cell, length) / span.astype(F32)


def mix_table(wide):
    coarse, block = iota((wide, BZ), 1), iota((wide, BZ), 0) // BZ
    table = weight_of(jnp.minimum(coarse, ZB - 1), block, ZB)
    table = table - jnp.where(coarse == block, 1.0, 0.0)
    return (jnp.where(coarse < ZB, table, 0.0) / BZ).astype(BF16)


def unmix_table(wide):
    block, coarse = iota((wide, BZ), 1), iota((wide, BZ), 0) // BZ
    table = sign_of(coarse, jnp.minimum(block, ZB - 1), ZB)
    table = table - jnp.where(coarse == block, 1.0, 0.0)
    return (jnp.where(block < ZB, table, 0.0) / BZ).astype(BF16)


def halves(value):
    high = value.astype(BF16)
    low = (value - high.astype(F32)).astype(BF16)
    return high, low


def left_product(table, value):
    high, low = halves(value)
    return jnp.dot(table, high, preferred_element_type=F32) + jnp.dot(
        table, low, preferred_element_type=F32
    )


def right_product(value, table):
    high, low = halves(value)
    return jnp.dot(high, table, preferred_element_type=F32) + jnp.dot(
        low, table, preferred_element_type=F32
    )


def remix(value, table):
    shift = right_product(value, table)
    return jnp.concatenate(
        [value[:, zb * BZ : (zb + 1) * BZ] + shift[:, zb : zb + 1] for zb in range(ZB)], axis=1
    )


def forward_levels(values):
    count = len(values)
    result = [None] * count
    step = 1
    while step < count:
        for place in range(step, count, 2 * step):
            low, high = values[place - step], values[place]
            result[place] = (low - high) * 0.5
            values[place - step] = (low + high) * 0.5
        step *= 2
    result[0] = values[0]
    return result


def inverse_levels(values):
    count = len(values)
    values = list(values)
    step = count // 2
    while step >= 1:
        for place in range(step, count, 2 * step):
            mean, detail = values[place - step], values[place]
            values[place - step] = mean + detail
            values[place] = mean - detail
        step //= 2
    return values


def spread_table(part, wide):
    cell, lane = iota((wide, BZ), 0), iota((wide, BZ), 1)
    return jnp.where(lane == part * SLICE + cell % SLICE, 1.0, 0.0).astype(BF16)


def gather_table(part, wide):
    lane, cell = iota((BZ, wide), 0), iota((BZ, wide), 1)
    return jnp.where(lane == part * SLICE + cell % SLICE, 1.0, 0.0).astype(BF16)


def pick_table(first, wide):
    lane, cell = iota((BZ, wide), 0), iota((BZ, wide), 1)
    return jnp.where(lane == first + cell // BZ, 1.0, 0.0).astype(BF16)


def head_kernel(counts_hbm, blocks_hbm, vort_hbm, send, line, own, counts, blocks, vort, sems):
    parts, cells, wide = vort.shape
    planes = cells // BY
    copies = [
        pltpu.make_async_copy(vort_hbm.at[c], vort.at[c], sems.at[c]) for c in range(parts)
    ]
    copies.append(pltpu.make_async_copy(blocks_hbm, blocks, sems.at[parts]))
    copies.append(pltpu.make_async_copy(counts_hbm, counts, sems.at[parts + 1]))
    for copy in copies:
        copy.start()
    row, column = iota((planes + BY, cells), 0), iota((planes + BY, cells), 1)
    fine = jnp.where(row - planes == column % BY, 1.0, 0.0) - 1.0 / BY
    table = jnp.where(
        row < planes,
        weight_of(jnp.minimum(row, planes - 1), column // BY, planes) / BY,
        fine / planes,
    ).astype(BF16)
    mix = mix_table(wide)
    target, cell = iota((planes, wide), 0), iota((planes, wide), 1)
    extra = jnp.zeros((planes, BZ), F32)
    for c in range(parts):
        copies[c].wait()
        rows = remix(jnp.dot(table, vort[c], preferred_element_type=F32), mix)
        for zb in range(ZB):
            chunk = c * ZB + zb
            part = rows[:, zb * BZ : (zb + 1) * BZ]
            send[pl.ds(chunk, planes, stride=ROWS), :] = part[0:planes]
            line[chunk * BY : (chunk + 1) * BY, :] = part[planes : planes + BY]
        corner = jnp.where(cell // SLICE == target, rows[0:1], 0.0)
        extra = extra + right_product(corner, spread_table(c, wide))
    copies[parts].wait()
    copies[parts + 1].wait()
    nblocks = blocks.shape[1]
    square = (nblocks, nblocks)
    listed = (blocks[...] == iota(square, 0)) & (iota(square, 1) < counts[0])
    kept = lax.dot_general(
        jnp.ones((planes, nblocks), BF16),
        jnp.where(listed, 1.0, 0.0).astype(BF16),
        (((1,), (1,)), ((), ())),
        preferred_element_type=F32,
    )
    kept = jnp.minimum(kept, 1.0)
    own[...] = kept[0:8]
    target, block = iota((planes, nblocks), 0), iota((planes, nblocks), 1)
    block_row, lane = iota(square, 0), iota(square, 1)
    mine = jnp.where(block // ZB == target, kept, 0.0).astype(BF16)
    slot = jnp.where(lane == OWN_KEPT + block_row % ZB, 1.0, 0.0).astype(BF16)
    extra = extra + jnp.dot(mine, slot, preferred_element_type=F32)
    every = jnp.where(block % ZB == target * SLICE // BZ, kept, 0.0).astype(BF16)
    slot = jnp.where(lane == ALL_KEPT + block_row // ZB, 1.0, 0.0).astype(BF16)
    extra = extra + jnp.dot(every, slot, preferred_element_type=F32)
    send[pl.ds(EXTRA, planes, stride=ROWS), :] = extra


def level_tables(length):
    square = (length, length)
    forward = weight_of(iota(square, 0), iota(square, 1), length).astype(BF16)
    inverse = sign_of(iota(square, 1), iota(square, 0), length).astype(BF16)
    return forward, inverse


def plane_kernel(own, recv, after, back, corner):
    del after
    planes = recv.shape[0] // ROWS
    forward, inverse = level_tables(planes)
    spread = jnp.where(iota((planes, BZ), 1) // ZB == iota((planes, BZ), 0), own[0:1], 0.0)
    pick = jnp.where(iota((BZ, ZB * BZ), 0) % ZB == iota((BZ, ZB * BZ), 1) // BZ, 1.0, 0.0)
    mask = jnp.dot(spread.astype(BF16), pick.astype(BF16), preferred_element_type=F32)
    extra = recv[pl.ds(EXTRA, planes, stride=ROWS), :]
    lane = iota((PACKED, BZ), 1)
    row = iota((PACKED, BZ), 0)
    heads = extra[0:1]
    low = jnp.sum(jnp.where(lane == ALL_KEPT + row, heads, 0.0), axis=1, keepdims=True)
    high = jnp.sum(jnp.where(lane == ALL_KEPT + PACKED + row, heads, 0.0), axis=1, keepdims=True)
    levels = left_product(forward, jnp.where(iota((planes, BZ), 1) < CORNER, extra, 0.0))
    packed = levels[0:PACKED] + pltpu.roll(levels[PACKED:planes], HALF, 1)
    packed = jnp.where(lane == CORNER, low, packed)
    packed = jnp.where(lane == HALF + CORNER, high, packed)
    shifted = pltpu.roll(jnp.broadcast_to(heads, (PACKED, BZ)), LINE_KEPT - OWN_KEPT, 1)
    packed = jnp.where((lane >= LINE_KEPT) & (lane < LINE_KEPT + ZB), shifted, packed)
    for g in range(corner.shape[0]):
        corner[g] = packed
    for c in range(3):
        data = jnp.concatenate(
            [recv[pl.ds(c * ZB + zb, planes, stride=ROWS), :] for zb in range(ZB)], axis=1
        )
        data = left_product(inverse, left_product(forward, data) * mask)
        for zb in range(ZB):
            back[pl.ds(c * ZB + zb, planes, stride=ROWS), :] = data[:, zb * BZ : (zb + 1) * BZ]


def corner_kernel(place, gathered, back_in, after, back):
    del after
    slabs = gathered.shape[0]
    planes = back.shape[0] // ROWS
    lane = iota((PACKED, BZ), 1)
    back[...] = back_in[...]
    values = forward_levels([gathered[g] for g in range(slabs)])
    total = jnp.zeros((PACKED, BZ), F32)
    for p in range(slabs):
        low = gathered[p, :, CORNER : CORNER + 1]
        high = gathered[p, :, HALF + CORNER : HALF + CORNER + 1]
        sign = sign_of(jnp.int32(p), place[0], slabs)
        total = total + values[p] * jnp.where(lane < HALF, low, high) * sign
    total = jnp.concatenate([total, pltpu.roll(total, HALF, 1)], axis=0)
    total = jnp.where(iota((planes, BZ), 1) < CORNER, total, 0.0)
    back[pl.ds(EXTRA, planes, stride=ROWS), :] = left_product(level_tables(planes)[1], total)


def details_kernel(recv, vort_hbm, velocity_hbm, after, detail, velocity, vort, sems):
    del after
    parts, cells, wide = vort.shape
    planes = cells // BY
    copies = [
        pltpu.make_async_copy(vort_hbm.at[c], vort.at[c], sems.at[c]) for c in range(parts)
    ]
    copies.append(pltpu.make_async_copy(velocity_hbm, velocity, sems.at[parts]))
    for copy in copies:
        copy.start()
    tall = jnp.where(
        (iota((cells, planes), 0) // BY == iota((cells, planes), 1))
        & (iota((cells, planes), 1) > 0),
        1.0,
        0.0,
    ).astype(BF16)
    kept = recv[pl.ds(EXTRA, planes, stride=ROWS), :].astype(BF16)
    kept = jnp.dot(tall, kept, preferred_element_type=F32).astype(BF16)
    mask = jnp.dot(kept, pick_table(OWN_KEPT, wide), preferred_element_type=F32)
    row, column = iota((cells, cells), 0), iota((cells, cells), 1)
    same = jnp.where(row % BY == column % BY, 1.0, 0.0)
    forward = (weight_of(row // BY, column // BY, planes) * (same - 1.0 / BY)).astype(BF16)
    inverse = (sign_of(column // BY, row // BY, planes) * same).astype(BF16)
    mix, unmix = mix_table(wide), unmix_table(wide)
    for c in range(parts):
        copies[c].wait()
        rows = jnp.dot(forward, vort[c], preferred_element_type=F32)
        rows = remix(rows, mix) * mask
        detail[c] = remix(left_product(inverse, rows), unmix)
    copies[parts].wait()


def finish_kernel(place, got, gathered, detail, velocity, *refs):
    pairs, (out, rows) = refs[:-2], refs[-2:]
    planes = got.shape[0] // ROWS
    parts, cells, wide = velocity.shape
    wanted = [gathered[0, 0:1, :]]
    for level in range(len(pairs) // 2):
        half = 1 << level
        slab = place[0] // (2 * half) * (2 * half) + half
        wanted.append(gathered[slab, 0:1, :])
    wanted += [jnp.zeros((1, BZ), F32)] * (8 - len(wanted))
    wanted = jnp.concatenate(wanted, axis=0).astype(BF16)
    mask = jnp.dot(wanted, pick_table(LINE_KEPT, wide), preferred_element_type=F32)
    inverse = level_tables(planes)[1]
    extra = got[pl.ds(EXTRA, planes, stride=ROWS), :]
    target, cell = iota((planes, wide), 0), iota((planes, wide), 1)
    for c in range(parts):
        for zb in range(ZB):
            span = slice((c * ZB + zb) * BY, (c * ZB + zb + 1) * BY)
            lanes = slice(zb * BZ, (zb + 1) * BZ)
            total = (pairs[-2][span, :] + pairs[-1][span, :]) * 0.5 * mask[0:1, lanes]
            for level in range(len(pairs) // 2):
                mine, other = pairs[2 * level][span, :], pairs[2 * level + 1][span, :]
                total = total + (mine - other) * 0.5 * mask[level + 1 : level + 2, lanes]
            rows[parts * planes + c * BY : parts * planes + (c + 1) * BY, lanes] = total
        corner = right_product(extra, gather_table(c, wide))
        corner = jnp.sum(jnp.where(cell // SLICE == target, corner, 0.0), axis=0, keepdims=True)
        data = jnp.concatenate(
            [got[pl.ds(c * ZB + zb, planes, stride=ROWS), :] for zb in range(ZB)], axis=1
        )
        data = jnp.where(target == 0, corner, data)
        rows[c * planes : (c + 1) * planes, :] = left_product(inverse, data)
    rows[...] = remix(rows[...], unmix_table(wide))
    for x in range(planes):
        span = slice(x * BY, (x + 1) * BY)
        smooth = [
            detail[c, span, :]
            + rows[c * planes + x : c * planes + x + 1, :]
            + rows[parts * planes + c * BY : parts * planes + (c + 1) * BY, :]
            for c in range(parts)
        ]
        speed = [velocity[c, span, :].astype(F32) for c in range(parts)]
        for c in range(parts):
            a, b = (c + 1) % parts, (c + 2) % parts
            out[c, span, :] = (smooth[a] * speed[b] - smooth[b] * speed[a]).astype(BF16)


def exchange(value, axis):
    return lax.all_to_all(value, axis, split_axis=0, concat_axis=0, tiled=True)


def over_yz(rows, planes):
    moved = exchange(rows.reshape(planes, ROWS, 1, BZ), "yz")
    return moved.reshape(planes * ROWS, BZ)


def from_partner(value, distance):
    pairs = [(source, source ^ distance) for source in range(lax.axis_size("gx"))]
    return lax.ppermute(value, "gx", pairs)


def body(vorticity, velocity, blocks, counts):
    parts, planes, tall, wide = vorticity.shape
    cells = planes * tall
    slabs = lax.axis_size("gx")
    smem = pl.BlockSpec(memory_space=pltpu.SMEM)
    vmem = pl.BlockSpec(memory_space=pltpu.VMEM)
    hbm = pl.BlockSpec(memory_space=pl.ANY)
    params = pltpu.CompilerParams(vmem_limit_bytes=32 * 1024 * 1024)
    large = pltpu.CompilerParams(vmem_limit_bytes=60 * 1024 * 1024)
    place = jnp.stack([lax.axis_index("gx"), lax.axis_index("yz")]).astype(jnp.int32)
    vort = vorticity.reshape(parts, cells, wide)
    speed = velocity.reshape(parts, cells, wide)

    def array(*shape):
        return jax.ShapeDtypeStruct(shape, F32)

    send, line, own = pl.pallas_call(
        head_kernel,
        out_shape=(array(planes * ROWS, BZ), array(CHUNKS * BY, BZ), array(8, BZ)),
        in_specs=[hbm, hbm, hbm],
        out_specs=(vmem, vmem, vmem),
        scratch_shapes=[
            pltpu.SMEM(counts.shape, jnp.int32),
            pltpu.VMEM(blocks.shape, jnp.int32),
            pltpu.VMEM((parts, cells, wide), BF16),
            pltpu.SemaphoreType.DMA((parts + 2,)),
        ],
        compiler_params=large,
        name="head",
    )(counts, blocks, vort)
    pairs = []
    distance = 1
    while distance < slabs:
        other = from_partner(line, distance)
        pairs += [line, other]
        line = (line + other) * 0.5
        distance *= 2
    recv = over_yz(send, planes)
    back, corner = pl.pallas_call(
        plane_kernel,
        out_shape=(array(planes * ROWS, BZ), array(slabs, PACKED, BZ)),
        in_specs=[vmem, vmem, hbm],
        out_specs=(vmem, vmem),
        compiler_params=params,
        name="plane",
    )(own, recv, pairs[min(4, len(pairs) - 2)])
    gathered = exchange(corner, "gx")
    back = pl.pallas_call(
        corner_kernel,
        out_shape=array(planes * ROWS, BZ),
        in_specs=[smem, vmem, vmem, hbm],
        out_specs=vmem,
        compiler_params=params,
        name="corner",
    )(place, gathered, back, pairs[min(6, len(pairs) - 2)])
    got = over_yz(back, planes)
    detail, speed = pl.pallas_call(
        details_kernel,
        out_shape=(array(parts, cells, wide), jax.ShapeDtypeStruct((parts, cells, wide), BF16)),
        in_specs=[vmem, hbm, hbm, hbm],
        out_specs=(vmem, vmem),
        scratch_shapes=[
            pltpu.VMEM((parts, cells, wide), BF16),
            pltpu.SemaphoreType.DMA((parts + 1,)),
        ],
        compiler_params=params,
        cost_estimate=pl.CostEstimate(
            flops=24 * parts * cells * cells * wide,
            bytes_accessed=6 * parts * cells * wide,
            transcendentals=0,
        ),
        name="details",
    )(recv, vort, speed, back)
    out = pl.pallas_call(
        finish_kernel,
        out_shape=jax.ShapeDtypeStruct((parts, cells, wide), BF16),
        in_specs=[smem] + [vmem] * (4 + len(pairs)),
        out_specs=vmem,
        scratch_shapes=[pltpu.VMEM((parts * (planes + tall), wide), F32)],
        compiler_params=params,
        name="finish",
    )(place, got, gathered, detail, speed, *pairs)
    return out.reshape(parts, planes, tall, wide)


def solution(mesh):
    return jax.shard_map(
        body,
        mesh=mesh,
        in_specs=(
            P(None, "gx", "yz", None),
            P(None, "gx", "yz", None),
            P(("gx", "yz"), None),
            P(("gx", "yz")),
        ),
        out_specs=P(None, "gx", "yz", None),
        check_vma=False,
    )
```

```python
import jax
import jax.numpy as jnp
from jax import lax
from jax.experimental import pallas as pl
from jax.experimental.pallas import tpu as pltpu
from jax.sharding import PartitionSpec as P


BY = 8
BZ = 128
ZB = 4
CHUNKS = 12
ROWS = 13
EXTRA = 12
CORNER = 48
SLICE = 16
HALF = 64
OWN_KEPT = 48
ALL_KEPT = 64
LINE_KEPT = 52
PACKED = 16
F32 = jnp.float32
BF16 = jnp.bfloat16


def iota(shape, dimension):
    return lax.broadcasted_iota(jnp.int32, shape, dimension)


def sign_of(place, cell, length):
    span = jnp.where(place == 0, length, 2 * (place & -place))
    sign = jnp.where((cell < place) | (place == 0), 1.0, -1.0)
    return jnp.where((cell ^ place) < span, sign, 0.0)


def weight_of(place, cell, length):
    span = jnp.where(place == 0, length, 2 * (place & -place))
    return sign_of(place, cell, length) / span.astype(F32)


def mix_table(wide):
    coarse = iota((8, BZ), 1)
    parts = []
    for block in range(wide // BZ):
        row = weight_of(jnp.minimum(coarse, ZB - 1), jnp.int32(block), ZB)
        row = jnp.where(coarse < ZB, row - jnp.where(coarse == block, 1.0, 0.0), 0.0) / BZ
        parts.append(jnp.broadcast_to(row[0:1], (BZ, BZ)))
    return jnp.concatenate(parts, axis=0).astype(BF16)


def unmix_table(wide):
    block = iota((8, BZ), 1)
    parts = []
    for coarse in range(wide // BZ):
        row = sign_of(jnp.int32(coarse), jnp.minimum(block, ZB - 1), ZB)
        row = jnp.where(block < ZB, row - jnp.where(block == coarse, 1.0, 0.0), 0.0) / BZ
        parts.append(jnp.broadcast_to(row[0:1], (BZ, BZ)))
    return jnp.concatenate(parts, axis=0).astype(BF16)


def halves(value):
    high = value.astype(BF16)
    low = (value - high.astype(F32)).astype(BF16)
    return high, low


def left_product(table, value):
    high, low = halves(value)
    return jnp.dot(table, high, preferred_element_type=F32) + jnp.dot(
        table, low, preferred_element_type=F32
    )


def right_product(value, table):
    high, low = halves(value)
    return jnp.dot(high, table, preferred_element_type=F32) + jnp.dot(
        low, table, preferred_element_type=F32
    )


def remix(value, table):
    shift = right_product(value, table)
    return jnp.concatenate(
        [value[:, zb * BZ : (zb + 1) * BZ] + shift[:, zb : zb + 1] for zb in range(ZB)], axis=1
    )


def forward_levels(values):
    count = len(values)
    result = [None] * count
    step = 1
    while step < count:
        for place in range(step, count, 2 * step):
            low, high = values[place - step], values[place]
            result[place] = (low - high) * 0.5
            values[place - step] = (low + high) * 0.5
        step *= 2
    result[0] = values[0]
    return result


def inverse_levels(values):
    count = len(values)
    values = list(values)
    step = count // 2
    while step >= 1:
        for place in range(step, count, 2 * step):
            mean, detail = values[place - step], values[place]
            values[place - step] = mean + detail
            values[place] = mean - detail
        step //= 2
    return values


def pick_table(first, wide):
    lane, cell = iota((BZ, wide), 0), iota((BZ, wide), 1)
    return jnp.where(lane == (first + (cell >> 7)) & (BZ - 1), 1.0, 0.0).astype(BF16)


def head_kernel(counts_hbm, blocks_hbm, vort_hbm, send, line, own, counts, blocks, vort, sems):
    parts, cells, wide = vort.shape
    planes = cells // BY
    copies = [
        pltpu.make_async_copy(vort_hbm.at[c], vort.at[c], sems.at[c]) for c in range(parts)
    ]
    copies.append(pltpu.make_async_copy(blocks_hbm, blocks, sems.at[parts]))
    copies.append(pltpu.make_async_copy(counts_hbm, counts, sems.at[parts + 1]))
    for copy in reversed(copies):
        copy.start()
    row, column = iota((planes + BY, cells), 0), iota((planes + BY, cells), 1)
    fine = jnp.where(row - planes == column & (BY - 1), 1.0, 0.0) - 1.0 / BY
    table = jnp.where(
        row < planes,
        weight_of(jnp.minimum(row, planes - 1), column >> 3, planes) * (1.0 / BY),
        fine * (1.0 / planes),
    ).astype(BF16)
    mix = mix_table(wide)
    copies[parts].wait()
    copies[parts + 1].wait()
    nblocks = blocks.shape[1]
    square = (nblocks, nblocks)
    listed = (blocks[...] == iota(square, 0)) & (iota(square, 1) < counts[0])
    kept = lax.dot_general(
        jnp.ones((planes, nblocks), BF16),
        jnp.where(listed, 1.0, 0.0).astype(BF16),
        (((1,), (1,)), ((), ())),
        preferred_element_type=F32,
    )
    kept = jnp.minimum(kept, 1.0)
    own[...] = kept[0:8]
    target, block = iota((planes, nblocks), 0), iota((planes, nblocks), 1)
    block_row, lane = iota(square, 0), iota(square, 1)
    mine = jnp.where(block >> 2 == target, kept, 0.0).astype(BF16)
    slot = jnp.where(lane == OWN_KEPT + (block_row & 3), 1.0, 0.0).astype(BF16)
    extra = jnp.dot(mine, slot, preferred_element_type=F32)
    every = jnp.where(block & 3 == target >> 3, kept, 0.0).astype(BF16)
    slot = jnp.where(lane == ALL_KEPT + (block_row >> 2), 1.0, 0.0).astype(BF16)
    extra = extra + jnp.dot(every, slot, preferred_element_type=F32)
    lane, turn = iota((8, BZ), 1), iota((8, BZ), 0)
    extra = [
        pltpu.roll(extra[zb * 8 : (zb + 1) * 8], 0, 1, stride=SLICE, stride_axis=0)
        for zb in range(ZB)
    ]
    for c in range(parts):
        copies[c].wait()
        rows = remix(jnp.dot(table, vort[c], preferred_element_type=F32), mix)
        for zb in range(ZB):
            chunk = c * ZB + zb
            part = rows[:, zb * BZ : (zb + 1) * BZ]
            send[pl.ds(chunk, planes, stride=ROWS), :] = part[0:planes]
            line[chunk * BY : (chunk + 1) * BY, :] = part[planes : planes + BY]
            turned = jnp.broadcast_to(part[0:1], (8, BZ))
            turned = pltpu.roll(turned, c * SLICE, 1) if c else turned
            extra[zb] = jnp.where(lane >> 4 == (turn + c) & 7, turned, extra[zb])
    send[pl.ds(EXTRA, planes, stride=ROWS), :] = jnp.concatenate(extra, axis=0)


def level_tables(length):
    square = (length, length)
    forward = weight_of(iota(square, 0), iota(square, 1), length).astype(BF16)
    inverse = sign_of(iota(square, 1), iota(square, 0), length).astype(BF16)
    return forward, inverse


def plane_kernel(place, own_hbm, recv, after, back, corner, own, sems):
    del after
    planes = recv.shape[0] // ROWS
    copy = pltpu.make_async_copy(own_hbm, own, sems.at[0])
    copy.start()
    forward, inverse = level_tables(planes)
    extra = recv[pl.ds(EXTRA, planes, stride=ROWS), :]
    extra = pltpu.roll(extra, (BZ - SLICE * (place[1] & 7)) & (BZ - 1), 1)
    lane = iota((PACKED, BZ), 1)
    row = iota((PACKED, BZ), 0)
    heads = extra[0:1]
    low = jnp.sum(jnp.where(lane == ALL_KEPT + row, heads, 0.0), axis=1, keepdims=True)
    high = jnp.sum(jnp.where(lane == ALL_KEPT + PACKED + row, heads, 0.0), axis=1, keepdims=True)
    levels = left_product(forward, jnp.where(iota((planes, BZ), 1) < CORNER, extra, 0.0))
    packed = levels[0:PACKED] + pltpu.roll(levels[PACKED:planes], HALF, 1)
    packed = jnp.where(lane == CORNER, low, packed)
    packed = jnp.where(lane == HALF + CORNER, high, packed)
    shifted = pltpu.roll(jnp.broadcast_to(heads, (PACKED, BZ)), LINE_KEPT - OWN_KEPT, 1)
    packed = jnp.where((lane >= LINE_KEPT) & (lane < LINE_KEPT + ZB), shifted, packed)
    for g in range(corner.shape[0]):
        corner[g] = packed
    pick = jnp.where(iota((BZ, ZB * BZ), 0) & 3 == iota((BZ, ZB * BZ), 1) >> 7, 1.0, 0.0)
    copy.wait()
    spread = jnp.where(iota((planes, BZ), 1) >> 2 == iota((planes, BZ), 0), own[0:1], 0.0)
    mask = jnp.dot(spread.astype(BF16), pick.astype(BF16), preferred_element_type=F32)
    for c in range(3):
        data = jnp.concatenate(
            [recv[pl.ds(c * ZB + zb, planes, stride=ROWS), :] for zb in range(ZB)], axis=1
        )
        data = left_product(inverse, left_product(forward, data) * mask)
        for zb in range(ZB):
            back[pl.ds(c * ZB + zb, planes, stride=ROWS), :] = data[:, zb * BZ : (zb + 1) * BZ]


def levels_kernel(vort_hbm, mine, other, after, rows, means, vort, sems):
    del after
    parts, cells, wide = vort.shape
    planes = cells // BY
    copies = [
        pltpu.make_async_copy(vort_hbm.at[c], vort.at[c], sems.at[c]) for c in range(parts)
    ]
    for copy in copies:
        copy.start()
    means[...] = (mine[...] + other[...]) * 0.5
    row, column = iota((cells, cells), 0), iota((cells, cells), 1)
    same = jnp.where(row & (BY - 1) == column & (BY - 1), 1.0 - 1.0 / BY, -1.0 / BY)
    forward = (sign_of(row >> 3, column >> 3, planes) * same).astype(BF16)
    mix = mix_table(wide)
    for c in range(parts):
        copies[c].wait()
        rows[c] = remix(jnp.dot(forward, vort[c], preferred_element_type=F32), mix)


def corner_kernel(place, gathered, back_in, after, back):
    del after
    slabs = gathered.shape[0]
    planes = back.shape[0] // ROWS
    lane = iota((PACKED, BZ), 1)
    back[...] = back_in[...]
    values = forward_levels([gathered[g] for g in range(slabs)])
    total = jnp.zeros((PACKED, BZ), F32)
    for p in range(slabs):
        low = gathered[p, :, CORNER : CORNER + 1]
        high = gathered[p, :, HALF + CORNER : HALF + CORNER + 1]
        sign = sign_of(jnp.int32(p), place[0], slabs)
        total = total + values[p] * jnp.where(lane < HALF, low, high) * sign
    total = jnp.concatenate([total, pltpu.roll(total, HALF, 1)], axis=0)
    total = jnp.where(iota((planes, BZ), 1) < CORNER, total, 0.0)
    total = pltpu.roll(left_product(level_tables(planes)[1], total), SLICE * (place[1] & 7), 1)
    back[pl.ds(EXTRA, planes, stride=ROWS), :] = total


def line_kernel(place, gathered, after, *refs):
    del after
    pairs, (total, means, mask) = refs[:-3], refs[-3:]
    levels = len(pairs) // 2
    wanted = [gathered[0, 0:1, :]]
    for level in range(levels + 1):
        half = 1 << level
        slab = ((place[0] >> (level + 1)) << (level + 1)) + half
        wanted.append(gathered[jnp.minimum(slab, gathered.shape[0] - 1), 0:1, :])
    wanted += [jnp.zeros((1, BZ), F32)] * (8 - len(wanted))
    wanted = jnp.concatenate(wanted, axis=0).astype(BF16)
    mask[...] = jnp.dot(wanted, pick_table(LINE_KEPT, mask.shape[1]), preferred_element_type=F32)
    means[...] = (pairs[-2][...] + pairs[-1][...]) * 0.5
    for chunk in range(CHUNKS):
        span = slice(chunk * BY, (chunk + 1) * BY)
        lanes = slice(chunk % ZB * BZ, (chunk % ZB + 1) * BZ)
        result = jnp.zeros((BY, BZ), F32)
        for level in range(levels):
            mine, other = pairs[2 * level][span, :], pairs[2 * level + 1][span, :]
            result = result + (mine - other) * 0.5 * mask[level + 1 : level + 2, lanes]
        total[span, :] = result


def details_kernel(place, recv, rows, velocity_hbm, after, detail, velocity, sems):
    del after
    parts, cells, wide = rows.shape
    planes = cells // BY
    copy = pltpu.make_async_copy(velocity_hbm, velocity, sems.at[0])
    copy.start()
    row, column = iota((cells, planes), 0), iota((cells, planes), 1)
    span = jnp.maximum(2 * (column & -column), 1).astype(F32)
    tall = jnp.where((row >> 3 == column) & (column > 0), 1.0 / span, 0.0).astype(BF16)
    kept = recv[pl.ds(EXTRA, planes, stride=ROWS), :].astype(BF16)
    kept = jnp.dot(tall, kept, preferred_element_type=F32).astype(BF16)
    mask = jnp.dot(kept, pick_table(OWN_KEPT + SLICE * (place[1] & 7), wide), preferred_element_type=F32)
    row, column = iota((cells, cells), 0), iota((cells, cells), 1)
    same = row & (BY - 1) == column & (BY - 1)
    inverse = jnp.where(same, sign_of(column >> 3, row >> 3, planes), 0.0).astype(BF16)
    unmix = unmix_table(wide)
    for c in range(parts):
        detail[c] = remix(left_product(inverse, rows[c] * mask), unmix)
    copy.wait()


def finish_kernel(got, mine, other, partial, mask, detail, velocity, out, rows):
    planes = got.shape[0] // ROWS
    parts, cells, wide = velocity.shape
    inverse = level_tables(planes)[1]
    extra = got[pl.ds(EXTRA, planes, stride=ROWS), :]
    slot, lane = iota((8, BZ), 0), iota((8, BZ), 1)
    for c in range(parts):
        columns = []
        for zb in range(ZB):
            span = slice((c * ZB + zb) * BY, (c * ZB + zb + 1) * BY)
            lanes = slice(zb * BZ, (zb + 1) * BZ)
            last = (mine[span, :] - other[span, :]) * 0.5
            mean = (mine[span, :] + other[span, :]) * 0.5
            total = partial[span, :] + last * mask[4:5, lanes] + mean * mask[0:1, lanes]
            rows[parts * planes + c * BY : parts * planes + (c + 1) * BY, lanes] = total
            corner = extra[zb * 8 : (zb + 1) * 8]
            corner = jnp.where(lane >> 4 == (slot + c) & 7, corner, 0.0)
            corner = jnp.sum(corner, axis=0, keepdims=True)
            corner = pltpu.roll(corner, BZ - c * SLICE, 1) if c else corner
            data = got[pl.ds(c * ZB + zb, planes, stride=ROWS), :]
            columns.append(jnp.where(iota((planes, BZ), 0) == 0, corner, data))
        rows[c * planes : (c + 1) * planes, :] = left_product(
            inverse, jnp.concatenate(columns, axis=1)
        )
    rows[...] = remix(rows[...], unmix_table(wide))
    for x in range(planes):
        span = slice(x * BY, (x + 1) * BY)
        smooth = [
            detail[c, span, :]
            + rows[c * planes + x : c * planes + x + 1, :]
            + rows[parts * planes + c * BY : parts * planes + (c + 1) * BY, :]
            for c in range(parts)
        ]
        speed = [velocity[c, span, :].astype(F32) for c in range(parts)]
        for c in range(parts):
            a, b = (c + 1) % parts, (c + 2) % parts
            out[c, span, :] = (smooth[a] * speed[b] - smooth[b] * speed[a]).astype(BF16)


def exchange(value, axis):
    return lax.all_to_all(value, axis, split_axis=0, concat_axis=0, tiled=True)


def over_yz(rows, planes):
    moved = exchange(rows.reshape(planes, ROWS, 1, BZ), "yz")
    return moved.reshape(planes * ROWS, BZ)


def from_partner(value, distance):
    if distance >= lax.axis_size("gx"):
        return value
    pairs = [(source, source ^ distance) for source in range(lax.axis_size("gx"))]
    return lax.ppermute(value, "gx", pairs)


def body(vorticity, velocity, blocks, counts):
    parts, planes, tall, wide = vorticity.shape
    cells = planes * tall
    slabs = lax.axis_size("gx")
    smem = pl.BlockSpec(memory_space=pltpu.SMEM)
    vmem = pl.BlockSpec(memory_space=pltpu.VMEM)
    loose = pl.BlockSpec(memory_space=pl.ANY)
    params = pltpu.CompilerParams(vmem_limit_bytes=32 * 1024 * 1024)
    place = jnp.stack([lax.axis_index("gx"), lax.axis_index("yz")]).astype(jnp.int32)
    vort = vorticity.reshape(parts, cells, wide)
    line_shape = (CHUNKS * BY, BZ)

    def array(*shape):
        return jax.ShapeDtypeStruct(shape, F32)

    def call(kernel, name, out_shape, in_specs, scratch=(), cost=None, params=params):
        many = isinstance(out_shape, tuple)
        return pl.pallas_call(
            kernel,
            out_shape=out_shape,
            in_specs=in_specs,
            out_specs=tuple(vmem for _ in out_shape) if many else vmem,
            scratch_shapes=list(scratch),
            compiler_params=params,
            cost_estimate=cost,
            name=name,
        )

    def cost(products):
        return pl.CostEstimate(
            flops=products * 2 * parts * cells * cells * wide,
            bytes_accessed=10 * parts * cells * wide,
            transcendentals=0,
        )

    vort_scratch = pltpu.VMEM((parts, cells, wide), BF16)
    send, line, own = call(
        head_kernel,
        "head",
        (array(planes * ROWS, BZ), array(*line_shape), array(8, BZ)),
        [loose] * 3,
        [
            pltpu.SMEM(counts.shape, jnp.int32),
            pltpu.VMEM(blocks.shape, jnp.int32),
            vort_scratch,
            pltpu.SemaphoreType.DMA((parts + 2,)),
        ],
        params=pltpu.CompilerParams(vmem_limit_bytes=60 * 1024 * 1024),
    )(counts, blocks, vort)
    recv = over_yz(send, planes)
    pairs = [line, from_partner(line, 1)]
    line = (pairs[0] + pairs[1]) * 0.5
    pairs += [line, from_partner(line, 2)]
    back, corner = call(
        plane_kernel,
        "plane",
        (array(planes * ROWS, BZ), array(slabs, PACKED, BZ)),
        [smem, loose, vmem, loose],
        [pltpu.VMEM((8, BZ), F32), pltpu.SemaphoreType.DMA((1,))],
    )(place, own, recv, pairs[3])
    gathered = exchange(corner, "gx")
    rows, line = call(
        levels_kernel,
        "levels",
        (array(parts, cells, wide), array(*line_shape)),
        [loose, vmem, vmem, loose],
        [vort_scratch, pltpu.SemaphoreType.DMA((parts,))],
        cost(3),
    )(vort, pairs[2], pairs[3], corner)
    pairs += [line, from_partner(line, 4)]
    back = call(
        corner_kernel, "corner", array(planes * ROWS, BZ), [smem, vmem, vmem, loose]
    )(place, gathered, back, line)
    got = over_yz(back, planes)
    partial, line, mask = call(
        line_kernel,
        "line",
        (array(*line_shape), array(*line_shape), array(8, wide)),
        [smem, vmem, loose] + [vmem] * 6,
    )(place, gathered, back, *pairs)
    other = from_partner(line, 8)
    detail, speed = call(
        details_kernel,
        "details",
        (array(parts, cells, wide), jax.ShapeDtypeStruct((parts, cells, wide), BF16)),
        [smem, vmem, vmem, loose, loose],
        [pltpu.SemaphoreType.DMA((1,))],
        cost(4),
    )(place, recv, rows, velocity.reshape(parts, cells, wide), line)
    out = call(
        finish_kernel,
        "finish",
        jax.ShapeDtypeStruct((parts, cells, wide), BF16),
        [vmem] * 7,
        [pltpu.VMEM((parts * (planes + tall), wide), F32)],
    )(got, line, other, partial, mask, detail, speed)
    return out.reshape(parts, planes, tall, wide)


def solution(mesh):
    return jax.shard_map(
        body,
        mesh=mesh,
        in_specs=(
            P(None, "gx", "yz", None),
            P(None, "gx", "yz", None),
            P(("gx", "yz"), None),
            P(("gx", "yz")),
        ),
        out_specs=P(None, "gx", "yz", None),
        check_vma=False,
    )
```

```python
import jax
import jax.numpy as jnp
from jax import lax
from jax.experimental import pallas as pl
from jax.experimental.pallas import tpu as pltpu
from jax.sharding import PartitionSpec as P


BY = 8
BZ = 128
ZB = 4
CHUNKS = 12
ROWS = 14
EXTRA = 12
KEPT = 13
CORNER = 48
SLICE = 16
HALF = 64
LINE_KEPT = 52
PACKED = 16
F32 = jnp.float32
BF16 = jnp.bfloat16


def iota(shape, dimension):
    return lax.broadcasted_iota(jnp.int32, shape, dimension)


def sign_of(place, cell, length):
    span = jnp.where(place == 0, length, 2 * (place & -place))
    sign = jnp.where((cell < place) | (place == 0), 1.0, -1.0)
    return jnp.where((cell ^ place) < span, sign, 0.0)


def weight_of(place, cell, length):
    span = jnp.where(place == 0, length, 2 * (place & -place))
    return sign_of(place, cell, length) / span.astype(F32)


def mix_table(wide):
    coarse = iota((8, BZ), 1)
    parts = []
    for block in range(wide // BZ):
        row = weight_of(jnp.minimum(coarse, ZB - 1), jnp.int32(block), ZB)
        row = jnp.where(coarse < ZB, row - jnp.where(coarse == block, 1.0, 0.0), 0.0) / BZ
        parts.append(jnp.broadcast_to(row[0:1], (BZ, BZ)))
    return jnp.concatenate(parts, axis=0).astype(BF16)


def unmix_table(wide):
    block = iota((8, BZ), 1)
    parts = []
    for coarse in range(wide // BZ):
        row = sign_of(jnp.int32(coarse), jnp.minimum(block, ZB - 1), ZB)
        row = jnp.where(block < ZB, row - jnp.where(block == coarse, 1.0, 0.0), 0.0) / BZ
        parts.append(jnp.broadcast_to(row[0:1], (BZ, BZ)))
    return jnp.concatenate(parts, axis=0).astype(BF16)


def halves(value):
    high = value.astype(BF16)
    low = (value - high.astype(F32)).astype(BF16)
    return high, low


def left_product(table, value):
    high, low = halves(value)
    return jnp.dot(table, high, preferred_element_type=F32) + jnp.dot(
        table, low, preferred_element_type=F32
    )


def right_product(value, table):
    high, low = halves(value)
    return jnp.dot(high, table, preferred_element_type=F32) + jnp.dot(
        low, table, preferred_element_type=F32
    )


def remix(value, table):
    shift = right_product(value, table)
    return jnp.concatenate(
        [value[:, zb * BZ : (zb + 1) * BZ] + shift[:, zb : zb + 1] for zb in range(ZB)], axis=1
    )


def forward_levels(values):
    count = len(values)
    result = [None] * count
    step = 1
    while step < count:
        for place in range(step, count, 2 * step):
            low, high = values[place - step], values[place]
            result[place] = (low - high) * 0.5
            values[place - step] = (low + high) * 0.5
        step *= 2
    result[0] = values[0]
    return result


def inverse_levels(values):
    count = len(values)
    values = list(values)
    step = count // 2
    while step >= 1:
        for place in range(step, count, 2 * step):
            mean, detail = values[place - step], values[place]
            values[place - step] = mean + detail
            values[place] = mean - detail
        step //= 2
    return values


def pick_table(first, wide):
    lane, cell = iota((BZ, wide), 0), iota((BZ, wide), 1)
    return jnp.where(lane == (first + (cell >> 7)) & (BZ - 1), 1.0, 0.0).astype(BF16)


def head_kernel(counts_hbm, blocks_hbm, vort_hbm, send, line, counts, blocks, vort, sems):
    parts, cells, wide = vort.shape
    planes = cells // BY
    copies = [
        pltpu.make_async_copy(vort_hbm.at[c], vort.at[c], sems.at[c]) for c in range(parts)
    ]
    copies.append(pltpu.make_async_copy(blocks_hbm, blocks, sems.at[parts]))
    copies.append(pltpu.make_async_copy(counts_hbm, counts, sems.at[parts + 1]))
    for copy in reversed(copies):
        copy.start()
    row, column = iota((planes + BY, cells), 0), iota((planes + BY, cells), 1)
    fine = jnp.where(row - planes == column & (BY - 1), 1.0, 0.0) - 1.0 / BY
    table = jnp.where(
        row < planes,
        weight_of(jnp.minimum(row, planes - 1), column >> 3, planes) * (1.0 / BY),
        fine * (1.0 / planes),
    ).astype(BF16)
    mix = mix_table(wide)
    copies[parts].wait()
    copies[parts + 1].wait()
    nblocks = blocks.shape[1]
    square = (nblocks, nblocks)
    listed = (blocks[...] == iota(square, 0)) & (iota(square, 1) < counts[0])
    kept = lax.dot_general(
        jnp.ones((planes, nblocks), BF16),
        jnp.where(listed, 1.0, 0.0).astype(BF16),
        (((1,), (1,)), ((), ())),
        preferred_element_type=F32,
    )
    send[pl.ds(KEPT, planes, stride=ROWS), :] = jnp.minimum(kept, 1.0)
    lane, turn = iota((8, BZ), 1), iota((8, BZ), 0)
    extra = [jnp.zeros((8, BZ), F32) for zb in range(ZB)]
    for c in range(parts):
        copies[c].wait()
        rows = remix(jnp.dot(table, vort[c], preferred_element_type=F32), mix)
        for zb in range(ZB):
            chunk = c * ZB + zb
            part = rows[:, zb * BZ : (zb + 1) * BZ]
            send[pl.ds(chunk, planes, stride=ROWS), :] = part[0:planes]
            line[chunk * BY : (chunk + 1) * BY, :] = part[planes : planes + BY]
            turned = jnp.broadcast_to(part[0:1], (8, BZ))
            turned = pltpu.roll(turned, c * SLICE, 1) if c else turned
            extra[zb] = jnp.where(lane >> 4 == (turn + c) & 7, turned, extra[zb])
    send[pl.ds(EXTRA, planes, stride=ROWS), :] = jnp.concatenate(extra, axis=0)


def level_tables(length):
    square = (length, length)
    forward = weight_of(iota(square, 0), iota(square, 1), length).astype(BF16)
    inverse = sign_of(iota(square, 1), iota(square, 0), length).astype(BF16)
    return forward, inverse


def plane_kernel(place, recv, after, back, corner):
    del after
    planes = recv.shape[0] // ROWS
    forward, inverse = level_tables(planes)
    extra = recv[pl.ds(EXTRA, planes, stride=ROWS), :]
    extra = pltpu.roll(extra, (BZ - SLICE * (place[1] & 7)) & (BZ - 1), 1)
    lane = iota((PACKED, BZ), 1)
    row = iota((PACKED, BZ), 0)
    heads = recv[KEPT : KEPT + 1, :]
    first = 4 * row + (place[1] >> 3)
    low = jnp.sum(jnp.where(lane == first, heads, 0.0), axis=1, keepdims=True)
    high = jnp.sum(jnp.where(lane == first + HALF, heads, 0.0), axis=1, keepdims=True)
    levels = left_product(forward, jnp.where(iota((planes, BZ), 1) < CORNER, extra, 0.0))
    packed = levels[0:PACKED] + pltpu.roll(levels[PACKED:planes], HALF, 1)
    packed = jnp.where(lane == CORNER, low, packed)
    packed = jnp.where(lane == HALF + CORNER, high, packed)
    shifted = pltpu.roll(jnp.broadcast_to(heads, (PACKED, BZ)), (LINE_KEPT - ZB * place[1]) & (BZ - 1), 1)
    packed = jnp.where((lane >= LINE_KEPT) & (lane < LINE_KEPT + ZB), shifted, packed)
    for g in range(corner.shape[0]):
        corner[g] = packed
    pick = jnp.where(iota((BZ, ZB * BZ), 0) & 3 == iota((BZ, ZB * BZ), 1) >> 7, 1.0, 0.0)
    own = recv[pl.ds(place[1] * ROWS + KEPT, 1), :]
    spread = jnp.where(iota((planes, BZ), 1) >> 2 == iota((planes, BZ), 0), own, 0.0)
    mask = jnp.dot(spread.astype(BF16), pick.astype(BF16), preferred_element_type=F32)
    for c in range(3):
        data = jnp.concatenate(
            [recv[pl.ds(c * ZB + zb, planes, stride=ROWS), :] for zb in range(ZB)], axis=1
        )
        data = left_product(inverse, left_product(forward, data) * mask)
        for zb in range(ZB):
            back[pl.ds(c * ZB + zb, planes, stride=ROWS), :] = data[:, zb * BZ : (zb + 1) * BZ]


def details_kernel(place, recv, vort_hbm, velocity_hbm, after, detail, velocity, vort, sems):
    del after
    parts, cells, wide = vort.shape
    planes = cells // BY
    copies = [
        pltpu.make_async_copy(vort_hbm.at[c], vort.at[c], sems.at[c]) for c in range(parts)
    ]
    copies.append(pltpu.make_async_copy(velocity_hbm, velocity, sems.at[parts]))
    for copy in copies:
        copy.start()
    row, column = iota((cells, planes), 0), iota((cells, planes), 1)
    span = jnp.maximum(2 * (column & -column), 1).astype(F32)
    tall = jnp.where((row >> 3 == column) & (column > 0), 1.0 / span, 0.0).astype(BF16)
    kept = recv[pl.ds(KEPT, planes, stride=ROWS), :].astype(BF16)
    kept = jnp.dot(tall, kept, preferred_element_type=F32).astype(BF16)
    mask = jnp.dot(kept, pick_table(ZB * place[1], wide), preferred_element_type=F32)
    row, column = iota((cells, cells), 0), iota((cells, cells), 1)
    same = row & (BY - 1) == column & (BY - 1)
    sign = sign_of(row >> 3, column >> 3, planes)
    forward = (sign * jnp.where(same, 1.0 - 1.0 / BY, -1.0 / BY)).astype(BF16)
    sign = sign_of(column >> 3, row >> 3, planes)
    inverse = jnp.where(same, sign, 0.0).astype(BF16)
    mix, unmix = mix_table(wide), unmix_table(wide)
    for c in range(parts):
        copies[c].wait()
        rows = remix(jnp.dot(forward, vort[c], preferred_element_type=F32), mix)
        detail[c] = remix(left_product(inverse, rows * mask), unmix)
    copies[parts].wait()


def corner_kernel(place, gathered, back_in, mine, other, back, means):
    means[...] = (mine[...] + other[...]) * 0.5
    slabs = gathered.shape[0]
    planes = back.shape[0] // ROWS
    lane = iota((PACKED, BZ), 1)
    back[...] = back_in[...]
    values = forward_levels([gathered[g] for g in range(slabs)])
    total = jnp.zeros((PACKED, BZ), F32)
    for p in range(slabs):
        low = gathered[p, :, CORNER : CORNER + 1]
        high = gathered[p, :, HALF + CORNER : HALF + CORNER + 1]
        sign = sign_of(jnp.int32(p), place[0], slabs)
        total = total + values[p] * jnp.where(lane < HALF, low, high) * sign
    total = jnp.concatenate([total, pltpu.roll(total, HALF, 1)], axis=0)
    total = jnp.where(iota((planes, BZ), 1) < CORNER, total, 0.0)
    total = pltpu.roll(left_product(level_tables(planes)[1], total), SLICE * (place[1] & 7), 1)
    back[pl.ds(EXTRA, planes, stride=ROWS), :] = total


def line_kernel(place, gathered, after, mine, one, two, three, half, other, total, mask):
    del after
    wanted = [gathered[0, 0:1, :]]
    for level in range(4):
        slab = ((place[0] >> (level + 1)) << (level + 1)) + (1 << level)
        wanted.append(gathered[jnp.minimum(slab, gathered.shape[0] - 1), 0:1, :])
    wanted += [jnp.zeros((1, BZ), F32)] * (8 - len(wanted))
    wanted = jnp.concatenate(wanted, axis=0).astype(BF16)
    mask[...] = jnp.dot(wanted, pick_table(LINE_KEPT, mask.shape[1]), preferred_element_type=F32)
    for chunk in range(CHUNKS):
        span = slice(chunk * BY, (chunk + 1) * BY)
        lanes = slice(chunk % ZB * BZ, (chunk % ZB + 1) * BZ)
        near, far = mine[span, :] + one[span, :], two[span, :] + three[span, :]
        result = (mine[span, :] - one[span, :]) * 0.5 * mask[1:2, lanes]
        result = result + (near - far) * 0.25 * mask[2:3, lanes]
        result = result + (half[span, :] - other[span, :]) * 0.5 * mask[3:4, lanes]
        total[span, :] = result


def finish_kernel(got, mine, other, partial, mask, detail, velocity, out, rows):
    planes = got.shape[0] // ROWS
    parts, cells, wide = velocity.shape
    inverse = level_tables(planes)[1]
    extra = got[pl.ds(EXTRA, planes, stride=ROWS), :]
    slot, lane = iota((8, BZ), 0), iota((8, BZ), 1)
    for c in range(parts):
        columns = []
        for zb in range(ZB):
            span = slice((c * ZB + zb) * BY, (c * ZB + zb + 1) * BY)
            lanes = slice(zb * BZ, (zb + 1) * BZ)
            last = (mine[span, :] - other[span, :]) * 0.5
            mean = (mine[span, :] + other[span, :]) * 0.5
            total = partial[span, :] + last * mask[4:5, lanes] + mean * mask[0:1, lanes]
            rows[parts * planes + c * BY : parts * planes + (c + 1) * BY, lanes] = total
            corner = extra[zb * 8 : (zb + 1) * 8]
            corner = jnp.where(lane >> 4 == (slot + c) & 7, corner, 0.0)
            corner = jnp.sum(corner, axis=0, keepdims=True)
            corner = pltpu.roll(corner, BZ - c * SLICE, 1) if c else corner
            data = got[pl.ds(c * ZB + zb, planes, stride=ROWS), :]
            columns.append(jnp.where(iota((planes, BZ), 0) == 0, corner, data))
        rows[c * planes : (c + 1) * planes, :] = left_product(
            inverse, jnp.concatenate(columns, axis=1)
        )
    rows[...] = remix(rows[...], unmix_table(wide))
    for x in range(planes):
        span = slice(x * BY, (x + 1) * BY)
        smooth = [
            detail[c, span, :]
            + rows[c * planes + x : c * planes + x + 1, :]
            + rows[parts * planes + c * BY : parts * planes + (c + 1) * BY, :]
            for c in range(parts)
        ]
        speed = [velocity[c, span, :].astype(F32) for c in range(parts)]
        for c in range(parts):
            a, b = (c + 1) % parts, (c + 2) % parts
            out[c, span, :] = (smooth[a] * speed[b] - smooth[b] * speed[a]).astype(BF16)


def exchange(value, axis):
    return lax.all_to_all(value, axis, split_axis=0, concat_axis=0, tiled=True)


def over_yz(rows, planes):
    moved = exchange(rows.reshape(planes, ROWS, 1, BZ), "yz")
    return moved.reshape(planes * ROWS, BZ)


def from_partner(value, distance):
    if distance >= lax.axis_size("gx"):
        return value
    pairs = [(source, source ^ distance) for source in range(lax.axis_size("gx"))]
    return lax.ppermute(value, "gx", pairs)


def body(vorticity, velocity, blocks, counts):
    parts, planes, tall, wide = vorticity.shape
    cells = planes * tall
    slabs = lax.axis_size("gx")
    smem = pl.BlockSpec(memory_space=pltpu.SMEM)
    vmem = pl.BlockSpec(memory_space=pltpu.VMEM)
    loose = pl.BlockSpec(memory_space=pl.ANY)
    params = pltpu.CompilerParams(vmem_limit_bytes=32 * 1024 * 1024)
    place = jnp.stack([lax.axis_index("gx"), lax.axis_index("yz")]).astype(jnp.int32)
    vort = vorticity.reshape(parts, cells, wide)
    line_shape = (CHUNKS * BY, BZ)

    def array(*shape):
        return jax.ShapeDtypeStruct(shape, F32)

    def call(kernel, name, out_shape, in_specs, scratch=(), cost=None, params=params):
        many = isinstance(out_shape, tuple)
        return pl.pallas_call(
            kernel,
            out_shape=out_shape,
            in_specs=in_specs,
            out_specs=tuple(vmem for _ in out_shape) if many else vmem,
            scratch_shapes=list(scratch),
            compiler_params=params,
            cost_estimate=cost,
            name=name,
        )

    def cost(products):
        return pl.CostEstimate(
            flops=products * 2 * parts * cells * cells * wide,
            bytes_accessed=10 * parts * cells * wide,
            transcendentals=0,
        )

    vort_scratch = pltpu.VMEM((parts, cells, wide), BF16)
    send, line = call(
        head_kernel,
        "head",
        (array(planes * ROWS, BZ), array(*line_shape)),
        [loose] * 3,
        [
            pltpu.SMEM(counts.shape, jnp.int32),
            pltpu.VMEM(blocks.shape, jnp.int32),
            vort_scratch,
            pltpu.SemaphoreType.DMA((parts + 2,)),
        ],
        params=pltpu.CompilerParams(vmem_limit_bytes=60 * 1024 * 1024),
    )(counts, blocks, vort)
    recv = over_yz(send, planes)
    near = [from_partner(line, distance) for distance in (1, 2, 3)]
    half = (line + near[0] + (near[1] + near[2])) * 0.25
    back, corner = call(
        plane_kernel,
        "plane",
        (array(planes * ROWS, BZ), array(slabs, PACKED, BZ)),
        [smem, vmem, loose],
    )(place, recv, half)
    gathered = exchange(corner, "gx")
    opposite = from_partner(half, 4)
    detail, speed = call(
        details_kernel,
        "details",
        (array(parts, cells, wide), jax.ShapeDtypeStruct((parts, cells, wide), BF16)),
        [smem, vmem, loose, loose, loose],
        [vort_scratch, pltpu.SemaphoreType.DMA((parts + 1,))],
        cost(7),
    )(place, recv, vort, velocity.reshape(parts, cells, wide), corner)
    back, means = call(
        corner_kernel,
        "corner",
        (array(planes * ROWS, BZ), array(*line_shape)),
        [smem] + [vmem] * 4,
    )(place, gathered, back, half, opposite)
    got = over_yz(back, planes)
    other = from_partner(means, 8)
    partial, mask = call(
        line_kernel,
        "line",
        (array(*line_shape), array(8, wide)),
        [smem, vmem, loose] + [vmem] * 6,
    )(place, gathered, means, line, *near, half, opposite)
    out = call(
        finish_kernel,
        "finish",
        jax.ShapeDtypeStruct((parts, cells, wide), BF16),
        [vmem] * 7,
        [pltpu.VMEM((parts * (planes + tall), wide), F32)],
    )(got, means, other, partial, mask, detail, speed)
    return out.reshape(parts, planes, tall, wide)


def solution(mesh):
    return jax.shard_map(
        body,
        mesh=mesh,
        in_specs=(
            P(None, "gx", "yz", None),
            P(None, "gx", "yz", None),
            P(("gx", "yz"), None),
            P(("gx", "yz")),
        ),
        out_specs=P(None, "gx", "yz", None),
        check_vma=False,
    )
```

```python
import jax
import jax.numpy as jnp
from jax import lax
from jax.experimental import pallas as pl
from jax.experimental.pallas import tpu as pltpu
from jax.sharding import PartitionSpec as P


BY = 8
BZ = 128
ZB = 4
CHUNKS = 12
ROWS = 14
EXTRA = 12
KEPT = 13
CORNER = 48
SLICE = 16
HALF = 64
LINE_KEPT = 52
PACKED = 16
F32 = jnp.float32
BF16 = jnp.bfloat16


def iota(shape, dimension):
    return lax.broadcasted_iota(jnp.int32, shape, dimension)


def sign_of(place, cell, length):
    span = jnp.where(place == 0, length, 2 * (place & -place))
    sign = jnp.where((cell < place) | (place == 0), 1.0, -1.0)
    return jnp.where((cell ^ place) < span, sign, 0.0)


def weight_of(place, cell, length):
    span = jnp.where(place == 0, length, 2 * (place & -place))
    return sign_of(place, cell, length) / span.astype(F32)


def mix_table(wide):
    coarse = iota((8, BZ), 1)
    parts = []
    for block in range(wide // BZ):
        row = weight_of(jnp.minimum(coarse, ZB - 1), jnp.int32(block), ZB)
        row = jnp.where(coarse < ZB, row - jnp.where(coarse == block, 1.0, 0.0), 0.0) / BZ
        parts.append(jnp.broadcast_to(row[0:1], (BZ, BZ)))
    return jnp.concatenate(parts, axis=0).astype(BF16)


def unmix_table(wide):
    block = iota((8, BZ), 1)
    parts = []
    for coarse in range(wide // BZ):
        row = sign_of(jnp.int32(coarse), jnp.minimum(block, ZB - 1), ZB)
        row = jnp.where(block < ZB, row - jnp.where(block == coarse, 1.0, 0.0), 0.0) / BZ
        parts.append(jnp.broadcast_to(row[0:1], (BZ, BZ)))
    return jnp.concatenate(parts, axis=0).astype(BF16)


def halves(value):
    high = value.astype(BF16)
    low = (value - high.astype(F32)).astype(BF16)
    return high, low


def left_product(table, value):
    high, low = halves(value)
    return jnp.dot(table, high, preferred_element_type=F32) + jnp.dot(
        table, low, preferred_element_type=F32
    )


def right_product(value, table):
    high, low = halves(value)
    return jnp.dot(high, table, preferred_element_type=F32) + jnp.dot(
        low, table, preferred_element_type=F32
    )


def remix(value, table):
    shift = right_product(value, table)
    return jnp.concatenate(
        [value[:, zb * BZ : (zb + 1) * BZ] + shift[:, zb : zb + 1] for zb in range(ZB)], axis=1
    )


def forward_levels(values):
    count = len(values)
    result = [None] * count
    step = 1
    while step < count:
        for place in range(step, count, 2 * step):
            low, high = values[place - step], values[place]
            result[place] = (low - high) * 0.5
            values[place - step] = (low + high) * 0.5
        step *= 2
    result[0] = values[0]
    return result


def inverse_levels(values):
    count = len(values)
    values = list(values)
    step = count // 2
    while step >= 1:
        for place in range(step, count, 2 * step):
            mean, detail = values[place - step], values[place]
            values[place - step] = mean + detail
            values[place] = mean - detail
        step //= 2
    return values


def pick_table(first, wide):
    lane, cell = iota((BZ, wide), 0), iota((BZ, wide), 1)
    return jnp.where(lane == (first + (cell >> 7)) & (BZ - 1), 1.0, 0.0).astype(BF16)


def head_kernel(counts_hbm, blocks_hbm, vort_hbm, send, line, counts, blocks, vort, sems):
    parts, cells, wide = vort.shape
    planes = cells // BY
    copies = [
        pltpu.make_async_copy(vort_hbm.at[c], vort.at[c], sems.at[c]) for c in range(parts)
    ]
    copies.append(pltpu.make_async_copy(blocks_hbm, blocks, sems.at[parts]))
    copies.append(pltpu.make_async_copy(counts_hbm, counts, sems.at[parts + 1]))
    for copy in reversed(copies):
        copy.start()
    row, column = iota((planes + BY, cells), 0), iota((planes + BY, cells), 1)
    fine = jnp.where(row - planes == column & (BY - 1), 1.0, 0.0) - 1.0 / BY
    table = jnp.where(
        row < planes,
        weight_of(jnp.minimum(row, planes - 1), column >> 3, planes) * (1.0 / BY),
        fine * (1.0 / planes),
    ).astype(BF16)
    mix = mix_table(wide)
    copies[parts].wait()
    copies[parts + 1].wait()
    nblocks = blocks.shape[1]
    square = (nblocks, nblocks)
    listed = (blocks[...] == iota(square, 0)) & (iota(square, 1) < counts[0])
    kept = lax.dot_general(
        jnp.ones((planes, nblocks), BF16),
        jnp.where(listed, 1.0, 0.0).astype(BF16),
        (((1,), (1,)), ((), ())),
        preferred_element_type=F32,
    )
    send[pl.ds(KEPT, planes, stride=ROWS), :] = jnp.minimum(kept, 1.0)
    lane, turn = iota((8, BZ), 1), iota((8, BZ), 0)
    extra = [jnp.zeros((8, BZ), F32) for zb in range(ZB)]
    for c in range(parts):
        copies[c].wait()
        rows = remix(jnp.dot(table, vort[c], preferred_element_type=F32), mix)
        for zb in range(ZB):
            chunk = c * ZB + zb
            part = rows[:, zb * BZ : (zb + 1) * BZ]
            send[pl.ds(chunk, planes, stride=ROWS), :] = part[0:planes]
            line[chunk * BY : (chunk + 1) * BY, :] = part[planes : planes + BY]
            turned = jnp.broadcast_to(part[0:1], (8, BZ))
            turned = pltpu.roll(turned, c * SLICE, 1) if c else turned
            extra[zb] = jnp.where(lane >> 4 == (turn + c) & 7, turned, extra[zb])
    send[pl.ds(EXTRA, planes, stride=ROWS), :] = jnp.concatenate(extra, axis=0)


def level_tables(length):
    square = (length, length)
    forward = weight_of(iota(square, 0), iota(square, 1), length).astype(BF16)
    inverse = sign_of(iota(square, 1), iota(square, 0), length).astype(BF16)
    return forward, inverse


def plane_kernel(place, recv, after, back, corner):
    del after
    planes = recv.shape[0] // ROWS
    forward, inverse = level_tables(planes)
    extra = recv[pl.ds(EXTRA, planes, stride=ROWS), :]
    extra = pltpu.roll(extra, (BZ - SLICE * (place[1] & 7)) & (BZ - 1), 1)
    lane = iota((PACKED, BZ), 1)
    row = iota((PACKED, BZ), 0)
    heads = recv[KEPT : KEPT + 1, :]
    first = 4 * row + (place[1] >> 3)
    low = jnp.sum(jnp.where(lane == first, heads, 0.0), axis=1, keepdims=True)
    high = jnp.sum(jnp.where(lane == first + HALF, heads, 0.0), axis=1, keepdims=True)
    levels = left_product(forward, jnp.where(iota((planes, BZ), 1) < CORNER, extra, 0.0))
    packed = levels[0:PACKED] + pltpu.roll(levels[PACKED:planes], HALF, 1)
    packed = jnp.where(lane == CORNER, low, packed)
    packed = jnp.where(lane == HALF + CORNER, high, packed)
    shifted = pltpu.roll(jnp.broadcast_to(heads, (PACKED, BZ)), (LINE_KEPT - ZB * place[1]) & (BZ - 1), 1)
    packed = jnp.where((lane >= LINE_KEPT) & (lane < LINE_KEPT + ZB), shifted, packed)
    for g in range(corner.shape[0]):
        corner[g] = packed
    pick = jnp.where(iota((BZ, ZB * BZ), 0) & 3 == iota((BZ, ZB * BZ), 1) >> 7, 1.0, 0.0)
    own = recv[pl.ds(place[1] * ROWS + KEPT, 1), :]
    spread = jnp.where(iota((planes, BZ), 1) >> 2 == iota((planes, BZ), 0), own, 0.0)
    mask = jnp.dot(spread.astype(BF16), pick.astype(BF16), preferred_element_type=F32)
    for c in range(3):
        data = jnp.concatenate(
            [recv[pl.ds(c * ZB + zb, planes, stride=ROWS), :] for zb in range(ZB)], axis=1
        )
        data = left_product(inverse, left_product(forward, data) * mask)
        for zb in range(ZB):
            back[pl.ds(c * ZB + zb, planes, stride=ROWS), :] = data[:, zb * BZ : (zb + 1) * BZ]


def details_kernel(place, recv, vort, after, detail):
    del after
    parts, cells, wide = vort.shape
    planes = cells // BY
    row, column = iota((cells, planes), 0), iota((cells, planes), 1)
    span = jnp.maximum(2 * (column & -column), 1).astype(F32)
    tall = jnp.where((row >> 3 == column) & (column > 0), 1.0 / span, 0.0).astype(BF16)
    kept = recv[pl.ds(KEPT, planes, stride=ROWS), :].astype(BF16)
    kept = jnp.dot(tall, kept, preferred_element_type=F32).astype(BF16)
    mask = jnp.dot(kept, pick_table(ZB * place[1], wide), preferred_element_type=F32)
    row, column = iota((cells, cells), 0), iota((cells, cells), 1)
    same = row & (BY - 1) == column & (BY - 1)
    sign = sign_of(row >> 3, column >> 3, planes)
    forward = (sign * jnp.where(same, 1.0 - 1.0 / BY, -1.0 / BY)).astype(BF16)
    sign = sign_of(column >> 3, row >> 3, planes)
    inverse = jnp.where(same, sign, 0.0).astype(BF16)
    mix, unmix = mix_table(wide), unmix_table(wide)
    for c in range(parts):
        rows = remix(jnp.dot(forward, vort[c], preferred_element_type=F32), mix)
        detail[c] = remix(left_product(inverse, rows * mask), unmix)


def corner_kernel(place, gathered, back_in, mine, other, after, back, means):
    del after
    means[...] = (mine[...] + other[...]) * 0.5
    slabs = gathered.shape[0]
    planes = back.shape[0] // ROWS
    lane = iota((PACKED, BZ), 1)
    back[...] = back_in[...]
    values = forward_levels([gathered[g] for g in range(slabs)])
    total = jnp.zeros((PACKED, BZ), F32)
    for p in range(slabs):
        low = gathered[p, :, CORNER : CORNER + 1]
        high = gathered[p, :, HALF + CORNER : HALF + CORNER + 1]
        sign = sign_of(jnp.int32(p), place[0], slabs)
        total = total + values[p] * jnp.where(lane < HALF, low, high) * sign
    total = jnp.concatenate([total, pltpu.roll(total, HALF, 1)], axis=0)
    total = jnp.where(iota((planes, BZ), 1) < CORNER, total, 0.0)
    total = pltpu.roll(left_product(level_tables(planes)[1], total), SLICE * (place[1] & 7), 1)
    back[pl.ds(EXTRA, planes, stride=ROWS), :] = total


def line_kernel(place, gathered, after, mine, one, two, three, half, other, total, mask):
    del after
    wanted = [gathered[0, 0:1, :]]
    for level in range(4):
        slab = ((place[0] >> (level + 1)) << (level + 1)) + (1 << level)
        wanted.append(gathered[jnp.minimum(slab, gathered.shape[0] - 1), 0:1, :])
    wanted += [jnp.zeros((1, BZ), F32)] * (8 - len(wanted))
    wanted = jnp.concatenate(wanted, axis=0).astype(BF16)
    mask[...] = jnp.dot(wanted, pick_table(LINE_KEPT, mask.shape[1]), preferred_element_type=F32)
    for chunk in range(CHUNKS):
        span = slice(chunk * BY, (chunk + 1) * BY)
        lanes = slice(chunk % ZB * BZ, (chunk % ZB + 1) * BZ)
        near, far = mine[span, :] + one[span, :], two[span, :] + three[span, :]
        result = (mine[span, :] - one[span, :]) * 0.5 * mask[1:2, lanes]
        result = result + (near - far) * 0.25 * mask[2:3, lanes]
        result = result + (half[span, :] - other[span, :]) * 0.5 * mask[3:4, lanes]
        total[span, :] = result


def finish_kernel(got, mine, other, partial, mask, detail, velocity, out, rows):
    planes = got.shape[0] // ROWS
    parts, cells, wide = velocity.shape
    inverse = level_tables(planes)[1]
    extra = got[pl.ds(EXTRA, planes, stride=ROWS), :]
    slot, lane = iota((8, BZ), 0), iota((8, BZ), 1)
    for c in range(parts):
        columns = []
        for zb in range(ZB):
            span = slice((c * ZB + zb) * BY, (c * ZB + zb + 1) * BY)
            lanes = slice(zb * BZ, (zb + 1) * BZ)
            last = (mine[span, :] - other[span, :]) * 0.5
            mean = (mine[span, :] + other[span, :]) * 0.5
            total = partial[span, :] + last * mask[4:5, lanes] + mean * mask[0:1, lanes]
            rows[parts * planes + c * BY : parts * planes + (c + 1) * BY, lanes] = total
            corner = extra[zb * 8 : (zb + 1) * 8]
            corner = jnp.where(lane >> 4 == (slot + c) & 7, corner, 0.0)
            corner = jnp.sum(corner, axis=0, keepdims=True)
            corner = pltpu.roll(corner, BZ - c * SLICE, 1) if c else corner
            data = got[pl.ds(c * ZB + zb, planes, stride=ROWS), :]
            columns.append(jnp.where(iota((planes, BZ), 0) == 0, corner, data))
        rows[c * planes : (c + 1) * planes, :] = left_product(
            inverse, jnp.concatenate(columns, axis=1)
        )
    rows[...] = remix(rows[...], unmix_table(wide))
    for x in range(planes):
        span = slice(x * BY, (x + 1) * BY)
        smooth = [
            detail[c, span, :]
            + rows[c * planes + x : c * planes + x + 1, :]
            + rows[parts * planes + c * BY : parts * planes + (c + 1) * BY, :]
            for c in range(parts)
        ]
        speed = [velocity[c, span, :].astype(F32) for c in range(parts)]
        for c in range(parts):
            a, b = (c + 1) % parts, (c + 2) % parts
            out[c, span, :] = (smooth[a] * speed[b] - smooth[b] * speed[a]).astype(BF16)


def exchange(value, axis):
    return lax.all_to_all(value, axis, split_axis=0, concat_axis=0, tiled=True)


def over_yz(rows, planes):
    moved = exchange(rows.reshape(planes, ROWS, 1, BZ), "yz")
    return moved.reshape(planes * ROWS, BZ)


def from_partner(value, distance):
    if distance >= lax.axis_size("gx"):
        return value
    pairs = [(source, source ^ distance) for source in range(lax.axis_size("gx"))]
    return lax.ppermute(value, "gx", pairs)


def body(vorticity, velocity, blocks, counts):
    parts, planes, tall, wide = vorticity.shape
    cells = planes * tall
    slabs = lax.axis_size("gx")
    smem = pl.BlockSpec(memory_space=pltpu.SMEM)
    vmem = pl.BlockSpec(memory_space=pltpu.VMEM)
    loose = pl.BlockSpec(memory_space=pl.ANY)
    params = pltpu.CompilerParams(vmem_limit_bytes=32 * 1024 * 1024)
    place = jnp.stack([lax.axis_index("gx"), lax.axis_index("yz")]).astype(jnp.int32)
    vort = vorticity.reshape(parts, cells, wide)
    line_shape = (CHUNKS * BY, BZ)

    def array(*shape):
        return jax.ShapeDtypeStruct(shape, F32)

    def call(kernel, name, out_shape, in_specs, scratch=(), cost=None, params=params):
        many = isinstance(out_shape, tuple)
        return pl.pallas_call(
            kernel,
            out_shape=out_shape,
            in_specs=in_specs,
            out_specs=tuple(vmem for _ in out_shape) if many else vmem,
            scratch_shapes=list(scratch),
            compiler_params=params,
            cost_estimate=cost,
            name=name,
        )

    def cost(products):
        return pl.CostEstimate(
            flops=products * 2 * parts * cells * cells * wide,
            bytes_accessed=10 * parts * cells * wide,
            transcendentals=0,
        )

    vort_scratch = pltpu.VMEM((parts, cells, wide), BF16)
    send, line = call(
        head_kernel,
        "head",
        (array(planes * ROWS, BZ), array(*line_shape)),
        [loose] * 3,
        [
            pltpu.SMEM(counts.shape, jnp.int32),
            pltpu.VMEM(blocks.shape, jnp.int32),
            vort_scratch,
            pltpu.SemaphoreType.DMA((parts + 2,)),
        ],
        params=pltpu.CompilerParams(vmem_limit_bytes=60 * 1024 * 1024),
    )(counts, blocks, vort)
    recv = over_yz(send, planes)
    near = [from_partner(line, distance) for distance in (1, 2, 3)]
    half = (line + near[0] + (near[1] + near[2])) * 0.25
    back, corner = call(
        plane_kernel,
        "plane",
        (array(planes * ROWS, BZ), array(slabs, PACKED, BZ)),
        [smem, vmem, loose],
    )(place, recv, half)
    gathered = exchange(corner, "gx")
    opposite = from_partner(half, 4)
    detail = call(
        details_kernel,
        "details",
        array(parts, cells, wide),
        [smem, vmem, vmem, loose],
        cost=cost(7),
    )(place, recv, vort, corner)
    back, means = call(
        corner_kernel,
        "corner",
        (array(planes * ROWS, BZ), array(*line_shape)),
        [smem] + [vmem] * 4 + [loose],
    )(place, gathered, back, half, opposite, detail)
    got = over_yz(back, planes)
    other = from_partner(means, 8)
    partial, mask = call(
        line_kernel,
        "line",
        (array(*line_shape), array(8, wide)),
        [smem, vmem, loose] + [vmem] * 6,
    )(place, gathered, means, line, *near, half, opposite)
    out = call(
        finish_kernel,
        "finish",
        jax.ShapeDtypeStruct((parts, cells, wide), BF16),
        [vmem] * 7,
        [pltpu.VMEM((parts * (planes + tall), wide), F32)],
    )(got, means, other, partial, mask, detail, velocity.reshape(parts, cells, wide))
    return out.reshape(parts, planes, tall, wide)


def solution(mesh):
    return jax.shard_map(
        body,
        mesh=mesh,
        in_specs=(
            P(None, "gx", "yz", None),
            P(None, "gx", "yz", None),
            P(("gx", "yz"), None),
            P(("gx", "yz")),
        ),
        out_specs=P(None, "gx", "yz", None),
        check_vma=False,
    )
```

```python
import jax
import jax.numpy as jnp
from jax import lax
from jax.experimental import pallas as pl
from jax.experimental.pallas import tpu as pltpu
from jax.sharding import PartitionSpec as P


BY = 8
BZ = 128
ZB = 4
CHUNKS = 12
ROWS = 14
BACK = 13
EXTRA = 12
KEPT = 13
CORNER = 48
SLICE = 16
HALF = 64
LINE_KEPT = 52
PACKED = 16
F32 = jnp.float32
BF16 = jnp.bfloat16


def iota(shape, dimension):
    return lax.broadcasted_iota(jnp.int32, shape, dimension)


def sign_of(place, cell, length):
    span = jnp.where(place == 0, length, 2 * (place & -place))
    sign = jnp.where((cell < place) | (place == 0), 1.0, -1.0)
    return jnp.where((cell ^ place) < span, sign, 0.0)


def weight_of(place, cell, length):
    span = jnp.where(place == 0, length, 2 * (place & -place))
    return sign_of(place, cell, length) / span.astype(F32)


def mix_table(wide):
    coarse = iota((8, BZ), 1)
    parts = []
    for block in range(wide // BZ):
        row = weight_of(jnp.minimum(coarse, ZB - 1), jnp.int32(block), ZB)
        row = jnp.where(coarse < ZB, row - jnp.where(coarse == block, 1.0, 0.0), 0.0) / BZ
        parts.append(jnp.broadcast_to(row[0:1], (BZ, BZ)))
    return jnp.concatenate(parts, axis=0).astype(BF16)


def unmix_table(wide):
    block = iota((8, BZ), 1)
    parts = []
    for coarse in range(wide // BZ):
        row = sign_of(jnp.int32(coarse), jnp.minimum(block, ZB - 1), ZB)
        row = jnp.where(block < ZB, row - jnp.where(block == coarse, 1.0, 0.0), 0.0) / BZ
        parts.append(jnp.broadcast_to(row[0:1], (BZ, BZ)))
    return jnp.concatenate(parts, axis=0).astype(BF16)


def halves(value):
    high = value.astype(BF16)
    low = (value - high.astype(F32)).astype(BF16)
    return high, low


def left_product(table, value):
    high, low = halves(value)
    return jnp.dot(table, high, preferred_element_type=F32) + jnp.dot(
        table, low, preferred_element_type=F32
    )


def right_product(value, table):
    high, low = halves(value)
    return jnp.dot(high, table, preferred_element_type=F32) + jnp.dot(
        low, table, preferred_element_type=F32
    )


def remix(value, table):
    shift = right_product(value, table)
    return jnp.concatenate(
        [value[:, zb * BZ : (zb + 1) * BZ] + shift[:, zb : zb + 1] for zb in range(ZB)], axis=1
    )


def forward_levels(values):
    count = len(values)
    result = [None] * count
    step = 1
    while step < count:
        for place in range(step, count, 2 * step):
            low, high = values[place - step], values[place]
            result[place] = (low - high) * 0.5
            values[place - step] = (low + high) * 0.5
        step *= 2
    result[0] = values[0]
    return result


def inverse_levels(values):
    count = len(values)
    values = list(values)
    step = count // 2
    while step >= 1:
        for place in range(step, count, 2 * step):
            mean, detail = values[place - step], values[place]
            values[place - step] = mean + detail
            values[place] = mean - detail
        step //= 2
    return values


def pick_table(first, wide):
    lane, cell = iota((BZ, wide), 0), iota((BZ, wide), 1)
    return jnp.where(lane == (first + (cell >> 7)) & (BZ - 1), 1.0, 0.0).astype(BF16)


def head_kernel(counts_hbm, blocks_hbm, vort_hbm, send, line, counts, blocks, vort, sems):
    parts, cells, wide = vort.shape
    planes = cells // BY
    copies = [
        pltpu.make_async_copy(vort_hbm.at[c], vort.at[c], sems.at[c]) for c in range(parts)
    ]
    copies.append(pltpu.make_async_copy(blocks_hbm, blocks, sems.at[parts]))
    copies.append(pltpu.make_async_copy(counts_hbm, counts, sems.at[parts + 1]))
    for copy in reversed(copies):
        copy.start()
    row, column = iota((planes + BY, cells), 0), iota((planes + BY, cells), 1)
    fine = jnp.where(row - planes == column & (BY - 1), 1.0, 0.0) - 1.0 / BY
    table = jnp.where(
        row < planes,
        weight_of(jnp.minimum(row, planes - 1), column >> 3, planes) * (1.0 / BY),
        fine * (1.0 / planes),
    ).astype(BF16)
    mix = mix_table(wide)
    copies[parts].wait()
    copies[parts + 1].wait()
    nblocks = blocks.shape[1]
    square = (nblocks, nblocks)
    listed = (blocks[...] == iota(square, 0)) & (iota(square, 1) < counts[0])
    kept = lax.dot_general(
        jnp.ones((planes, nblocks), BF16),
        jnp.where(listed, 1.0, 0.0).astype(BF16),
        (((1,), (1,)), ((), ())),
        preferred_element_type=F32,
    )
    send[pl.ds(KEPT, planes, stride=ROWS), :] = jnp.minimum(kept, 1.0)
    lane, turn = iota((8, BZ), 1), iota((8, BZ), 0)
    extra = [jnp.zeros((8, BZ), F32) for zb in range(ZB)]
    for c in range(parts):
        copies[c].wait()
        rows = remix(jnp.dot(table, vort[c], preferred_element_type=F32), mix)
        for zb in range(ZB):
            chunk = c * ZB + zb
            part = rows[:, zb * BZ : (zb + 1) * BZ]
            send[pl.ds(chunk, planes, stride=ROWS), :] = part[0:planes]
            line[chunk * BY : (chunk + 1) * BY, :] = part[planes : planes + BY]
            turned = jnp.broadcast_to(part[0:1], (8, BZ))
            turned = pltpu.roll(turned, c * SLICE, 1) if c else turned
            extra[zb] = jnp.where(lane >> 4 == (7 - turn + c) & 7, turned, extra[zb])
    for zb in range(ZB):
        turned = pltpu.roll(extra[zb], 0, 1, stride=SLICE, stride_axis=0)
        turned = pltpu.roll(turned, SLICE, 1)
        for row in range(8):
            at = (zb * 8 + 7 - row) * ROWS + EXTRA
            send[at : at + 1, :] = turned[row : row + 1]


def level_tables(length):
    square = (length, length)
    forward = weight_of(iota(square, 0), iota(square, 1), length).astype(BF16)
    inverse = sign_of(iota(square, 1), iota(square, 0), length).astype(BF16)
    return forward, inverse


def plane_kernel(place, recv, after, back, corner):
    del after
    planes = recv.shape[0] // ROWS
    forward, inverse = level_tables(planes)
    extra = recv[pl.ds(EXTRA, planes, stride=ROWS), :]
    lane = iota((PACKED, BZ), 1)
    row = iota((PACKED, BZ), 0)
    heads = recv[KEPT : KEPT + 1, :]
    first = 4 * row + (place[1] >> 3)
    low = jnp.sum(jnp.where(lane == first, heads, 0.0), axis=1, keepdims=True)
    high = jnp.sum(jnp.where(lane == first + HALF, heads, 0.0), axis=1, keepdims=True)
    levels = left_product(forward, extra)
    packed = levels[0:PACKED] + pltpu.roll(levels[PACKED:planes], HALF, 1)
    packed = jnp.where(lane == CORNER, low, packed)
    packed = jnp.where(lane == HALF + CORNER, high, packed)
    own = jnp.where(lane >> 2 == place[1], heads, 0.0).astype(BF16)
    source, target = iota((BZ, BZ), 0), iota((BZ, BZ), 1)
    slot = jnp.where(target == LINE_KEPT + (source & 3), 1.0, 0.0).astype(BF16)
    packed = packed + jnp.dot(own, slot, preferred_element_type=F32)
    for g in range(corner.shape[0]):
        corner[g] = packed
    pick = jnp.where(iota((BZ, ZB * BZ), 0) & 3 == iota((BZ, ZB * BZ), 1) >> 7, 1.0, 0.0)
    own = recv[pl.ds(place[1] * ROWS + KEPT, 1), :]
    spread = jnp.where(iota((planes, BZ), 1) >> 2 == iota((planes, BZ), 0), own, 0.0)
    mask = jnp.dot(spread.astype(BF16), pick.astype(BF16), preferred_element_type=F32)
    for c in range(3):
        data = jnp.concatenate(
            [recv[pl.ds(c * ZB + zb, planes, stride=ROWS), :] for zb in range(ZB)], axis=1
        )
        data = left_product(inverse, left_product(forward, data) * mask)
        for zb in range(ZB):
            back[pl.ds(c * ZB + zb, planes, stride=BACK), :] = data[:, zb * BZ : (zb + 1) * BZ]


def details_kernel(place, recv, vort, after, detail):
    del after
    parts, cells, wide = vort.shape
    planes = cells // BY
    row, column = iota((cells, planes), 0), iota((cells, planes), 1)
    span = jnp.maximum(2 * (column & -column), 1).astype(F32)
    tall = jnp.where((row >> 3 == column) & (column > 0), 1.0 / span, 0.0).astype(BF16)
    kept = recv[pl.ds(KEPT, planes, stride=ROWS), :].astype(BF16)
    kept = jnp.dot(tall, kept, preferred_element_type=F32).astype(BF16)
    mask = jnp.dot(kept, pick_table(ZB * place[1], wide), preferred_element_type=F32)
    row, column = iota((cells, cells), 0), iota((cells, cells), 1)
    same = row & (BY - 1) == column & (BY - 1)
    sign = sign_of(row >> 3, column >> 3, planes)
    forward = (sign * jnp.where(same, 1.0 - 1.0 / BY, -1.0 / BY)).astype(BF16)
    sign = sign_of(column >> 3, row >> 3, planes)
    inverse = jnp.where(same, sign, 0.0).astype(BF16)
    mix, unmix = mix_table(wide), unmix_table(wide)
    for c in range(parts):
        rows = remix(jnp.dot(forward, vort[c], preferred_element_type=F32), mix)
        detail[c] = remix(left_product(inverse, rows * mask), unmix)


def corner_kernel(place, gathered, back_in, mine, other, after, back, means):
    del after
    means[...] = (mine[...] + other[...]) * 0.5
    slabs = gathered.shape[0]
    planes = back.shape[0] // BACK
    lane = iota((PACKED, BZ), 1)
    back[...] = back_in[...]
    values = forward_levels([gathered[g] for g in range(slabs)])
    total = jnp.zeros((PACKED, BZ), F32)
    for p in range(slabs):
        low = gathered[p, :, CORNER : CORNER + 1]
        high = gathered[p, :, HALF + CORNER : HALF + CORNER + 1]
        sign = sign_of(jnp.int32(p), place[0], slabs)
        total = total + values[p] * jnp.where(lane < HALF, low, high) * sign
    total = jnp.concatenate([total, pltpu.roll(total, HALF, 1)], axis=0)
    total = jnp.where(iota((planes, BZ), 1) < CORNER, total, 0.0)
    back[pl.ds(EXTRA, planes, stride=BACK), :] = left_product(level_tables(planes)[1], total)


def line_kernel(place, gathered, after, mine, one, two, three, half, other, total, mask):
    del after
    wanted = [gathered[0, 0:1, :]]
    for level in range(4):
        slab = ((place[0] >> (level + 1)) << (level + 1)) + (1 << level)
        wanted.append(gathered[jnp.minimum(slab, gathered.shape[0] - 1), 0:1, :])
    wanted += [jnp.zeros((1, BZ), F32)] * (8 - len(wanted))
    wanted = jnp.concatenate(wanted, axis=0).astype(BF16)
    mask[...] = jnp.dot(wanted, pick_table(LINE_KEPT, mask.shape[1]), preferred_element_type=F32)
    for chunk in range(CHUNKS):
        span = slice(chunk * BY, (chunk + 1) * BY)
        lanes = slice(chunk % ZB * BZ, (chunk % ZB + 1) * BZ)
        near, far = mine[span, :] + one[span, :], two[span, :] + three[span, :]
        result = (mine[span, :] - one[span, :]) * 0.5 * mask[1:2, lanes]
        result = result + (near - far) * 0.25 * mask[2:3, lanes]
        result = result + (half[span, :] - other[span, :]) * 0.5 * mask[3:4, lanes]
        total[span, :] = result


def finish_kernel(got, mine, other, partial, mask, detail, velocity, out_hbm, rows, out, sems):
    planes = got.shape[0] // BACK
    parts, cells, wide = velocity.shape
    inverse = level_tables(planes)[1]
    extra = got[pl.ds(EXTRA, planes, stride=BACK), :]
    slot, lane = iota((8, BZ), 0), iota((8, BZ), 1)
    turned = [
        pltpu.roll(extra[zb * 8 : (zb + 1) * 8], 0, 1, stride=SLICE, stride_axis=0)
        for zb in range(ZB)
    ]
    for c in range(parts):
        columns = []
        for zb in range(ZB):
            span = slice((c * ZB + zb) * BY, (c * ZB + zb + 1) * BY)
            lanes = slice(zb * BZ, (zb + 1) * BZ)
            last = (mine[span, :] - other[span, :]) * 0.5
            mean = (mine[span, :] + other[span, :]) * 0.5
            total = partial[span, :] + last * mask[4:5, lanes] + mean * mask[0:1, lanes]
            rows[parts * planes + c * BY : parts * planes + (c + 1) * BY, lanes] = total
            corner = jnp.where(lane >> 4 == (slot + c) & 7, turned[zb], 0.0)
            corner = jnp.sum(corner, axis=0, keepdims=True)
            corner = pltpu.roll(corner, BZ - c * SLICE, 1) if c else corner
            data = got[pl.ds(c * ZB + zb, planes, stride=BACK), :]
            columns.append(jnp.where(iota((planes, BZ), 0) == 0, corner, data))
        rows[c * planes : (c + 1) * planes, :] = left_product(
            inverse, jnp.concatenate(columns, axis=1)
        )
    rows[...] = remix(rows[...], unmix_table(wide))
    copies = []
    for x in range(planes):
        span = slice(x * BY, (x + 1) * BY)
        smooth = [
            detail[c, span, :]
            + rows[c * planes + x : c * planes + x + 1, :]
            + rows[parts * planes + c * BY : parts * planes + (c + 1) * BY, :]
            for c in range(parts)
        ]
        speed = [velocity[c, span, :].astype(F32) for c in range(parts)]
        for c in range(parts):
            a, b = (c + 1) % parts, (c + 2) % parts
            out[c, span, :] = (smooth[a] * speed[b] - smooth[b] * speed[a]).astype(BF16)
        if (x + 1) % 8 == 0:
            done = pl.ds((x - 7) * BY, 8 * BY)
            for c in range(parts):
                copies.append(
                    pltpu.make_async_copy(
                        out.at[c, done, :], out_hbm.at[c, done, :], sems.at[len(copies)]
                    )
                )
                copies[-1].start()
    for copy in copies:
        copy.wait()


def exchange(value, axis):
    return lax.all_to_all(value, axis, split_axis=0, concat_axis=0, tiled=True)


def over_yz(rows, planes):
    moved = exchange(rows.reshape(planes, -1, 1, BZ), "yz")
    return moved.reshape(rows.shape)


def from_partner(value, distance):
    if distance >= lax.axis_size("gx"):
        return value
    pairs = [(source, source ^ distance) for source in range(lax.axis_size("gx"))]
    return lax.ppermute(value, "gx", pairs)


def body(vorticity, velocity, blocks, counts):
    parts, planes, tall, wide = vorticity.shape
    cells = planes * tall
    slabs = lax.axis_size("gx")
    smem = pl.BlockSpec(memory_space=pltpu.SMEM)
    vmem = pl.BlockSpec(memory_space=pltpu.VMEM)
    loose = pl.BlockSpec(memory_space=pl.ANY)
    params = pltpu.CompilerParams(vmem_limit_bytes=32 * 1024 * 1024)
    place = jnp.stack([lax.axis_index("gx"), lax.axis_index("yz")]).astype(jnp.int32)
    vort = vorticity.reshape(parts, cells, wide)
    line_shape = (CHUNKS * BY, BZ)

    def array(*shape):
        return jax.ShapeDtypeStruct(shape, F32)

    def call(kernel, name, out_shape, in_specs, scratch=(), cost=None, params=params, out=vmem):
        many = isinstance(out_shape, tuple)
        return pl.pallas_call(
            kernel,
            out_shape=out_shape,
            in_specs=in_specs,
            out_specs=tuple(out for _ in out_shape) if many else out,
            scratch_shapes=list(scratch),
            compiler_params=params,
            cost_estimate=cost,
            name=name,
        )

    def cost(products):
        return pl.CostEstimate(
            flops=products * 2 * parts * cells * cells * wide,
            bytes_accessed=10 * parts * cells * wide,
            transcendentals=0,
        )

    vort_scratch = pltpu.VMEM((parts, cells, wide), BF16)
    send, line = call(
        head_kernel,
        "head",
        (array(planes * ROWS, BZ), array(*line_shape)),
        [loose] * 3,
        [
            pltpu.SMEM(counts.shape, jnp.int32),
            pltpu.VMEM(blocks.shape, jnp.int32),
            vort_scratch,
            pltpu.SemaphoreType.DMA((parts + 2,)),
        ],
        params=pltpu.CompilerParams(vmem_limit_bytes=60 * 1024 * 1024),
    )(counts, blocks, vort)
    recv = over_yz(send, planes)
    near = [from_partner(line, distance) for distance in (1, 2, 3)]
    half = (line + near[0] + (near[1] + near[2])) * 0.25
    back, corner = call(
        plane_kernel,
        "plane",
        (array(planes * BACK, BZ), array(slabs, PACKED, BZ)),
        [smem, vmem, loose],
    )(place, recv, half)
    gathered = exchange(corner, "gx")
    opposite = from_partner(half, 4)
    detail = call(
        details_kernel,
        "details",
        array(parts, cells, wide),
        [smem, vmem, vmem, loose],
        cost=cost(7),
    )(place, recv, vort, corner)
    back, means = call(
        corner_kernel,
        "corner",
        (array(planes * BACK, BZ), array(*line_shape)),
        [smem] + [vmem] * 4 + [loose],
    )(place, gathered, back, half, opposite, detail)
    got = over_yz(back, planes)
    other = from_partner(means, 8)
    partial, mask = call(
        line_kernel,
        "line",
        (array(*line_shape), array(8, wide)),
        [smem, vmem, loose] + [vmem] * 6,
    )(place, gathered, means, line, *near, half, opposite)
    out = call(
        finish_kernel,
        "finish",
        jax.ShapeDtypeStruct((parts, cells, wide), BF16),
        [vmem] * 7,
        [
            pltpu.VMEM((parts * (planes + tall), wide), F32),
            pltpu.VMEM((parts, cells, wide), BF16),
            pltpu.SemaphoreType.DMA((parts * planes // 8,)),
        ],
        out=loose,
    )(got, means, other, partial, mask, detail, velocity.reshape(parts, cells, wide))
    return out.reshape(parts, planes, tall, wide)


def solution(mesh):
    return jax.shard_map(
        body,
        mesh=mesh,
        in_specs=(
            P(None, "gx", "yz", None),
            P(None, "gx", "yz", None),
            P(("gx", "yz"), None),
            P(("gx", "yz")),
        ),
        out_specs=P(None, "gx", "yz", None),
        check_vma=False,
    )
```

```python
import jax
import jax.numpy as jnp
from jax import lax
from jax.experimental import pallas as pl
from jax.experimental.pallas import tpu as pltpu
from jax.sharding import PartitionSpec as P


BY = 8
BZ = 128
ZB = 4
CHUNKS = 12
ROWS = 14
BACK = 13
EXTRA = 12
KEPT = 13
CORNER = 48
SLICE = 16
HALF = 64
LINE_KEPT = 52
PACKED = 16
PIECES = 4
F32 = jnp.float32
BF16 = jnp.bfloat16


def iota(shape, dimension):
    return lax.broadcasted_iota(jnp.int32, shape, dimension)


def sign_of(place, cell, length):
    span = jnp.where(place == 0, length, 2 * (place & -place))
    sign = jnp.where((cell < place) | (place == 0), 1.0, -1.0)
    return jnp.where((cell ^ place) < span, sign, 0.0)


def weight_of(place, cell, length):
    span = jnp.where(place == 0, length, 2 * (place & -place))
    return sign_of(place, cell, length) / span.astype(F32)


def mix_table(wide):
    coarse = iota((8, BZ), 1)
    parts = []
    for block in range(wide // BZ):
        row = weight_of(jnp.minimum(coarse, ZB - 1), jnp.int32(block), ZB)
        row = jnp.where(coarse < ZB, row - jnp.where(coarse == block, 1.0, 0.0), 0.0) / BZ
        parts.append(jnp.broadcast_to(row[0:1], (BZ, BZ)))
    return jnp.concatenate(parts, axis=0).astype(BF16)


def unmix_table(wide):
    block = iota((8, BZ), 1)
    parts = []
    for coarse in range(wide // BZ):
        row = sign_of(jnp.int32(coarse), jnp.minimum(block, ZB - 1), ZB)
        row = jnp.where(block < ZB, row - jnp.where(block == coarse, 1.0, 0.0), 0.0) / BZ
        parts.append(jnp.broadcast_to(row[0:1], (BZ, BZ)))
    return jnp.concatenate(parts, axis=0).astype(BF16)


def halves(value):
    high = value.astype(BF16)
    low = (value - high.astype(F32)).astype(BF16)
    return high, low


def left_product(table, value):
    high, low = halves(value)
    return jnp.dot(table, high, preferred_element_type=F32) + jnp.dot(
        table, low, preferred_element_type=F32
    )


def right_product(value, table):
    high, low = halves(value)
    return jnp.dot(high, table, preferred_element_type=F32) + jnp.dot(
        low, table, preferred_element_type=F32
    )


def remix(value, table):
    shift = right_product(value, table)
    return jnp.concatenate(
        [value[:, zb * BZ : (zb + 1) * BZ] + shift[:, zb : zb + 1] for zb in range(ZB)], axis=1
    )


def forward_levels(values):
    count = len(values)
    result = [None] * count
    step = 1
    while step < count:
        for place in range(step, count, 2 * step):
            low, high = values[place - step], values[place]
            result[place] = (low - high) * 0.5
            values[place - step] = (low + high) * 0.5
        step *= 2
    result[0] = values[0]
    return result


def inverse_levels(values):
    count = len(values)
    values = list(values)
    step = count // 2
    while step >= 1:
        for place in range(step, count, 2 * step):
            mean, detail = values[place - step], values[place]
            values[place - step] = mean + detail
            values[place] = mean - detail
        step //= 2
    return values


def pick_table(first, wide):
    lane, cell = iota((BZ, wide), 0), iota((BZ, wide), 1)
    return jnp.where(lane == (first + (cell >> 7)) & (BZ - 1), 1.0, 0.0).astype(BF16)


def head_kernel(counts_hbm, blocks_hbm, vort_hbm, send, line, counts, blocks, vort, sems):
    parts, cells, wide = vort.shape
    planes = cells // BY
    lists = [
        pltpu.make_async_copy(blocks_hbm, blocks, sems.at[parts * PIECES]),
        pltpu.make_async_copy(counts_hbm, counts, sems.at[parts * PIECES + 1]),
    ]
    for copy in lists:
        copy.start()
    copies = []
    size = cells // PIECES
    for c in range(parts):
        for piece in range(PIECES):
            part = pl.ds(piece * size, size)
            copies.append(
                pltpu.make_async_copy(
                    vort_hbm.at[c, part, :], vort.at[c, part, :], sems.at[len(copies)]
                )
            )
            copies[-1].start()
    row, column = iota((planes + BY, cells), 0), iota((planes + BY, cells), 1)
    fine = jnp.where(row - planes == column & (BY - 1), 1.0, 0.0) - 1.0 / BY
    table = jnp.where(
        row < planes,
        weight_of(jnp.minimum(row, planes - 1), column >> 3, planes) * (1.0 / BY),
        fine * (1.0 / planes),
    ).astype(BF16)
    mix = mix_table(wide)
    for copy in lists:
        copy.wait()
    nblocks = blocks.shape[1]
    square = (nblocks, nblocks)
    listed = (blocks[...] == iota(square, 0)) & (iota(square, 1) < counts[0])
    kept = lax.dot_general(
        jnp.ones((planes, nblocks), BF16),
        jnp.where(listed, 1.0, 0.0).astype(BF16),
        (((1,), (1,)), ((), ())),
        preferred_element_type=F32,
    )
    send[pl.ds(KEPT, planes, stride=ROWS), :] = jnp.minimum(kept, 1.0)
    lane, turn = iota((8, BZ), 1), iota((8, BZ), 0)
    extra = [jnp.zeros((8, BZ), F32) for zb in range(ZB)]
    for c in range(parts):
        for piece in range(PIECES):
            copies[c * PIECES + piece].wait()
        rows = remix(jnp.dot(table, vort[c], preferred_element_type=F32), mix)
        for zb in range(ZB):
            chunk = c * ZB + zb
            part = rows[:, zb * BZ : (zb + 1) * BZ]
            send[pl.ds(chunk, planes, stride=ROWS), :] = part[0:planes]
            line[chunk * BY : (chunk + 1) * BY, :] = part[planes : planes + BY]
            turned = jnp.broadcast_to(part[0:1], (8, BZ))
            turned = pltpu.roll(turned, c * SLICE, 1) if c else turned
            extra[zb] = jnp.where(lane >> 4 == (7 - turn + c) & 7, turned, extra[zb])
    for zb in range(ZB):
        turned = pltpu.roll(extra[zb], 0, 1, stride=SLICE, stride_axis=0)
        turned = pltpu.roll(turned, SLICE, 1)
        for row in range(8):
            at = (zb * 8 + 7 - row) * ROWS + EXTRA
            send[at : at + 1, :] = turned[row : row + 1]


def level_tables(length):
    square = (length, length)
    forward = weight_of(iota(square, 0), iota(square, 1), length).astype(BF16)
    inverse = sign_of(iota(square, 1), iota(square, 0), length).astype(BF16)
    return forward, inverse


def plane_kernel(place, recv, after, back, corner):
    del after
    planes = recv.shape[0] // ROWS
    forward, inverse = level_tables(planes)
    extra = recv[pl.ds(EXTRA, planes, stride=ROWS), :]
    lane = iota((PACKED, BZ), 1)
    row = iota((PACKED, BZ), 0)
    heads = recv[KEPT : KEPT + 1, :]
    first = 4 * row + (place[1] >> 3)
    low = jnp.sum(jnp.where(lane == first, heads, 0.0), axis=1, keepdims=True)
    high = jnp.sum(jnp.where(lane == first + HALF, heads, 0.0), axis=1, keepdims=True)
    levels = left_product(forward, extra)
    packed = levels[0:PACKED] + pltpu.roll(levels[PACKED:planes], HALF, 1)
    packed = jnp.where(lane == CORNER, low, packed)
    packed = jnp.where(lane == HALF + CORNER, high, packed)
    own = jnp.where(lane >> 2 == place[1], heads, 0.0).astype(BF16)
    source, target = iota((BZ, BZ), 0), iota((BZ, BZ), 1)
    slot = jnp.where(target == LINE_KEPT + (source & 3), 1.0, 0.0).astype(BF16)
    packed = packed + jnp.dot(own, slot, preferred_element_type=F32)
    for g in range(corner.shape[0]):
        corner[g] = packed
    pick = jnp.where(iota((BZ, ZB * BZ), 0) & 3 == iota((BZ, ZB * BZ), 1) >> 7, 1.0, 0.0)
    own = recv[pl.ds(place[1] * ROWS + KEPT, 1), :]
    spread = jnp.where(iota((planes, BZ), 1) >> 2 == iota((planes, BZ), 0), own, 0.0)
    mask = jnp.dot(spread.astype(BF16), pick.astype(BF16), preferred_element_type=F32)
    for c in range(3):
        data = jnp.concatenate(
            [recv[pl.ds(c * ZB + zb, planes, stride=ROWS), :] for zb in range(ZB)], axis=1
        )
        data = left_product(inverse, left_product(forward, data) * mask)
        for zb in range(ZB):
            back[pl.ds(c * ZB + zb, planes, stride=BACK), :] = data[:, zb * BZ : (zb + 1) * BZ]


def details_kernel(place, recv, vort, after, detail):
    del after
    parts, cells, wide = vort.shape
    planes = cells // BY
    row, column = iota((cells, planes), 0), iota((cells, planes), 1)
    span = jnp.maximum(2 * (column & -column), 1).astype(F32)
    tall = jnp.where((row >> 3 == column) & (column > 0), 1.0 / span, 0.0).astype(BF16)
    kept = recv[pl.ds(KEPT, planes, stride=ROWS), :].astype(BF16)
    kept = jnp.dot(tall, kept, preferred_element_type=F32).astype(BF16)
    mask = jnp.dot(kept, pick_table(ZB * place[1], wide), preferred_element_type=F32)
    row, column = iota((cells, cells), 0), iota((cells, cells), 1)
    same = row & (BY - 1) == column & (BY - 1)
    sign = sign_of(row >> 3, column >> 3, planes)
    forward = (sign * jnp.where(same, 1.0 - 1.0 / BY, -1.0 / BY)).astype(BF16)
    sign = sign_of(column >> 3, row >> 3, planes)
    inverse = jnp.where(same, sign, 0.0).astype(BF16)
    mix, unmix = mix_table(wide), unmix_table(wide)
    for c in range(parts):
        rows = remix(jnp.dot(forward, vort[c], preferred_element_type=F32), mix)
        detail[c] = remix(left_product(inverse, rows * mask), unmix)


def corner_kernel(place, gathered, back_in, mine, other, after, back, means):
    del after
    means[...] = (mine[...] + other[...]) * 0.5
    slabs = gathered.shape[0]
    planes = back.shape[0] // BACK
    lane = iota((PACKED, BZ), 1)
    back[...] = back_in[...]
    values = forward_levels([gathered[g] for g in range(slabs)])
    total = jnp.zeros((PACKED, BZ), F32)
    for p in range(slabs):
        low = gathered[p, :, CORNER : CORNER + 1]
        high = gathered[p, :, HALF + CORNER : HALF + CORNER + 1]
        sign = sign_of(jnp.int32(p), place[0], slabs)
        total = total + values[p] * jnp.where(lane < HALF, low, high) * sign
    total = jnp.concatenate([total, pltpu.roll(total, HALF, 1)], axis=0)
    total = jnp.where(iota((planes, BZ), 1) < CORNER, total, 0.0)
    back[pl.ds(EXTRA, planes, stride=BACK), :] = left_product(level_tables(planes)[1], total)


def line_kernel(place, gathered, after, mine, one, two, three, half, other, total, mask):
    del after
    wanted = [gathered[0, 0:1, :]]
    for level in range(4):
        slab = ((place[0] >> (level + 1)) << (level + 1)) + (1 << level)
        wanted.append(gathered[jnp.minimum(slab, gathered.shape[0] - 1), 0:1, :])
    wanted += [jnp.zeros((1, BZ), F32)] * (8 - len(wanted))
    wanted = jnp.concatenate(wanted, axis=0).astype(BF16)
    mask[...] = jnp.dot(wanted, pick_table(LINE_KEPT, mask.shape[1]), preferred_element_type=F32)
    for chunk in range(CHUNKS):
        span = slice(chunk * BY, (chunk + 1) * BY)
        lanes = slice(chunk % ZB * BZ, (chunk % ZB + 1) * BZ)
        near, far = mine[span, :] + one[span, :], two[span, :] + three[span, :]
        result = (mine[span, :] - one[span, :]) * 0.5 * mask[1:2, lanes]
        result = result + (near - far) * 0.25 * mask[2:3, lanes]
        result = result + (half[span, :] - other[span, :]) * 0.5 * mask[3:4, lanes]
        total[span, :] = result


def finish_kernel(got, mine, other, partial, mask, detail, velocity, out_hbm, rows, line, out, sems):
    planes = got.shape[0] // BACK
    parts, cells, wide = velocity.shape
    inverse = level_tables(planes)[1]
    extra = got[pl.ds(EXTRA, planes, stride=BACK), :]
    slot, lane = iota((8, BZ), 0), iota((8, BZ), 1)
    turned = [
        pltpu.roll(extra[zb * 8 : (zb + 1) * 8], 0, 1, stride=SLICE, stride_axis=0)
        for zb in range(ZB)
    ]
    for c in range(parts):
        columns = []
        for zb in range(ZB):
            span = slice((c * ZB + zb) * BY, (c * ZB + zb + 1) * BY)
            lanes = slice(zb * BZ, (zb + 1) * BZ)
            last = (mine[span, :] - other[span, :]) * 0.5
            mean = (mine[span, :] + other[span, :]) * 0.5
            total = partial[span, :] + last * mask[4:5, lanes] + mean * mask[0:1, lanes]
            line[c * BY : (c + 1) * BY, lanes] = total
            corner = jnp.where(lane >> 4 == (slot + c) & 7, turned[zb], 0.0)
            corner = jnp.sum(corner, axis=0, keepdims=True)
            corner = pltpu.roll(corner, BZ - c * SLICE, 1) if c else corner
            data = got[pl.ds(c * ZB + zb, planes, stride=BACK), :]
            columns.append(jnp.where(iota((planes, BZ), 0) == 0, corner, data))
        rows[c * planes : (c + 1) * planes, :] = left_product(
            inverse, jnp.concatenate(columns, axis=1)
        )
    unmix = unmix_table(wide)
    line[...] = remix(line[...], unmix)
    rows[...] = remix(rows[...], unmix)
    copies = []
    for x in range(planes):
        span = slice(x * BY, (x + 1) * BY)
        smooth = [
            detail[c, span, :]
            + rows[c * planes + x : c * planes + x + 1, :]
            + line[c * BY : (c + 1) * BY, :]
            for c in range(parts)
        ]
        speed = [velocity[c, span, :].astype(F32) for c in range(parts)]
        for c in range(parts):
            a, b = (c + 1) % parts, (c + 2) % parts
            out[c, span, :] = (smooth[a] * speed[b] - smooth[b] * speed[a]).astype(BF16)
        if (x + 1) % 8 == 0:
            done = pl.ds((x - 7) * BY, 8 * BY)
            for c in range(parts):
                copies.append(
                    pltpu.make_async_copy(
                        out.at[c, done, :], out_hbm.at[c, done, :], sems.at[len(copies)]
                    )
                )
                copies[-1].start()
    for copy in copies:
        copy.wait()


def exchange(value, axis):
    return lax.all_to_all(value, axis, split_axis=0, concat_axis=0, tiled=True)


def over_yz(rows, planes):
    moved = exchange(rows.reshape(planes, -1, 1, BZ), "yz")
    return moved.reshape(rows.shape)


def from_partner(value, distance):
    if distance >= lax.axis_size("gx"):
        return value
    pairs = [(source, source ^ distance) for source in range(lax.axis_size("gx"))]
    return lax.ppermute(value, "gx", pairs)


def body(vorticity, velocity, blocks, counts):
    parts, planes, tall, wide = vorticity.shape
    cells = planes * tall
    slabs = lax.axis_size("gx")
    smem = pl.BlockSpec(memory_space=pltpu.SMEM)
    vmem = pl.BlockSpec(memory_space=pltpu.VMEM)
    loose = pl.BlockSpec(memory_space=pl.ANY)
    params = pltpu.CompilerParams(vmem_limit_bytes=32 * 1024 * 1024)
    place = jnp.stack([lax.axis_index("gx"), lax.axis_index("yz")]).astype(jnp.int32)
    vort = vorticity.reshape(parts, cells, wide)
    line_shape = (CHUNKS * BY, BZ)

    def array(*shape):
        return jax.ShapeDtypeStruct(shape, F32)

    def call(kernel, name, out_shape, in_specs, scratch=(), cost=None, params=params, out=vmem):
        many = isinstance(out_shape, tuple)
        return pl.pallas_call(
            kernel,
            out_shape=out_shape,
            in_specs=in_specs,
            out_specs=tuple(out for _ in out_shape) if many else out,
            scratch_shapes=list(scratch),
            compiler_params=params,
            cost_estimate=cost,
            name=name,
        )

    def cost(products):
        return pl.CostEstimate(
            flops=products * 2 * parts * cells * cells * wide,
            bytes_accessed=10 * parts * cells * wide,
            transcendentals=0,
        )

    vort_scratch = pltpu.VMEM((parts, cells, wide), BF16)
    send, line = call(
        head_kernel,
        "head",
        (array(planes * ROWS, BZ), array(*line_shape)),
        [loose] * 3,
        [
            pltpu.SMEM(counts.shape, jnp.int32),
            pltpu.VMEM(blocks.shape, jnp.int32),
            vort_scratch,
            pltpu.SemaphoreType.DMA((parts * PIECES + 2,)),
        ],
        params=pltpu.CompilerParams(vmem_limit_bytes=60 * 1024 * 1024),
    )(counts, blocks, vort)
    recv = over_yz(send, planes)
    near = [from_partner(line, distance) for distance in (1, 2, 3)]
    half = (line + near[0] + (near[1] + near[2])) * 0.25
    back, corner = call(
        plane_kernel,
        "plane",
        (array(planes * BACK, BZ), array(slabs, PACKED, BZ)),
        [smem, vmem, loose],
    )(place, recv, half)
    gathered = exchange(corner, "gx")
    opposite = from_partner(half, 4)
    detail = call(
        details_kernel,
        "details",
        array(parts, cells, wide),
        [smem, vmem, vmem, loose],
        cost=cost(7),
    )(place, recv, vort, corner)
    back, means = call(
        corner_kernel,
        "corner",
        (array(planes * BACK, BZ), array(*line_shape)),
        [smem] + [vmem] * 4 + [loose],
    )(place, gathered, back, half, opposite, detail)
    got = over_yz(back, planes)
    other = from_partner(means, 8)
    partial, mask = call(
        line_kernel,
        "line",
        (array(*line_shape), array(8, wide)),
        [smem, vmem, loose] + [vmem] * 6,
    )(place, gathered, means, line, *near, half, opposite)
    out = call(
        finish_kernel,
        "finish",
        jax.ShapeDtypeStruct((parts, cells, wide), BF16),
        [vmem] * 7,
        [
            pltpu.VMEM((parts * planes, wide), F32),
            pltpu.VMEM((parts * tall, wide), F32),
            pltpu.VMEM((parts, cells, wide), BF16),
            pltpu.SemaphoreType.DMA((parts * planes // 8,)),
        ],
        out=loose,
    )(got, means, other, partial, mask, detail, velocity.reshape(parts, cells, wide))
    return out.reshape(parts, planes, tall, wide)


def solution(mesh):
    return jax.shard_map(
        body,
        mesh=mesh,
        in_specs=(
            P(None, "gx", "yz", None),
            P(None, "gx", "yz", None),
            P(("gx", "yz"), None),
            P(("gx", "yz")),
        ),
        out_specs=P(None, "gx", "yz", None),
        check_vma=False,
    )
```

```python
import jax
import jax.numpy as jnp
from jax import lax
from jax.experimental import pallas as pl
from jax.experimental.pallas import tpu as pltpu
from jax.sharding import PartitionSpec as P


BY = 8
BZ = 128
ZB = 4
CHUNKS = 12
ROWS = 14
BACK = 13
EXTRA = 12
KEPT = 13
CORNER = 48
SLICE = 16
HALF = 64
LINE_KEPT = 52
PACKED = 16
PIECES = 4
F32 = jnp.float32
BF16 = jnp.bfloat16


def iota(shape, dimension):
    return lax.broadcasted_iota(jnp.int32, shape, dimension)


def sign_of(place, cell, length):
    span = jnp.where(place == 0, length, 2 * (place & -place))
    sign = jnp.where((cell < place) | (place == 0), 1.0, -1.0)
    return jnp.where((cell ^ place) < span, sign, 0.0)


def weight_of(place, cell, length):
    span = jnp.where(place == 0, length, 2 * (place & -place))
    return sign_of(place, cell, length) / span.astype(F32)


def mix_table(wide):
    coarse = iota((8, BZ), 1)
    parts = []
    for block in range(wide // BZ):
        row = weight_of(jnp.minimum(coarse, ZB - 1), jnp.int32(block), ZB)
        row = jnp.where(coarse < ZB, row - jnp.where(coarse == block, 1.0, 0.0), 0.0) / BZ
        parts.append(jnp.broadcast_to(row[0:1], (BZ, BZ)))
    return jnp.concatenate(parts, axis=0).astype(BF16)


def unmix_table(wide):
    block = iota((8, BZ), 1)
    parts = []
    for coarse in range(wide // BZ):
        row = sign_of(jnp.int32(coarse), jnp.minimum(block, ZB - 1), ZB)
        row = jnp.where(block < ZB, row - jnp.where(block == coarse, 1.0, 0.0), 0.0) / BZ
        parts.append(jnp.broadcast_to(row[0:1], (BZ, BZ)))
    return jnp.concatenate(parts, axis=0).astype(BF16)


def halves(value):
    high = value.astype(BF16)
    low = (value - high.astype(F32)).astype(BF16)
    return high, low


def left_product(table, value):
    high, low = halves(value)
    return jnp.dot(table, high, preferred_element_type=F32) + jnp.dot(
        table, low, preferred_element_type=F32
    )


def right_product(value, table):
    high, low = halves(value)
    return jnp.dot(high, table, preferred_element_type=F32) + jnp.dot(
        low, table, preferred_element_type=F32
    )


def remix(value, table):
    shift = right_product(value, table)
    return jnp.concatenate(
        [value[:, zb * BZ : (zb + 1) * BZ] + shift[:, zb : zb + 1] for zb in range(ZB)], axis=1
    )


def forward_levels(values):
    count = len(values)
    result = [None] * count
    step = 1
    while step < count:
        for place in range(step, count, 2 * step):
            low, high = values[place - step], values[place]
            result[place] = (low - high) * 0.5
            values[place - step] = (low + high) * 0.5
        step *= 2
    result[0] = values[0]
    return result


def inverse_levels(values):
    count = len(values)
    values = list(values)
    step = count // 2
    while step >= 1:
        for place in range(step, count, 2 * step):
            mean, detail = values[place - step], values[place]
            values[place - step] = mean + detail
            values[place] = mean - detail
        step //= 2
    return values


def pick_table(first, wide):
    lane, cell = iota((BZ, wide), 0), iota((BZ, wide), 1)
    return jnp.where(lane == (first + (cell >> 7)) & (BZ - 1), 1.0, 0.0).astype(BF16)


def head_kernel(counts_hbm, blocks_hbm, vort_hbm, send, line, counts, blocks, vort, sems):
    parts, cells, wide = vort.shape
    planes = cells // BY
    lists = [
        pltpu.make_async_copy(blocks_hbm, blocks, sems.at[parts * PIECES]),
        pltpu.make_async_copy(counts_hbm, counts, sems.at[parts * PIECES + 1]),
    ]
    for copy in lists:
        copy.start()
    copies = []
    size = cells // PIECES
    for c in range(parts):
        for piece in range(PIECES):
            part = pl.ds(piece * size, size)
            copies.append(
                pltpu.make_async_copy(
                    vort_hbm.at[c, part, :], vort.at[c, part, :], sems.at[len(copies)]
                )
            )
            copies[-1].start()
    row, column = iota((planes + BY, cells), 0), iota((planes + BY, cells), 1)
    fine = jnp.where(row - planes == column & (BY - 1), 1.0, 0.0) - 1.0 / BY
    table = jnp.where(
        row < planes,
        weight_of(jnp.minimum(row, planes - 1), column >> 3, planes) * (1.0 / BY),
        fine * (1.0 / planes),
    ).astype(BF16)
    mix = mix_table(wide)
    for copy in lists:
        copy.wait()
    nblocks = blocks.shape[1]
    square = (nblocks, nblocks)
    listed = (blocks[...] == iota(square, 0)) & (iota(square, 1) < counts[0])
    kept = lax.dot_general(
        jnp.ones((planes, nblocks), BF16),
        jnp.where(listed, 1.0, 0.0).astype(BF16),
        (((1,), (1,)), ((), ())),
        preferred_element_type=F32,
    )
    send[pl.ds(KEPT, planes, stride=ROWS), :] = jnp.minimum(kept, 1.0)
    lane, turn = iota((8, BZ), 1), iota((8, BZ), 0)
    extra = [jnp.zeros((8, BZ), F32) for zb in range(ZB)]
    for c in range(parts):
        for piece in range(PIECES):
            copies[c * PIECES + piece].wait()
        rows = remix(jnp.dot(table, vort[c], preferred_element_type=F32), mix)
        for zb in range(ZB):
            chunk = c * ZB + zb
            part = rows[:, zb * BZ : (zb + 1) * BZ]
            send[pl.ds(chunk, planes, stride=ROWS), :] = part[0:planes]
            line[chunk * BY : (chunk + 1) * BY, :] = part[planes : planes + BY]
            turned = jnp.broadcast_to(part[0:1], (8, BZ))
            turned = pltpu.roll(turned, c * SLICE, 1) if c else turned
            extra[zb] = jnp.where(lane >> 4 == (7 - turn + c) & 7, turned, extra[zb])
    for zb in range(ZB):
        turned = pltpu.roll(extra[zb], 0, 1, stride=SLICE, stride_axis=0)
        turned = pltpu.roll(turned, SLICE, 1)
        for row in range(8):
            at = (zb * 8 + 7 - row) * ROWS + EXTRA
            send[at : at + 1, :] = turned[row : row + 1]


def level_tables(length):
    square = (length, length)
    forward = weight_of(iota(square, 0), iota(square, 1), length).astype(BF16)
    inverse = sign_of(iota(square, 1), iota(square, 0), length).astype(BF16)
    return forward, inverse


def pack_kernel(place, recv, after, corner):
    del after
    planes = recv.shape[0] // ROWS
    forward = level_tables(planes)[0]
    extra = recv[pl.ds(EXTRA, planes, stride=ROWS), :]
    lane = iota((PACKED, BZ), 1)
    row = iota((PACKED, BZ), 0)
    heads = recv[KEPT : KEPT + 1, :]
    first = 4 * row + (place[1] >> 3)
    low = jnp.sum(jnp.where(lane == first, heads, 0.0), axis=1, keepdims=True)
    high = jnp.sum(jnp.where(lane == first + HALF, heads, 0.0), axis=1, keepdims=True)
    levels = left_product(forward, extra)
    packed = levels[0:PACKED] + pltpu.roll(levels[PACKED:planes], HALF, 1)
    packed = jnp.where(lane == CORNER, low, packed)
    packed = jnp.where(lane == HALF + CORNER, high, packed)
    own = jnp.where(lane >> 2 == place[1], heads, 0.0).astype(BF16)
    source, target = iota((BZ, BZ), 0), iota((BZ, BZ), 1)
    slot = jnp.where(target == LINE_KEPT + (source & 3), 1.0, 0.0).astype(BF16)
    packed = packed + jnp.dot(own, slot, preferred_element_type=F32)
    for g in range(corner.shape[0]):
        corner[g] = packed


def plane_kernel(place, recv, after, back):
    del after
    planes = recv.shape[0] // ROWS
    forward, inverse = level_tables(planes)
    pick = jnp.where(iota((BZ, ZB * BZ), 0) & 3 == iota((BZ, ZB * BZ), 1) >> 7, 1.0, 0.0)
    own = recv[pl.ds(place[1] * ROWS + KEPT, 1), :]
    spread = jnp.where(iota((planes, BZ), 1) >> 2 == iota((planes, BZ), 0), own, 0.0)
    mask = jnp.dot(spread.astype(BF16), pick.astype(BF16), preferred_element_type=F32)
    for c in range(3):
        data = jnp.concatenate(
            [recv[pl.ds(c * ZB + zb, planes, stride=ROWS), :] for zb in range(ZB)], axis=1
        )
        data = left_product(inverse, left_product(forward, data) * mask)
        for zb in range(ZB):
            back[pl.ds(c * ZB + zb, planes, stride=BACK), :] = data[:, zb * BZ : (zb + 1) * BZ]


def details_kernel(place, recv, vort, after, detail):
    del after
    parts, cells, wide = vort.shape
    planes = cells // BY
    row, column = iota((cells, planes), 0), iota((cells, planes), 1)
    span = jnp.maximum(2 * (column & -column), 1).astype(F32)
    tall = jnp.where((row >> 3 == column) & (column > 0), 1.0 / span, 0.0).astype(BF16)
    kept = recv[pl.ds(KEPT, planes, stride=ROWS), :].astype(BF16)
    kept = jnp.dot(tall, kept, preferred_element_type=F32).astype(BF16)
    mask = jnp.dot(kept, pick_table(ZB * place[1], wide), preferred_element_type=F32)
    row, column = iota((cells, cells), 0), iota((cells, cells), 1)
    same = row & (BY - 1) == column & (BY - 1)
    sign = sign_of(row >> 3, column >> 3, planes)
    forward = (sign * jnp.where(same, 1.0 - 1.0 / BY, -1.0 / BY)).astype(BF16)
    sign = sign_of(column >> 3, row >> 3, planes)
    inverse = jnp.where(same, sign, 0.0).astype(BF16)
    mix, unmix = mix_table(wide), unmix_table(wide)
    for c in range(parts):
        rows = remix(jnp.dot(forward, vort[c], preferred_element_type=F32), mix)
        detail[c] = remix(left_product(inverse, rows * mask), unmix)


def corner_kernel(place, gathered, back_in, mine, other, back, means):
    means[...] = (mine[...] + other[...]) * 0.5
    slabs = gathered.shape[0]
    planes = back.shape[0] // BACK
    lane = iota((PACKED, BZ), 1)
    back[...] = back_in[...]
    values = forward_levels([gathered[g] for g in range(slabs)])
    total = jnp.zeros((PACKED, BZ), F32)
    for p in range(slabs):
        low = gathered[p, :, CORNER : CORNER + 1]
        high = gathered[p, :, HALF + CORNER : HALF + CORNER + 1]
        sign = sign_of(jnp.int32(p), place[0], slabs)
        total = total + values[p] * jnp.where(lane < HALF, low, high) * sign
    total = jnp.concatenate([total, pltpu.roll(total, HALF, 1)], axis=0)
    total = jnp.where(iota((planes, BZ), 1) < CORNER, total, 0.0)
    back[pl.ds(EXTRA, planes, stride=BACK), :] = left_product(level_tables(planes)[1], total)


def line_kernel(place, gathered, after, mine, one, two, three, half, other, total, mask):
    del after
    wanted = [gathered[0, 0:1, :]]
    for level in range(4):
        slab = ((place[0] >> (level + 1)) << (level + 1)) + (1 << level)
        wanted.append(gathered[jnp.minimum(slab, gathered.shape[0] - 1), 0:1, :])
    wanted += [jnp.zeros((1, BZ), F32)] * (8 - len(wanted))
    wanted = jnp.concatenate(wanted, axis=0).astype(BF16)
    mask[...] = jnp.dot(wanted, pick_table(LINE_KEPT, mask.shape[1]), preferred_element_type=F32)
    for chunk in range(CHUNKS):
        span = slice(chunk * BY, (chunk + 1) * BY)
        lanes = slice(chunk % ZB * BZ, (chunk % ZB + 1) * BZ)
        near, far = mine[span, :] + one[span, :], two[span, :] + three[span, :]
        result = (mine[span, :] - one[span, :]) * 0.5 * mask[1:2, lanes]
        result = result + (near - far) * 0.25 * mask[2:3, lanes]
        result = result + (half[span, :] - other[span, :]) * 0.5 * mask[3:4, lanes]
        total[span, :] = result


def finish_kernel(got, mine, other, partial, mask, detail, velocity, out_hbm, rows, line, out, sems):
    planes = got.shape[0] // BACK
    parts, cells, wide = velocity.shape
    inverse = level_tables(planes)[1]
    extra = got[pl.ds(EXTRA, planes, stride=BACK), :]
    slot, lane = iota((8, BZ), 0), iota((8, BZ), 1)
    turned = [
        pltpu.roll(extra[zb * 8 : (zb + 1) * 8], 0, 1, stride=SLICE, stride_axis=0)
        for zb in range(ZB)
    ]
    for c in range(parts):
        columns = []
        for zb in range(ZB):
            span = slice((c * ZB + zb) * BY, (c * ZB + zb + 1) * BY)
            lanes = slice(zb * BZ, (zb + 1) * BZ)
            last = (mine[span, :] - other[span, :]) * 0.5
            mean = (mine[span, :] + other[span, :]) * 0.5
            total = partial[span, :] + last * mask[4:5, lanes] + mean * mask[0:1, lanes]
            line[c * BY : (c + 1) * BY, lanes] = total
            corner = jnp.where(lane >> 4 == (slot + c) & 7, turned[zb], 0.0)
            corner = jnp.sum(corner, axis=0, keepdims=True)
            corner = pltpu.roll(corner, BZ - c * SLICE, 1) if c else corner
            data = got[pl.ds(c * ZB + zb, planes, stride=BACK), :]
            columns.append(jnp.where(iota((planes, BZ), 0) == 0, corner, data))
        rows[c * planes : (c + 1) * planes, :] = left_product(
            inverse, jnp.concatenate(columns, axis=1)
        )
    unmix = unmix_table(wide)
    line[...] = remix(line[...], unmix)
    rows[...] = remix(rows[...], unmix)
    copies = []
    for x in range(planes):
        span = slice(x * BY, (x + 1) * BY)
        smooth = [
            detail[c, span, :]
            + rows[c * planes + x : c * planes + x + 1, :]
            + line[c * BY : (c + 1) * BY, :]
            for c in range(parts)
        ]
        speed = [velocity[c, span, :].astype(F32) for c in range(parts)]
        for c in range(parts):
            a, b = (c + 1) % parts, (c + 2) % parts
            out[c, span, :] = (smooth[a] * speed[b] - smooth[b] * speed[a]).astype(BF16)
        if (x + 1) % 8 == 0:
            done = pl.ds((x - 7) * BY, 8 * BY)
            for c in range(parts):
                copies.append(
                    pltpu.make_async_copy(
                        out.at[c, done, :], out_hbm.at[c, done, :], sems.at[len(copies)]
                    )
                )
                copies[-1].start()
    for copy in copies:
        copy.wait()


def exchange(value, axis):
    return lax.all_to_all(value, axis, split_axis=0, concat_axis=0, tiled=True)


def over_yz(rows, planes):
    moved = exchange(rows.reshape(planes, -1, 1, BZ), "yz")
    return moved.reshape(rows.shape)


def from_partner(value, distance):
    if distance >= lax.axis_size("gx"):
        return value
    pairs = [(source, source ^ distance) for source in range(lax.axis_size("gx"))]
    return lax.ppermute(value, "gx", pairs)


def body(vorticity, velocity, blocks, counts):
    parts, planes, tall, wide = vorticity.shape
    cells = planes * tall
    slabs = lax.axis_size("gx")
    smem = pl.BlockSpec(memory_space=pltpu.SMEM)
    vmem = pl.BlockSpec(memory_space=pltpu.VMEM)
    loose = pl.BlockSpec(memory_space=pl.ANY)
    params = pltpu.CompilerParams(vmem_limit_bytes=32 * 1024 * 1024)
    place = jnp.stack([lax.axis_index("gx"), lax.axis_index("yz")]).astype(jnp.int32)
    vort = vorticity.reshape(parts, cells, wide)
    line_shape = (CHUNKS * BY, BZ)

    def array(*shape):
        return jax.ShapeDtypeStruct(shape, F32)

    def call(kernel, name, out_shape, in_specs, scratch=(), cost=None, params=params, out=vmem):
        many = isinstance(out_shape, tuple)
        return pl.pallas_call(
            kernel,
            out_shape=out_shape,
            in_specs=in_specs,
            out_specs=tuple(out for _ in out_shape) if many else out,
            scratch_shapes=list(scratch),
            compiler_params=params,
            cost_estimate=cost,
            name=name,
        )

    def cost(products):
        return pl.CostEstimate(
            flops=products * 2 * parts * cells * cells * wide,
            bytes_accessed=10 * parts * cells * wide,
            transcendentals=0,
        )

    vort_scratch = pltpu.VMEM((parts, cells, wide), BF16)
    send, line = call(
        head_kernel,
        "head",
        (array(planes * ROWS, BZ), array(*line_shape)),
        [loose] * 3,
        [
            pltpu.SMEM(counts.shape, jnp.int32),
            pltpu.VMEM(blocks.shape, jnp.int32),
            vort_scratch,
            pltpu.SemaphoreType.DMA((parts * PIECES + 2,)),
        ],
        params=pltpu.CompilerParams(vmem_limit_bytes=60 * 1024 * 1024),
    )(counts, blocks, vort)
    recv = over_yz(send, planes)
    near = [from_partner(line, distance) for distance in (1, 2, 3)]
    half = (line + near[0] + (near[1] + near[2])) * 0.25
    corner = call(
        pack_kernel, "pack", array(slabs, PACKED, BZ), [smem, vmem, loose]
    )(place, recv, half)
    gathered = exchange(corner, "gx")
    opposite = from_partner(half, 4)
    back = call(
        plane_kernel, "plane", array(planes * BACK, BZ), [smem, vmem, loose]
    )(place, recv, corner)
    back, means = call(
        corner_kernel,
        "corner",
        (array(planes * BACK, BZ), array(*line_shape)),
        [smem] + [vmem] * 4,
    )(place, gathered, back, half, opposite)
    got = over_yz(back, planes)
    other = from_partner(means, 8)
    partial, mask = call(
        line_kernel,
        "line",
        (array(*line_shape), array(8, wide)),
        [smem, vmem, loose] + [vmem] * 6,
    )(place, gathered, means, line, *near, half, opposite)
    detail = call(
        details_kernel,
        "details",
        array(parts, cells, wide),
        [smem, vmem, vmem, loose],
        cost=cost(7),
    )(place, recv, vort, partial)
    out = call(
        finish_kernel,
        "finish",
        jax.ShapeDtypeStruct((parts, cells, wide), BF16),
        [vmem] * 7,
        [
            pltpu.VMEM((parts * planes, wide), F32),
            pltpu.VMEM((parts * tall, wide), F32),
            pltpu.VMEM((parts, cells, wide), BF16),
            pltpu.SemaphoreType.DMA((parts * planes // 8,)),
        ],
        out=loose,
    )(got, means, other, partial, mask, detail, velocity.reshape(parts, cells, wide))
    return out.reshape(parts, planes, tall, wide)


def solution(mesh):
    return jax.shard_map(
        body,
        mesh=mesh,
        in_specs=(
            P(None, "gx", "yz", None),
            P(None, "gx", "yz", None),
            P(("gx", "yz"), None),
            P(("gx", "yz")),
        ),
        out_specs=P(None, "gx", "yz", None),
        check_vma=False,
    )
```

```python
import jax
import jax.numpy as jnp
from jax import lax
from jax.experimental import pallas as pl
from jax.experimental.pallas import tpu as pltpu
from jax.sharding import PartitionSpec as P


BY = 8
BZ = 128
ZB = 4
CHUNKS = 12
ROWS = 14
BACK = 13
EXTRA = 12
KEPT = 13
CORNER = 48
SLICE = 16
HALF = 64
LINE_KEPT = 52
PACKED = 16
PIECES = 4
F32 = jnp.float32
BF16 = jnp.bfloat16


def iota(shape, dimension):
    return lax.broadcasted_iota(jnp.int32, shape, dimension)


def sign_of(place, cell, length):
    span = jnp.where(place == 0, length, 2 * (place & -place))
    sign = jnp.where((cell < place) | (place == 0), 1.0, -1.0)
    return jnp.where((cell ^ place) < span, sign, 0.0)


def weight_of(place, cell, length):
    span = jnp.where(place == 0, length, 2 * (place & -place))
    return sign_of(place, cell, length) / span.astype(F32)


def mix_table(wide):
    coarse = iota((8, BZ), 1)
    parts = []
    for block in range(wide // BZ):
        row = weight_of(jnp.minimum(coarse, ZB - 1), jnp.int32(block), ZB)
        row = jnp.where(coarse < ZB, row - jnp.where(coarse == block, 1.0, 0.0), 0.0) / BZ
        parts.append(jnp.broadcast_to(row[0:1], (BZ, BZ)))
    return jnp.concatenate(parts, axis=0).astype(BF16)


def unmix_table(wide):
    block = iota((8, BZ), 1)
    parts = []
    for coarse in range(wide // BZ):
        row = sign_of(jnp.int32(coarse), jnp.minimum(block, ZB - 1), ZB)
        row = jnp.where(block < ZB, row - jnp.where(block == coarse, 1.0, 0.0), 0.0) / BZ
        parts.append(jnp.broadcast_to(row[0:1], (BZ, BZ)))
    return jnp.concatenate(parts, axis=0).astype(BF16)


def halves(value):
    high = value.astype(BF16)
    low = (value - high.astype(F32)).astype(BF16)
    return high, low


def left_product(table, value):
    high, low = halves(value)
    return jnp.dot(table, high, preferred_element_type=F32) + jnp.dot(
        table, low, preferred_element_type=F32
    )


def right_product(value, table):
    high, low = halves(value)
    return jnp.dot(high, table, preferred_element_type=F32) + jnp.dot(
        low, table, preferred_element_type=F32
    )


def remix(value, table):
    shift = right_product(value, table)
    return jnp.concatenate(
        [value[:, zb * BZ : (zb + 1) * BZ] + shift[:, zb : zb + 1] for zb in range(ZB)], axis=1
    )


def forward_levels(values):
    count = len(values)
    result = [None] * count
    step = 1
    while step < count:
        for place in range(step, count, 2 * step):
            low, high = values[place - step], values[place]
            result[place] = (low - high) * 0.5
            values[place - step] = (low + high) * 0.5
        step *= 2
    result[0] = values[0]
    return result


def inverse_levels(values):
    count = len(values)
    values = list(values)
    step = count // 2
    while step >= 1:
        for place in range(step, count, 2 * step):
            mean, detail = values[place - step], values[place]
            values[place - step] = mean + detail
            values[place] = mean - detail
        step //= 2
    return values


def pick_table(first, wide):
    lane, cell = iota((BZ, wide), 0), iota((BZ, wide), 1)
    return jnp.where(lane == (first + (cell >> 7)) & (BZ - 1), 1.0, 0.0).astype(BF16)


def head_kernel(counts_hbm, blocks_hbm, vort_hbm, send, line, counts, blocks, vort, sems):
    parts, cells, wide = vort.shape
    planes = cells // BY
    lists = [
        pltpu.make_async_copy(blocks_hbm, blocks, sems.at[parts * PIECES]),
        pltpu.make_async_copy(counts_hbm, counts, sems.at[parts * PIECES + 1]),
    ]
    for copy in lists:
        copy.start()
    copies = []
    size = cells // PIECES
    for c in range(parts):
        for piece in range(PIECES):
            part = pl.ds(piece * size, size)
            copies.append(
                pltpu.make_async_copy(
                    vort_hbm.at[c, part, :], vort.at[c, part, :], sems.at[len(copies)]
                )
            )
            copies[-1].start()
    row, column = iota((planes + BY, cells), 0), iota((planes + BY, cells), 1)
    fine = jnp.where(row - planes == column & (BY - 1), 1.0, 0.0) - 1.0 / BY
    table = jnp.where(
        row < planes,
        weight_of(jnp.minimum(row, planes - 1), column >> 3, planes) * (1.0 / BY),
        fine * (1.0 / planes),
    ).astype(BF16)
    mix = mix_table(wide)
    for copy in lists:
        copy.wait()
    nblocks = blocks.shape[1]
    square = (nblocks, nblocks)
    listed = (blocks[...] == iota(square, 0)) & (iota(square, 1) < counts[0])
    kept = lax.dot_general(
        jnp.ones((planes, nblocks), BF16),
        jnp.where(listed, 1.0, 0.0).astype(BF16),
        (((1,), (1,)), ((), ())),
        preferred_element_type=F32,
    )
    send[pl.ds(KEPT, planes, stride=ROWS), :] = jnp.minimum(kept, 1.0)
    lane, turn = iota((8, BZ), 1), iota((8, BZ), 0)
    extra = [jnp.zeros((8, BZ), F32) for zb in range(ZB)]
    for c in range(parts):
        for piece in range(PIECES):
            copies[c * PIECES + piece].wait()
        rows = remix(jnp.dot(table, vort[c], preferred_element_type=F32), mix)
        for zb in range(ZB):
            chunk = c * ZB + zb
            part = rows[:, zb * BZ : (zb + 1) * BZ]
            send[pl.ds(chunk, planes, stride=ROWS), :] = part[0:planes]
            line[chunk * BY : (chunk + 1) * BY, :] = part[planes : planes + BY]
            turned = jnp.broadcast_to(part[0:1], (8, BZ))
            turned = pltpu.roll(turned, c * SLICE, 1) if c else turned
            extra[zb] = jnp.where(lane >> 4 == (7 - turn + c) & 7, turned, extra[zb])
    for zb in range(ZB):
        turned = pltpu.roll(extra[zb], 0, 1, stride=SLICE, stride_axis=0)
        turned = pltpu.roll(turned, SLICE, 1)
        for row in range(8):
            at = (zb * 8 + 7 - row) * ROWS + EXTRA
            send[at : at + 1, :] = turned[row : row + 1]


def own_place():
    return lax.axis_index("gx"), lax.axis_index("yz")


def level_tables(length):
    square = (length, length)
    forward = weight_of(iota(square, 0), iota(square, 1), length).astype(BF16)
    inverse = sign_of(iota(square, 1), iota(square, 0), length).astype(BF16)
    return forward, inverse


def plane_kernel(recv, after, back, corner):
    place = own_place()
    del after
    planes = recv.shape[0] // ROWS
    forward, inverse = level_tables(planes)
    extra = recv[pl.ds(EXTRA, planes, stride=ROWS), :]
    lane = iota((PACKED, BZ), 1)
    row = iota((PACKED, BZ), 0)
    heads = recv[KEPT : KEPT + 1, :]
    first = 4 * row + (place[1] >> 3)
    low = jnp.sum(jnp.where(lane == first, heads, 0.0), axis=1, keepdims=True)
    high = jnp.sum(jnp.where(lane == first + HALF, heads, 0.0), axis=1, keepdims=True)
    levels = left_product(forward, extra)
    packed = levels[0:PACKED] + pltpu.roll(levels[PACKED:planes], HALF, 1)
    packed = jnp.where(lane == CORNER, low, packed)
    packed = jnp.where(lane == HALF + CORNER, high, packed)
    own = jnp.where(lane >> 2 == place[1], heads, 0.0).astype(BF16)
    source, target = iota((BZ, BZ), 0), iota((BZ, BZ), 1)
    slot = jnp.where(target == LINE_KEPT + (source & 3), 1.0, 0.0).astype(BF16)
    packed = packed + jnp.dot(own, slot, preferred_element_type=F32)
    for g in range(corner.shape[0]):
        corner[g] = packed
    pick = jnp.where(iota((BZ, ZB * BZ), 0) & 3 == iota((BZ, ZB * BZ), 1) >> 7, 1.0, 0.0)
    own = recv[pl.ds(place[1] * ROWS + KEPT, 1), :]
    spread = jnp.where(iota((planes, BZ), 1) >> 2 == iota((planes, BZ), 0), own, 0.0)
    mask = jnp.dot(spread.astype(BF16), pick.astype(BF16), preferred_element_type=F32)
    for c in range(3):
        data = jnp.concatenate(
            [recv[pl.ds(c * ZB + zb, planes, stride=ROWS), :] for zb in range(ZB)], axis=1
        )
        data = left_product(inverse, left_product(forward, data) * mask)
        for zb in range(ZB):
            back[pl.ds(c * ZB + zb, planes, stride=BACK), :] = data[:, zb * BZ : (zb + 1) * BZ]


def details_kernel(recv, vort, after, detail):
    place = own_place()
    del after
    parts, cells, wide = vort.shape
    planes = cells // BY
    row, column = iota((cells, planes), 0), iota((cells, planes), 1)
    span = jnp.maximum(2 * (column & -column), 1).astype(F32)
    tall = jnp.where((row >> 3 == column) & (column > 0), 1.0 / span, 0.0).astype(BF16)
    kept = recv[pl.ds(KEPT, planes, stride=ROWS), :].astype(BF16)
    kept = jnp.dot(tall, kept, preferred_element_type=F32).astype(BF16)
    mask = jnp.dot(kept, pick_table(ZB * place[1], wide), preferred_element_type=F32)
    row, column = iota((cells, cells), 0), iota((cells, cells), 1)
    same = row & (BY - 1) == column & (BY - 1)
    sign = sign_of(row >> 3, column >> 3, planes)
    forward = (sign * jnp.where(same, 1.0 - 1.0 / BY, -1.0 / BY)).astype(BF16)
    sign = sign_of(column >> 3, row >> 3, planes)
    inverse = jnp.where(same, sign, 0.0).astype(BF16)
    mix, unmix = mix_table(wide), unmix_table(wide)
    for c in range(parts):
        rows = remix(jnp.dot(forward, vort[c], preferred_element_type=F32), mix)
        detail[c] = remix(left_product(inverse, rows * mask), unmix)


def corner_kernel(gathered, back_in, mine, other, after, back, means):
    place = own_place()
    del after
    means[...] = (mine[...] + other[...]) * 0.5
    slabs = gathered.shape[0]
    planes = back.shape[0] // BACK
    lane = iota((PACKED, BZ), 1)
    back[...] = back_in[...]
    values = forward_levels([gathered[g] for g in range(slabs)])
    total = jnp.zeros((PACKED, BZ), F32)
    for p in range(slabs):
        low = gathered[p, :, CORNER : CORNER + 1]
        high = gathered[p, :, HALF + CORNER : HALF + CORNER + 1]
        sign = sign_of(jnp.int32(p), place[0], slabs)
        total = total + values[p] * jnp.where(lane < HALF, low, high) * sign
    total = jnp.concatenate([total, pltpu.roll(total, HALF, 1)], axis=0)
    total = jnp.where(iota((planes, BZ), 1) < CORNER, total, 0.0)
    back[pl.ds(EXTRA, planes, stride=BACK), :] = left_product(level_tables(planes)[1], total)


def line_kernel(gathered, after, mine, one, two, three, half, other, total, mask):
    place = own_place()
    del after
    wanted = [gathered[0, 0:1, :]]
    for level in range(4):
        slab = ((place[0] >> (level + 1)) << (level + 1)) + (1 << level)
        wanted.append(gathered[jnp.minimum(slab, gathered.shape[0] - 1), 0:1, :])
    wanted += [jnp.zeros((1, BZ), F32)] * (8 - len(wanted))
    wanted = jnp.concatenate(wanted, axis=0).astype(BF16)
    mask[...] = jnp.dot(wanted, pick_table(LINE_KEPT, mask.shape[1]), preferred_element_type=F32)
    for chunk in range(CHUNKS):
        span = slice(chunk * BY, (chunk + 1) * BY)
        lanes = slice(chunk % ZB * BZ, (chunk % ZB + 1) * BZ)
        near, far = mine[span, :] + one[span, :], two[span, :] + three[span, :]
        result = (mine[span, :] - one[span, :]) * 0.5 * mask[1:2, lanes]
        result = result + (near - far) * 0.25 * mask[2:3, lanes]
        result = result + (half[span, :] - other[span, :]) * 0.5 * mask[3:4, lanes]
        total[span, :] = result


def finish_kernel(got, mine, other, partial, mask, detail, velocity, out_hbm, rows, line, out, sems):
    planes = got.shape[0] // BACK
    parts, cells, wide = velocity.shape
    inverse = level_tables(planes)[1]
    extra = got[pl.ds(EXTRA, planes, stride=BACK), :]
    slot, lane = iota((8, BZ), 0), iota((8, BZ), 1)
    turned = [
        pltpu.roll(extra[zb * 8 : (zb + 1) * 8], 0, 1, stride=SLICE, stride_axis=0)
        for zb in range(ZB)
    ]
    for c in range(parts):
        columns = []
        for zb in range(ZB):
            span = slice((c * ZB + zb) * BY, (c * ZB + zb + 1) * BY)
            lanes = slice(zb * BZ, (zb + 1) * BZ)
            last = (mine[span, :] - other[span, :]) * 0.5
            mean = (mine[span, :] + other[span, :]) * 0.5
            total = partial[span, :] + last * mask[4:5, lanes] + mean * mask[0:1, lanes]
            line[c * BY : (c + 1) * BY, lanes] = total
            corner = jnp.where(lane >> 4 == (slot + c) & 7, turned[zb], 0.0)
            corner = jnp.sum(corner, axis=0, keepdims=True)
            corner = pltpu.roll(corner, BZ - c * SLICE, 1) if c else corner
            data = got[pl.ds(c * ZB + zb, planes, stride=BACK), :]
            columns.append(jnp.where(iota((planes, BZ), 0) == 0, corner, data))
        rows[c * planes : (c + 1) * planes, :] = left_product(
            inverse, jnp.concatenate(columns, axis=1)
        )
    unmix = unmix_table(wide)
    line[...] = remix(line[...], unmix)
    rows[...] = remix(rows[...], unmix)
    copies = []
    for x in range(planes):
        span = slice(x * BY, (x + 1) * BY)
        smooth = [
            detail[c, span, :]
            + rows[c * planes + x : c * planes + x + 1, :]
            + line[c * BY : (c + 1) * BY, :]
            for c in range(parts)
        ]
        speed = [velocity[c, span, :].astype(F32) for c in range(parts)]
        for c in range(parts):
            a, b = (c + 1) % parts, (c + 2) % parts
            out[c, span, :] = (smooth[a] * speed[b] - smooth[b] * speed[a]).astype(BF16)
        if (x + 1) % 8 == 0:
            done = pl.ds((x - 7) * BY, 8 * BY)
            for c in range(parts):
                copies.append(
                    pltpu.make_async_copy(
                        out.at[c, done, :], out_hbm.at[c, done, :], sems.at[len(copies)]
                    )
                )
                copies[-1].start()
    for copy in copies:
        copy.wait()


def exchange(value, axis):
    return lax.all_to_all(value, axis, split_axis=0, concat_axis=0, tiled=True)


def over_yz(rows, planes):
    moved = exchange(rows.reshape(planes, -1, 1, BZ), "yz")
    return moved.reshape(rows.shape)


def from_partner(value, distance):
    if distance >= lax.axis_size("gx"):
        return value
    pairs = [(source, source ^ distance) for source in range(lax.axis_size("gx"))]
    return lax.ppermute(value, "gx", pairs)


def body(vorticity, velocity, blocks, counts):
    parts, planes, tall, wide = vorticity.shape
    cells = planes * tall
    slabs = lax.axis_size("gx")
    vmem = pl.BlockSpec(memory_space=pltpu.VMEM)
    loose = pl.BlockSpec(memory_space=pl.ANY)
    params = pltpu.CompilerParams(vmem_limit_bytes=32 * 1024 * 1024)
    vort = vorticity.reshape(parts, cells, wide)
    line_shape = (CHUNKS * BY, BZ)

    def array(*shape):
        return jax.ShapeDtypeStruct(shape, F32)

    def call(kernel, name, out_shape, in_specs, scratch=(), cost=None, params=params, out=vmem):
        many = isinstance(out_shape, tuple)
        return pl.pallas_call(
            kernel,
            out_shape=out_shape,
            in_specs=in_specs,
            out_specs=tuple(out for _ in out_shape) if many else out,
            scratch_shapes=list(scratch),
            compiler_params=params,
            cost_estimate=cost,
            name=name,
        )

    def cost(products):
        return pl.CostEstimate(
            flops=products * 2 * parts * cells * cells * wide,
            bytes_accessed=10 * parts * cells * wide,
            transcendentals=0,
        )

    vort_scratch = pltpu.VMEM((parts, cells, wide), BF16)
    send, line = call(
        head_kernel,
        "head",
        (array(planes * ROWS, BZ), array(*line_shape)),
        [loose] * 3,
        [
            pltpu.SMEM(counts.shape, jnp.int32),
            pltpu.VMEM(blocks.shape, jnp.int32),
            vort_scratch,
            pltpu.SemaphoreType.DMA((parts * PIECES + 2,)),
        ],
        params=pltpu.CompilerParams(vmem_limit_bytes=60 * 1024 * 1024),
    )(counts, blocks, vort)
    recv = over_yz(send, planes)
    near = [from_partner(line, distance) for distance in (1, 2, 3)]
    half = (line + near[0] + (near[1] + near[2])) * 0.25
    back, corner = call(
        plane_kernel,
        "plane",
        (array(planes * BACK, BZ), array(slabs, PACKED, BZ)),
        [vmem, loose],
    )(recv, half)
    gathered = exchange(corner, "gx")
    opposite = from_partner(half, 4)
    detail = call(
        details_kernel,
        "details",
        array(parts, cells, wide),
        [vmem, vmem, loose],
        cost=cost(7),
    )(recv, vort, corner)
    back, means = call(
        corner_kernel,
        "corner",
        (array(planes * BACK, BZ), array(*line_shape)),
        [vmem] * 4 + [loose],
    )(gathered, back, half, opposite, detail)
    got = over_yz(back, planes)
    other = from_partner(means, 8)
    partial, mask = call(
        line_kernel,
        "line",
        (array(*line_shape), array(8, wide)),
        [vmem, loose] + [vmem] * 6,
    )(gathered, means, line, *near, half, opposite)
    out = call(
        finish_kernel,
        "finish",
        jax.ShapeDtypeStruct((parts, cells, wide), BF16),
        [vmem] * 7,
        [
            pltpu.VMEM((parts * planes, wide), F32),
            pltpu.VMEM((parts * tall, wide), F32),
            pltpu.VMEM((parts, cells, wide), BF16),
            pltpu.SemaphoreType.DMA((parts * planes // 8,)),
        ],
        out=loose,
    )(got, means, other, partial, mask, detail, velocity.reshape(parts, cells, wide))
    return out.reshape(parts, planes, tall, wide)


def solution(mesh):
    return jax.shard_map(
        body,
        mesh=mesh,
        in_specs=(
            P(None, "gx", "yz", None),
            P(None, "gx", "yz", None),
            P(("gx", "yz"), None),
            P(("gx", "yz")),
        ),
        out_specs=P(None, "gx", "yz", None),
        check_vma=False,
    )
```

```python
import jax
import jax.numpy as jnp
from jax import lax
from jax.experimental import pallas as pl
from jax.experimental.pallas import tpu as pltpu
from jax.sharding import PartitionSpec as P


BY = 8
BZ = 128
ZB = 4
CHUNKS = 12
ROWS = 14
BACK = 13
EXTRA = 12
KEPT = 13
CORNER = 48
SLICE = 16
HALF = 64
LINE_KEPT = 52
PACKED = 16
PIECES = 4
F32 = jnp.float32
BF16 = jnp.bfloat16


def iota(shape, dimension):
    return lax.broadcasted_iota(jnp.int32, shape, dimension)


def sign_of(place, cell, length):
    span = jnp.where(place == 0, length, 2 * (place & -place))
    sign = jnp.where((cell < place) | (place == 0), 1.0, -1.0)
    return jnp.where((cell ^ place) < span, sign, 0.0)


def weight_of(place, cell, length):
    span = jnp.where(place == 0, length, 2 * (place & -place))
    return sign_of(place, cell, length) / span.astype(F32)


def mix_table(wide):
    coarse = iota((8, BZ), 1)
    parts = []
    for block in range(wide // BZ):
        row = weight_of(jnp.minimum(coarse, ZB - 1), jnp.int32(block), ZB)
        row = jnp.where(coarse < ZB, row - jnp.where(coarse == block, 1.0, 0.0), 0.0) / BZ
        parts.append(jnp.broadcast_to(row[0:1], (BZ, BZ)))
    return jnp.concatenate(parts, axis=0).astype(BF16)


def unmix_table(wide):
    block = iota((8, BZ), 1)
    parts = []
    for coarse in range(wide // BZ):
        row = sign_of(jnp.int32(coarse), jnp.minimum(block, ZB - 1), ZB)
        row = jnp.where(block < ZB, row - jnp.where(block == coarse, 1.0, 0.0), 0.0) / BZ
        parts.append(jnp.broadcast_to(row[0:1], (BZ, BZ)))
    return jnp.concatenate(parts, axis=0).astype(BF16)


def halves(value):
    high = value.astype(BF16)
    low = (value - high.astype(F32)).astype(BF16)
    return high, low


def left_product(table, value):
    high, low = halves(value)
    return jnp.dot(table, high, preferred_element_type=F32) + jnp.dot(
        table, low, preferred_element_type=F32
    )


def right_product(value, table):
    high, low = halves(value)
    return jnp.dot(high, table, preferred_element_type=F32) + jnp.dot(
        low, table, preferred_element_type=F32
    )


def remix(value, table):
    shift = right_product(value, table)
    return jnp.concatenate(
        [value[:, zb * BZ : (zb + 1) * BZ] + shift[:, zb : zb + 1] for zb in range(ZB)], axis=1
    )


def forward_levels(values):
    count = len(values)
    result = [None] * count
    step = 1
    while step < count:
        for place in range(step, count, 2 * step):
            low, high = values[place - step], values[place]
            result[place] = (low - high) * 0.5
            values[place - step] = (low + high) * 0.5
        step *= 2
    result[0] = values[0]
    return result


def inverse_levels(values):
    count = len(values)
    values = list(values)
    step = count // 2
    while step >= 1:
        for place in range(step, count, 2 * step):
            mean, detail = values[place - step], values[place]
            values[place - step] = mean + detail
            values[place] = mean - detail
        step //= 2
    return values


def pick_table(first, wide):
    lane, cell = iota((BZ, wide), 0), iota((BZ, wide), 1)
    return jnp.where(lane == (first + (cell >> 7)) & (BZ - 1), 1.0, 0.0).astype(BF16)


def head_kernel(counts_hbm, blocks_hbm, vort_hbm, send, line, counts, blocks, vort, sems):
    parts, cells, wide = vort.shape
    planes = cells // BY
    lists = [
        pltpu.make_async_copy(blocks_hbm, blocks, sems.at[parts * PIECES]),
        pltpu.make_async_copy(counts_hbm, counts, sems.at[parts * PIECES + 1]),
    ]
    for copy in lists:
        copy.start()
    copies = []
    size = cells // PIECES
    for c in range(parts):
        for piece in range(PIECES):
            part = pl.ds(piece * size, size)
            copies.append(
                pltpu.make_async_copy(
                    vort_hbm.at[c, part, :], vort.at[c, part, :], sems.at[len(copies)]
                )
            )
            copies[-1].start()
    row, column = iota((planes + BY, cells), 0), iota((planes + BY, cells), 1)
    fine = jnp.where(row - planes == column & (BY - 1), 1.0, 0.0) - 1.0 / BY
    table = jnp.where(
        row < planes,
        weight_of(jnp.minimum(row, planes - 1), column >> 3, planes) * (1.0 / BY),
        fine * (1.0 / planes),
    ).astype(BF16)
    mix = mix_table(wide)
    for copy in lists:
        copy.wait()
    nblocks = blocks.shape[1]
    square = (nblocks, nblocks)
    listed = (blocks[...] == iota(square, 0)) & (iota(square, 1) < counts[0])
    kept = lax.dot_general(
        jnp.ones((planes, nblocks), BF16),
        jnp.where(listed, 1.0, 0.0).astype(BF16),
        (((1,), (1,)), ((), ())),
        preferred_element_type=F32,
    )
    send[pl.ds(KEPT, planes, stride=ROWS), :] = jnp.minimum(kept, 1.0)
    lane, turn = iota((8, BZ), 1), iota((8, BZ), 0)
    extra = [jnp.zeros((8, BZ), F32) for zb in range(ZB)]
    for c in range(parts):
        for piece in range(PIECES):
            copies[c * PIECES + piece].wait()
        rows = remix(jnp.dot(table, vort[c], preferred_element_type=F32), mix)
        for zb in range(ZB):
            chunk = c * ZB + zb
            part = rows[:, zb * BZ : (zb + 1) * BZ]
            send[pl.ds(chunk, planes, stride=ROWS), :] = part[0:planes]
            line[chunk * BY : (chunk + 1) * BY, :] = part[planes : planes + BY]
            turned = jnp.broadcast_to(part[0:1], (8, BZ))
            turned = pltpu.roll(turned, c * SLICE, 1) if c else turned
            extra[zb] = jnp.where(lane >> 4 == (7 - turn + c) & 7, turned, extra[zb])
    for zb in range(ZB):
        turned = pltpu.roll(extra[zb], 0, 1, stride=SLICE, stride_axis=0)
        turned = pltpu.roll(turned, SLICE, 1)
        for row in range(8):
            at = (zb * 8 + 7 - row) * ROWS + EXTRA
            send[at : at + 1, :] = turned[row : row + 1]


def own_place():
    return lax.axis_index("gx"), lax.axis_index("yz")


def level_tables(length):
    square = (length, length)
    forward = weight_of(iota(square, 0), iota(square, 1), length).astype(BF16)
    inverse = sign_of(iota(square, 1), iota(square, 0), length).astype(BF16)
    return forward, inverse


def pack_kernel(recv, after, corner):
    place = own_place()
    del after
    planes = recv.shape[0] // ROWS
    forward = level_tables(planes)[0]
    extra = recv[pl.ds(EXTRA, planes, stride=ROWS), :]
    lane = iota((PACKED, BZ), 1)
    row = iota((PACKED, BZ), 0)
    heads = recv[KEPT : KEPT + 1, :]
    first = 4 * row + (place[1] >> 3)
    low = jnp.sum(jnp.where(lane == first, heads, 0.0), axis=1, keepdims=True)
    high = jnp.sum(jnp.where(lane == first + HALF, heads, 0.0), axis=1, keepdims=True)
    levels = left_product(forward, extra)
    packed = levels[0:PACKED] + pltpu.roll(levels[PACKED:planes], HALF, 1)
    packed = jnp.where(lane == CORNER, low, packed)
    packed = jnp.where(lane == HALF + CORNER, high, packed)
    own = jnp.where(lane >> 2 == place[1], heads, 0.0).astype(BF16)
    source, target = iota((BZ, BZ), 0), iota((BZ, BZ), 1)
    slot = jnp.where(target == LINE_KEPT + (source & 3), 1.0, 0.0).astype(BF16)
    packed = packed + jnp.dot(own, slot, preferred_element_type=F32)
    for g in range(corner.shape[0]):
        corner[g] = packed


def plane_kernel(recv, after, back):
    place = own_place()
    del after
    planes = recv.shape[0] // ROWS
    forward, inverse = level_tables(planes)
    unmix = unmix_table(ZB * BZ)
    pick = jnp.where(iota((BZ, ZB * BZ), 0) & 3 == iota((BZ, ZB * BZ), 1) >> 7, 1.0, 0.0)
    own = recv[pl.ds(place[1] * ROWS + KEPT, 1), :]
    spread = jnp.where(iota((planes, BZ), 1) >> 2 == iota((planes, BZ), 0), own, 0.0)
    mask = jnp.dot(spread.astype(BF16), pick.astype(BF16), preferred_element_type=F32)
    for c in range(3):
        data = jnp.concatenate(
            [recv[pl.ds(c * ZB + zb, planes, stride=ROWS), :] for zb in range(ZB)], axis=1
        )
        data = remix(left_product(inverse, left_product(forward, data) * mask), unmix)
        for zb in range(ZB):
            back[pl.ds(c * ZB + zb, planes, stride=BACK), :] = data[:, zb * BZ : (zb + 1) * BZ]


def details_kernel(recv, vort, after, detail):
    place = own_place()
    del after
    parts, cells, wide = vort.shape
    planes = cells // BY
    row, column = iota((cells, planes), 0), iota((cells, planes), 1)
    span = jnp.maximum(2 * (column & -column), 1).astype(F32)
    tall = jnp.where((row >> 3 == column) & (column > 0), 1.0 / span, 0.0).astype(BF16)
    kept = recv[pl.ds(KEPT, planes, stride=ROWS), :].astype(BF16)
    kept = jnp.dot(tall, kept, preferred_element_type=F32).astype(BF16)
    mask = jnp.dot(kept, pick_table(ZB * place[1], wide), preferred_element_type=F32)
    row, column = iota((cells, cells), 0), iota((cells, cells), 1)
    same = row & (BY - 1) == column & (BY - 1)
    sign = sign_of(row >> 3, column >> 3, planes)
    forward = (sign * jnp.where(same, 1.0 - 1.0 / BY, -1.0 / BY)).astype(BF16)
    sign = sign_of(column >> 3, row >> 3, planes)
    inverse = jnp.where(same, sign, 0.0).astype(BF16)
    mix, unmix = mix_table(wide), unmix_table(wide)
    for c in range(parts):
        rows = remix(jnp.dot(forward, vort[c], preferred_element_type=F32), mix)
        detail[c] = remix(left_product(inverse, rows * mask), unmix)


def corner_kernel(gathered, back_in, mine, other, after, back, means):
    place = own_place()
    del after
    means[...] = (mine[...] + other[...]) * 0.5
    slabs = gathered.shape[0]
    planes = back.shape[0] // BACK
    lane = iota((PACKED, BZ), 1)
    back[...] = back_in[...]
    values = forward_levels([gathered[g] for g in range(slabs)])
    total = jnp.zeros((PACKED, BZ), F32)
    for p in range(slabs):
        low = gathered[p, :, CORNER : CORNER + 1]
        high = gathered[p, :, HALF + CORNER : HALF + CORNER + 1]
        sign = sign_of(jnp.int32(p), place[0], slabs)
        total = total + values[p] * jnp.where(lane < HALF, low, high) * sign
    total = jnp.concatenate([total, pltpu.roll(total, HALF, 1)], axis=0)
    total = jnp.where(iota((planes, BZ), 1) < CORNER, total, 0.0)
    back[pl.ds(EXTRA, planes, stride=BACK), :] = left_product(level_tables(planes)[1], total)


def line_kernel(gathered, after, mine, one, two, three, half, other, total, mask):
    place = own_place()
    del after
    wanted = [gathered[0, 0:1, :]]
    for level in range(4):
        slab = ((place[0] >> (level + 1)) << (level + 1)) + (1 << level)
        wanted.append(gathered[jnp.minimum(slab, gathered.shape[0] - 1), 0:1, :])
    wanted += [jnp.zeros((1, BZ), F32)] * (8 - len(wanted))
    wanted = jnp.concatenate(wanted, axis=0).astype(BF16)
    mask[...] = jnp.dot(wanted, pick_table(LINE_KEPT, mask.shape[1]), preferred_element_type=F32)
    for chunk in range(CHUNKS):
        span = slice(chunk * BY, (chunk + 1) * BY)
        lanes = slice(chunk % ZB * BZ, (chunk % ZB + 1) * BZ)
        near, far = mine[span, :] + one[span, :], two[span, :] + three[span, :]
        result = (mine[span, :] - one[span, :]) * 0.5 * mask[1:2, lanes]
        result = result + (near - far) * 0.25 * mask[2:3, lanes]
        result = result + (half[span, :] - other[span, :]) * 0.5 * mask[3:4, lanes]
        total[span, :] = result


def finish_kernel(got, mine, other, partial, mask, detail, velocity, out_hbm, rows, line, out, sems):
    planes = got.shape[0] // BACK
    parts, cells, wide = velocity.shape
    inverse = level_tables(planes)[1]
    extra = got[pl.ds(EXTRA, planes, stride=BACK), :]
    slot, lane = iota((8, BZ), 0), iota((8, BZ), 1)
    turned = [
        pltpu.roll(extra[zb * 8 : (zb + 1) * 8], 0, 1, stride=SLICE, stride_axis=0)
        for zb in range(ZB)
    ]
    for c in range(parts):
        columns = []
        for zb in range(ZB):
            span = slice((c * ZB + zb) * BY, (c * ZB + zb + 1) * BY)
            lanes = slice(zb * BZ, (zb + 1) * BZ)
            last = (mine[span, :] - other[span, :]) * 0.5
            mean = (mine[span, :] + other[span, :]) * 0.5
            total = partial[span, :] + last * mask[4:5, lanes] + mean * mask[0:1, lanes]
            corner = jnp.where(lane >> 4 == (slot + c) & 7, turned[zb], 0.0)
            corner = jnp.sum(corner, axis=0, keepdims=True)
            corner = pltpu.roll(corner, BZ - c * SLICE, 1) if c else corner
            line[c * BY : (c + 1) * BY, lanes] = total + corner
            data = got[pl.ds(c * ZB + zb, planes, stride=BACK), :]
            columns.append(jnp.where(iota((planes, BZ), 0) == 0, 0.0, data))
        rows[c * planes : (c + 1) * planes, :] = left_product(
            inverse, jnp.concatenate(columns, axis=1)
        )
    line[...] = remix(line[...], unmix_table(wide))
    copies = []
    for x in range(planes):
        span = slice(x * BY, (x + 1) * BY)
        smooth = [
            detail[c, span, :]
            + rows[c * planes + x : c * planes + x + 1, :]
            + line[c * BY : (c + 1) * BY, :]
            for c in range(parts)
        ]
        speed = [velocity[c, span, :].astype(F32) for c in range(parts)]
        for c in range(parts):
            a, b = (c + 1) % parts, (c + 2) % parts
            out[c, span, :] = (smooth[a] * speed[b] - smooth[b] * speed[a]).astype(BF16)
        if (x + 1) % 8 == 0:
            done = pl.ds((x - 7) * BY, 8 * BY)
            for c in range(parts):
                copies.append(
                    pltpu.make_async_copy(
                        out.at[c, done, :], out_hbm.at[c, done, :], sems.at[len(copies)]
                    )
                )
                copies[-1].start()
    for copy in copies:
        copy.wait()


def exchange(value, axis):
    return lax.all_to_all(value, axis, split_axis=0, concat_axis=0, tiled=True)


def over_yz(rows, planes):
    moved = exchange(rows.reshape(planes, -1, 1, BZ), "yz")
    return moved.reshape(rows.shape)


def from_partner(value, distance):
    if distance >= lax.axis_size("gx"):
        return value
    pairs = [(source, source ^ distance) for source in range(lax.axis_size("gx"))]
    return lax.ppermute(value, "gx", pairs)


def body(vorticity, velocity, blocks, counts):
    parts, planes, tall, wide = vorticity.shape
    cells = planes * tall
    slabs = lax.axis_size("gx")
    vmem = pl.BlockSpec(memory_space=pltpu.VMEM)
    loose = pl.BlockSpec(memory_space=pl.ANY)
    params = pltpu.CompilerParams(vmem_limit_bytes=32 * 1024 * 1024)
    vort = vorticity.reshape(parts, cells, wide)
    line_shape = (CHUNKS * BY, BZ)

    def array(*shape):
        return jax.ShapeDtypeStruct(shape, F32)

    def call(kernel, name, out_shape, in_specs, scratch=(), cost=None, params=params, out=vmem):
        many = isinstance(out_shape, tuple)
        return pl.pallas_call(
            kernel,
            out_shape=out_shape,
            in_specs=in_specs,
            out_specs=tuple(out for _ in out_shape) if many else out,
            scratch_shapes=list(scratch),
            compiler_params=params,
            cost_estimate=cost,
            name=name,
        )

    def cost(products):
        return pl.CostEstimate(
            flops=products * 2 * parts * cells * cells * wide,
            bytes_accessed=10 * parts * cells * wide,
            transcendentals=0,
        )

    vort_scratch = pltpu.VMEM((parts, cells, wide), BF16)
    send, line = call(
        head_kernel,
        "head",
        (array(planes * ROWS, BZ), array(*line_shape)),
        [loose] * 3,
        [
            pltpu.SMEM(counts.shape, jnp.int32),
            pltpu.VMEM(blocks.shape, jnp.int32),
            vort_scratch,
            pltpu.SemaphoreType.DMA((parts * PIECES + 2,)),
        ],
        params=pltpu.CompilerParams(vmem_limit_bytes=60 * 1024 * 1024),
    )(counts, blocks, vort)
    recv = over_yz(send, planes)
    near = [from_partner(line, distance) for distance in (1, 2, 3)]
    half = (line + near[0] + (near[1] + near[2])) * 0.25
    corner = call(pack_kernel, "pack", array(slabs, PACKED, BZ), [vmem, loose])(recv, half)
    gathered = exchange(corner, "gx")
    opposite = from_partner(half, 4)
    back = call(plane_kernel, "plane", array(planes * BACK, BZ), [vmem, loose])(recv, corner)
    detail = call(
        details_kernel,
        "details",
        array(parts, cells, wide),
        [vmem, vmem, loose],
        cost=cost(7),
    )(recv, vort, corner)
    back, means = call(
        corner_kernel,
        "corner",
        (array(planes * BACK, BZ), array(*line_shape)),
        [vmem] * 4 + [loose],
    )(gathered, back, half, opposite, detail)
    got = over_yz(back, planes)
    other = from_partner(means, 8)
    partial, mask = call(
        line_kernel,
        "line",
        (array(*line_shape), array(8, wide)),
        [vmem, loose] + [vmem] * 6,
    )(gathered, means, line, *near, half, opposite)
    out = call(
        finish_kernel,
        "finish",
        jax.ShapeDtypeStruct((parts, cells, wide), BF16),
        [vmem] * 7,
        [
            pltpu.VMEM((parts * planes, wide), F32),
            pltpu.VMEM((parts * tall, wide), F32),
            pltpu.VMEM((parts, cells, wide), BF16),
            pltpu.SemaphoreType.DMA((parts * planes // 8,)),
        ],
        out=loose,
    )(got, means, other, partial, mask, detail, velocity.reshape(parts, cells, wide))
    return out.reshape(parts, planes, tall, wide)


def solution(mesh):
    return jax.shard_map(
        body,
        mesh=mesh,
        in_specs=(
            P(None, "gx", "yz", None),
            P(None, "gx", "yz", None),
            P(("gx", "yz"), None),
            P(("gx", "yz")),
        ),
        out_specs=P(None, "gx", "yz", None),
        check_vma=False,
    )
```

```python
import jax
import jax.numpy as jnp
from jax import lax
from jax.experimental import pallas as pl
from jax.experimental.pallas import tpu as pltpu
from jax.sharding import PartitionSpec as P


BY = 8
BZ = 128
ZB = 4
CHUNKS = 12
ROWS = 14
BACK = 13
EXTRA = 12
KEPT = 13
CORNER = 48
SLICE = 16
HALF = 64
LINE_KEPT = 52
PACKED = 16
PIECES = 4
F32 = jnp.float32
BF16 = jnp.bfloat16


def iota(shape, dimension):
    return lax.broadcasted_iota(jnp.int32, shape, dimension)


def sign_of(place, cell, length):
    span = jnp.where(place == 0, length, 2 * (place & -place))
    sign = jnp.where((cell < place) | (place == 0), 1.0, -1.0)
    return jnp.where((cell ^ place) < span, sign, 0.0)


def weight_of(place, cell, length):
    span = jnp.where(place == 0, length, 2 * (place & -place))
    return sign_of(place, cell, length) / span.astype(F32)


def mix_table(wide):
    coarse = iota((8, BZ), 1)
    parts = []
    for block in range(wide // BZ):
        row = weight_of(jnp.minimum(coarse, ZB - 1), jnp.int32(block), ZB)
        row = jnp.where(coarse < ZB, row - jnp.where(coarse == block, 1.0, 0.0), 0.0) / BZ
        parts.append(jnp.broadcast_to(row[0:1], (BZ, BZ)))
    return jnp.concatenate(parts, axis=0).astype(BF16)


def unmix_table(wide):
    block = iota((8, BZ), 1)
    parts = []
    for coarse in range(wide // BZ):
        row = sign_of(jnp.int32(coarse), jnp.minimum(block, ZB - 1), ZB)
        row = jnp.where(block < ZB, row - jnp.where(block == coarse, 1.0, 0.0), 0.0) / BZ
        parts.append(jnp.broadcast_to(row[0:1], (BZ, BZ)))
    return jnp.concatenate(parts, axis=0).astype(BF16)


def halves(value):
    high = value.astype(BF16)
    low = (value - high.astype(F32)).astype(BF16)
    return high, low


def left_product(table, value):
    high, low = halves(value)
    return jnp.dot(table, high, preferred_element_type=F32) + jnp.dot(
        table, low, preferred_element_type=F32
    )


def right_product(value, table):
    high, low = halves(value)
    return jnp.dot(high, table, preferred_element_type=F32) + jnp.dot(
        low, table, preferred_element_type=F32
    )


def remix(value, table):
    shift = right_product(value, table)
    return jnp.concatenate(
        [value[:, zb * BZ : (zb + 1) * BZ] + shift[:, zb : zb + 1] for zb in range(ZB)], axis=1
    )


def forward_levels(values):
    count = len(values)
    result = [None] * count
    step = 1
    while step < count:
        for place in range(step, count, 2 * step):
            low, high = values[place - step], values[place]
            result[place] = (low - high) * 0.5
            values[place - step] = (low + high) * 0.5
        step *= 2
    result[0] = values[0]
    return result


def inverse_levels(values):
    count = len(values)
    values = list(values)
    step = count // 2
    while step >= 1:
        for place in range(step, count, 2 * step):
            mean, detail = values[place - step], values[place]
            values[place - step] = mean + detail
            values[place] = mean - detail
        step //= 2
    return values


def pick_table(first, wide):
    lane, cell = iota((BZ, wide), 0), iota((BZ, wide), 1)
    return jnp.where(lane == (first + (cell >> 7)) & (BZ - 1), 1.0, 0.0).astype(BF16)


def head_kernel(counts_hbm, blocks_hbm, vort_hbm, send, line, counts, blocks, vort, sems):
    parts, cells, wide = vort.shape
    planes = cells // BY
    lists = [
        pltpu.make_async_copy(blocks_hbm, blocks, sems.at[parts * PIECES]),
        pltpu.make_async_copy(counts_hbm, counts, sems.at[parts * PIECES + 1]),
    ]
    for copy in lists:
        copy.start()
    copies = []
    size = cells // PIECES
    for c in range(parts):
        for piece in range(PIECES):
            part = pl.ds(piece * size, size)
            copies.append(
                pltpu.make_async_copy(
                    vort_hbm.at[c, part, :], vort.at[c, part, :], sems.at[len(copies)]
                )
            )
            copies[-1].start()
    row, column = iota((planes + BY, cells), 0), iota((planes + BY, cells), 1)
    fine = jnp.where(row - planes == column & (BY - 1), 1.0, 0.0) - 1.0 / BY
    table = jnp.where(
        row < planes,
        weight_of(jnp.minimum(row, planes - 1), column >> 3, planes) * (1.0 / BY),
        fine * (1.0 / planes),
    ).astype(BF16)
    mix = mix_table(wide)
    for copy in lists:
        copy.wait()
    nblocks = blocks.shape[1]
    square = (nblocks, nblocks)
    listed = (blocks[...] == iota(square, 0)) & (iota(square, 1) < counts[0])
    kept = lax.dot_general(
        jnp.ones((planes, nblocks), BF16),
        jnp.where(listed, 1.0, 0.0).astype(BF16),
        (((1,), (1,)), ((), ())),
        preferred_element_type=F32,
    )
    send[pl.ds(KEPT, planes, stride=ROWS), :] = jnp.minimum(kept, 1.0)
    lane, turn = iota((8, BZ), 1), iota((8, BZ), 0)
    extra = [jnp.zeros((8, BZ), F32) for zb in range(ZB)]
    for c in range(parts):
        for piece in range(PIECES):
            copies[c * PIECES + piece].wait()
        rows = remix(jnp.dot(table, vort[c], preferred_element_type=F32), mix)
        for zb in range(ZB):
            chunk = c * ZB + zb
            part = rows[:, zb * BZ : (zb + 1) * BZ]
            send[pl.ds(chunk, planes, stride=ROWS), :] = part[0:planes]
            line[chunk * BY : (chunk + 1) * BY, :] = part[planes : planes + BY]
            turned = jnp.broadcast_to(part[0:1], (8, BZ))
            turned = pltpu.roll(turned, c * SLICE, 1) if c else turned
            extra[zb] = jnp.where(lane >> 4 == (7 - turn + c) & 7, turned, extra[zb])
    for zb in range(ZB):
        turned = pltpu.roll(extra[zb], 0, 1, stride=SLICE, stride_axis=0)
        turned = pltpu.roll(turned, SLICE, 1)
        for row in range(8):
            at = (zb * 8 + 7 - row) * ROWS + EXTRA
            send[at : at + 1, :] = turned[row : row + 1]


def own_place():
    return lax.axis_index("gx"), lax.axis_index("yz")


def level_tables(length):
    square = (length, length)
    forward = weight_of(iota(square, 0), iota(square, 1), length).astype(BF16)
    inverse = sign_of(iota(square, 1), iota(square, 0), length).astype(BF16)
    return forward, inverse


def plane_kernel(recv, mine, one, two, three, back, corner, half):
    place = own_place()
    planes = recv.shape[0] // ROWS
    forward, inverse = level_tables(planes)
    extra = recv[pl.ds(EXTRA, planes, stride=ROWS), :]
    lane = iota((PACKED, BZ), 1)
    row = iota((PACKED, BZ), 0)
    heads = recv[KEPT : KEPT + 1, :]
    first = 4 * row + (place[1] >> 3)
    low = jnp.sum(jnp.where(lane == first, heads, 0.0), axis=1, keepdims=True)
    high = jnp.sum(jnp.where(lane == first + HALF, heads, 0.0), axis=1, keepdims=True)
    levels = left_product(forward, extra)
    packed = levels[0:PACKED] + pltpu.roll(levels[PACKED:planes], HALF, 1)
    packed = jnp.where(lane == CORNER, low, packed)
    packed = jnp.where(lane == HALF + CORNER, high, packed)
    own = jnp.where(lane >> 2 == place[1], heads, 0.0).astype(BF16)
    source, target = iota((BZ, BZ), 0), iota((BZ, BZ), 1)
    slot = jnp.where(target == LINE_KEPT + (source & 3), 1.0, 0.0).astype(BF16)
    packed = packed + jnp.dot(own, slot, preferred_element_type=F32)
    for g in range(corner.shape[0]):
        corner[g] = packed
    half[...] = (mine[...] + one[...] + (two[...] + three[...])) * 0.25
    pick = jnp.where(iota((BZ, ZB * BZ), 0) & 3 == iota((BZ, ZB * BZ), 1) >> 7, 1.0, 0.0)
    own = recv[pl.ds(place[1] * ROWS + KEPT, 1), :]
    spread = jnp.where(iota((planes, BZ), 1) >> 2 == iota((planes, BZ), 0), own, 0.0)
    mask = jnp.dot(spread.astype(BF16), pick.astype(BF16), preferred_element_type=F32)
    for c in range(3):
        data = jnp.concatenate(
            [recv[pl.ds(c * ZB + zb, planes, stride=ROWS), :] for zb in range(ZB)], axis=1
        )
        data = left_product(inverse, left_product(forward, data) * mask)
        for zb in range(ZB):
            back[pl.ds(c * ZB + zb, planes, stride=BACK), :] = data[:, zb * BZ : (zb + 1) * BZ]


def details_kernel(recv, vort, after, detail):
    place = own_place()
    del after
    parts, cells, wide = vort.shape
    planes = cells // BY
    row, column = iota((cells, planes), 0), iota((cells, planes), 1)
    span = jnp.maximum(2 * (column & -column), 1).astype(F32)
    tall = jnp.where((row >> 3 == column) & (column > 0), 1.0 / span, 0.0).astype(BF16)
    kept = recv[pl.ds(KEPT, planes, stride=ROWS), :].astype(BF16)
    kept = jnp.dot(tall, kept, preferred_element_type=F32).astype(BF16)
    mask = jnp.dot(kept, pick_table(ZB * place[1], wide), preferred_element_type=F32)
    row, column = iota((cells, cells), 0), iota((cells, cells), 1)
    same = row & (BY - 1) == column & (BY - 1)
    sign = sign_of(row >> 3, column >> 3, planes)
    forward = (sign * jnp.where(same, 1.0 - 1.0 / BY, -1.0 / BY)).astype(BF16)
    sign = sign_of(column >> 3, row >> 3, planes)
    inverse = jnp.where(same, sign, 0.0).astype(BF16)
    mix, unmix = mix_table(wide), unmix_table(wide)
    for c in range(parts):
        rows = remix(jnp.dot(forward, vort[c], preferred_element_type=F32), mix)
        detail[c] = remix(left_product(inverse, rows * mask), unmix)


def corner_kernel(gathered, back_in, mine, other, after, back, means):
    place = own_place()
    del after
    means[...] = (mine[...] + other[...]) * 0.5
    slabs = gathered.shape[0]
    planes = back.shape[0] // BACK
    lane = iota((PACKED, BZ), 1)
    back[...] = back_in[...]
    values = forward_levels([gathered[g] for g in range(slabs)])
    total = jnp.zeros((PACKED, BZ), F32)
    for p in range(slabs):
        low = gathered[p, :, CORNER : CORNER + 1]
        high = gathered[p, :, HALF + CORNER : HALF + CORNER + 1]
        sign = sign_of(jnp.int32(p), place[0], slabs)
        total = total + values[p] * jnp.where(lane < HALF, low, high) * sign
    total = jnp.concatenate([total, pltpu.roll(total, HALF, 1)], axis=0)
    total = jnp.where(iota((planes, BZ), 1) < CORNER, total, 0.0)
    back[pl.ds(EXTRA, planes, stride=BACK), :] = left_product(level_tables(planes)[1], total)


def line_kernel(gathered, after, mine, one, two, three, half, other, total, mask):
    place = own_place()
    del after
    wanted = [gathered[0, 0:1, :]]
    for level in range(4):
        slab = ((place[0] >> (level + 1)) << (level + 1)) + (1 << level)
        wanted.append(gathered[jnp.minimum(slab, gathered.shape[0] - 1), 0:1, :])
    wanted += [jnp.zeros((1, BZ), F32)] * (8 - len(wanted))
    wanted = jnp.concatenate(wanted, axis=0).astype(BF16)
    mask[...] = jnp.dot(wanted, pick_table(LINE_KEPT, mask.shape[1]), preferred_element_type=F32)
    for chunk in range(CHUNKS):
        span = slice(chunk * BY, (chunk + 1) * BY)
        lanes = slice(chunk % ZB * BZ, (chunk % ZB + 1) * BZ)
        near, far = mine[span, :] + one[span, :], two[span, :] + three[span, :]
        result = (mine[span, :] - one[span, :]) * 0.5 * mask[1:2, lanes]
        result = result + (near - far) * 0.25 * mask[2:3, lanes]
        result = result + (half[span, :] - other[span, :]) * 0.5 * mask[3:4, lanes]
        total[span, :] = result


def finish_kernel(got, mine, other, partial, mask, detail, velocity, out_hbm, rows, line, out, sems):
    planes = got.shape[0] // BACK
    parts, cells, wide = velocity.shape
    inverse = level_tables(planes)[1]
    extra = got[pl.ds(EXTRA, planes, stride=BACK), :]
    slot, lane = iota((8, BZ), 0), iota((8, BZ), 1)
    turned = [
        pltpu.roll(extra[zb * 8 : (zb + 1) * 8], 0, 1, stride=SLICE, stride_axis=0)
        for zb in range(ZB)
    ]
    for c in range(parts):
        columns = []
        for zb in range(ZB):
            span = slice((c * ZB + zb) * BY, (c * ZB + zb + 1) * BY)
            lanes = slice(zb * BZ, (zb + 1) * BZ)
            last = (mine[span, :] - other[span, :]) * 0.5
            mean = (mine[span, :] + other[span, :]) * 0.5
            total = partial[span, :] + last * mask[4:5, lanes] + mean * mask[0:1, lanes]
            line[c * BY : (c + 1) * BY, lanes] = total
            corner = jnp.where(lane >> 4 == (slot + c) & 7, turned[zb], 0.0)
            corner = jnp.sum(corner, axis=0, keepdims=True)
            corner = pltpu.roll(corner, BZ - c * SLICE, 1) if c else corner
            data = got[pl.ds(c * ZB + zb, planes, stride=BACK), :]
            columns.append(jnp.where(iota((planes, BZ), 0) == 0, corner, data))
        rows[c * planes : (c + 1) * planes, :] = left_product(
            inverse, jnp.concatenate(columns, axis=1)
        )
    unmix = unmix_table(wide)
    line[...] = remix(line[...], unmix)
    rows[...] = remix(rows[...], unmix)
    copies = []
    for x in range(planes):
        span = slice(x * BY, (x + 1) * BY)
        smooth = [
            detail[c, span, :]
            + rows[c * planes + x : c * planes + x + 1, :]
            + line[c * BY : (c + 1) * BY, :]
            for c in range(parts)
        ]
        speed = [velocity[c, span, :].astype(F32) for c in range(parts)]
        for c in range(parts):
            a, b = (c + 1) % parts, (c + 2) % parts
            out[c, span, :] = (smooth[a] * speed[b] - smooth[b] * speed[a]).astype(BF16)
        if (x + 1) % 8 == 0:
            done = pl.ds((x - 7) * BY, 8 * BY)
            for c in range(parts):
                copies.append(
                    pltpu.make_async_copy(
                        out.at[c, done, :], out_hbm.at[c, done, :], sems.at[len(copies)]
                    )
                )
                copies[-1].start()
    for copy in copies:
        copy.wait()


def exchange(value, axis):
    return lax.all_to_all(value, axis, split_axis=0, concat_axis=0, tiled=True)


def over_yz(rows, planes):
    moved = exchange(rows.reshape(planes, -1, 1, BZ), "yz")
    return moved.reshape(rows.shape)


def from_partner(value, distance):
    if distance >= lax.axis_size("gx"):
        return value
    pairs = [(source, source ^ distance) for source in range(lax.axis_size("gx"))]
    return lax.ppermute(value, "gx", pairs)


def body(vorticity, velocity, blocks, counts):
    parts, planes, tall, wide = vorticity.shape
    cells = planes * tall
    slabs = lax.axis_size("gx")
    vmem = pl.BlockSpec(memory_space=pltpu.VMEM)
    loose = pl.BlockSpec(memory_space=pl.ANY)
    params = pltpu.CompilerParams(vmem_limit_bytes=32 * 1024 * 1024)
    vort = vorticity.reshape(parts, cells, wide)
    line_shape = (CHUNKS * BY, BZ)

    def array(*shape):
        return jax.ShapeDtypeStruct(shape, F32)

    def call(kernel, name, out_shape, in_specs, scratch=(), cost=None, params=params, out=vmem):
        many = isinstance(out_shape, tuple)
        return pl.pallas_call(
            kernel,
            out_shape=out_shape,
            in_specs=in_specs,
            out_specs=tuple(out for _ in out_shape) if many else out,
            scratch_shapes=list(scratch),
            compiler_params=params,
            cost_estimate=cost,
            name=name,
        )

    def cost(products):
        return pl.CostEstimate(
            flops=products * 2 * parts * cells * cells * wide,
            bytes_accessed=10 * parts * cells * wide,
            transcendentals=0,
        )

    vort_scratch = pltpu.VMEM((parts, cells, wide), BF16)
    send, line = call(
        head_kernel,
        "head",
        (array(planes * ROWS, BZ), array(*line_shape)),
        [loose] * 3,
        [
            pltpu.SMEM(counts.shape, jnp.int32),
            pltpu.VMEM(blocks.shape, jnp.int32),
            vort_scratch,
            pltpu.SemaphoreType.DMA((parts * PIECES + 2,)),
        ],
        params=pltpu.CompilerParams(vmem_limit_bytes=60 * 1024 * 1024),
    )(counts, blocks, vort)
    recv = over_yz(send, planes)
    near = [from_partner(line, distance) for distance in (1, 2, 3)]
    back, corner, half = call(
        plane_kernel,
        "plane",
        (array(planes * BACK, BZ), array(slabs, PACKED, BZ), array(*line_shape)),
        [vmem] * 5,
    )(recv, line, *near)
    gathered = exchange(corner, "gx")
    opposite = from_partner(half, 4)
    detail = call(
        details_kernel,
        "details",
        array(parts, cells, wide),
        [vmem, vmem, loose],
        cost=cost(7),
    )(recv, vort, corner)
    back, means = call(
        corner_kernel,
        "corner",
        (array(planes * BACK, BZ), array(*line_shape)),
        [vmem] * 4 + [loose],
    )(gathered, back, half, opposite, detail)
    got = over_yz(back, planes)
    other = from_partner(means, 8)
    partial, mask = call(
        line_kernel,
        "line",
        (array(*line_shape), array(8, wide)),
        [vmem, loose] + [vmem] * 6,
    )(gathered, means, line, *near, half, opposite)
    out = call(
        finish_kernel,
        "finish",
        jax.ShapeDtypeStruct((parts, cells, wide), BF16),
        [vmem] * 7,
        [
            pltpu.VMEM((parts * planes, wide), F32),
            pltpu.VMEM((parts * tall, wide), F32),
            pltpu.VMEM((parts, cells, wide), BF16),
            pltpu.SemaphoreType.DMA((parts * planes // 8,)),
        ],
        out=loose,
    )(got, means, other, partial, mask, detail, velocity.reshape(parts, cells, wide))
    return out.reshape(parts, planes, tall, wide)


def solution(mesh):
    return jax.shard_map(
        body,
        mesh=mesh,
        in_specs=(
            P(None, "gx", "yz", None),
            P(None, "gx", "yz", None),
            P(("gx", "yz"), None),
            P(("gx", "yz")),
        ),
        out_specs=P(None, "gx", "yz", None),
        check_vma=False,
    )
```

```python
import jax
import jax.numpy as jnp
from jax import lax
from jax.experimental import pallas as pl
from jax.experimental.pallas import tpu as pltpu
from jax.sharding import PartitionSpec as P


BY = 8
BZ = 128
ZB = 4
CHUNKS = 12
ROWS = 14
BACK = 13
EXTRA = 12
KEPT = 13
CORNER = 48
SLICE = 16
HALF = 64
LINE_KEPT = 52
PACKED = 16
PIECES = 4
F32 = jnp.float32
BF16 = jnp.bfloat16


def iota(shape, dimension):
    return lax.broadcasted_iota(jnp.int32, shape, dimension)


def sign_of(place, cell, length):
    span = jnp.where(place == 0, length, 2 * (place & -place))
    sign = jnp.where((cell < place) | (place == 0), 1.0, -1.0)
    return jnp.where((cell ^ place) < span, sign, 0.0)


def weight_of(place, cell, length):
    span = jnp.where(place == 0, length, 2 * (place & -place))
    return sign_of(place, cell, length) / span.astype(F32)


def mix_table(wide):
    coarse = iota((8, BZ), 1)
    parts = []
    for block in range(wide // BZ):
        row = weight_of(jnp.minimum(coarse, ZB - 1), jnp.int32(block), ZB)
        row = jnp.where(coarse < ZB, row - jnp.where(coarse == block, 1.0, 0.0), 0.0) / BZ
        parts.append(jnp.broadcast_to(row[0:1], (BZ, BZ)))
    return jnp.concatenate(parts, axis=0).astype(BF16)


def unmix_table(wide):
    block = iota((8, BZ), 1)
    parts = []
    for coarse in range(wide // BZ):
        row = sign_of(jnp.int32(coarse), jnp.minimum(block, ZB - 1), ZB)
        row = jnp.where(block < ZB, row - jnp.where(block == coarse, 1.0, 0.0), 0.0) / BZ
        parts.append(jnp.broadcast_to(row[0:1], (BZ, BZ)))
    return jnp.concatenate(parts, axis=0).astype(BF16)


def halves(value):
    high = value.astype(BF16)
    low = (value - high.astype(F32)).astype(BF16)
    return high, low


def left_product(table, value):
    high, low = halves(value)
    return jnp.dot(table, high, preferred_element_type=F32) + jnp.dot(
        table, low, preferred_element_type=F32
    )


def right_product(value, table):
    rows = value.shape[0]
    low = value - value.astype(BF16).astype(F32)
    stacked = jnp.concatenate([value, low], axis=0).astype(BF16)
    result = jnp.dot(stacked, table, preferred_element_type=F32)
    return result[0:rows] + result[rows:]


def remix(value, table):
    shift = right_product(value, table)
    return jnp.concatenate(
        [value[:, zb * BZ : (zb + 1) * BZ] + shift[:, zb : zb + 1] for zb in range(ZB)], axis=1
    )


def forward_levels(values):
    count = len(values)
    result = [None] * count
    step = 1
    while step < count:
        for place in range(step, count, 2 * step):
            low, high = values[place - step], values[place]
            result[place] = (low - high) * 0.5
            values[place - step] = (low + high) * 0.5
        step *= 2
    result[0] = values[0]
    return result


def inverse_levels(values):
    count = len(values)
    values = list(values)
    step = count // 2
    while step >= 1:
        for place in range(step, count, 2 * step):
            mean, detail = values[place - step], values[place]
            values[place - step] = mean + detail
            values[place] = mean - detail
        step //= 2
    return values


def pick_table(first, wide):
    lane, cell = iota((BZ, wide), 0), iota((BZ, wide), 1)
    return jnp.where(lane == (first + (cell >> 7)) & (BZ - 1), 1.0, 0.0).astype(BF16)


def head_kernel(counts_hbm, blocks_hbm, vort_hbm, send, line, counts, blocks, vort, sems):
    parts, cells, wide = vort.shape
    planes = cells // BY
    lists = [
        pltpu.make_async_copy(blocks_hbm, blocks, sems.at[parts * PIECES]),
        pltpu.make_async_copy(counts_hbm, counts, sems.at[parts * PIECES + 1]),
    ]
    for copy in lists:
        copy.start()
    copies = []
    size = cells // PIECES
    for c in range(parts):
        for piece in range(PIECES):
            part = pl.ds(piece * size, size)
            copies.append(
                pltpu.make_async_copy(
                    vort_hbm.at[c, part, :], vort.at[c, part, :], sems.at[len(copies)]
                )
            )
            copies[-1].start()
    row, column = iota((planes + BY, cells), 0), iota((planes + BY, cells), 1)
    fine = jnp.where(row - planes == column & (BY - 1), 1.0, 0.0) - 1.0 / BY
    table = jnp.where(
        row < planes,
        weight_of(jnp.minimum(row, planes - 1), column >> 3, planes) * (1.0 / BY),
        fine * (1.0 / planes),
    ).astype(BF16)
    mix = mix_table(wide)
    for copy in lists:
        copy.wait()
    nblocks = blocks.shape[1]
    square = (nblocks, nblocks)
    listed = (blocks[...] == iota(square, 0)) & (iota(square, 1) < counts[0])
    kept = lax.dot_general(
        jnp.ones((planes, nblocks), BF16),
        jnp.where(listed, 1.0, 0.0).astype(BF16),
        (((1,), (1,)), ((), ())),
        preferred_element_type=F32,
    )
    send[pl.ds(KEPT, planes, stride=ROWS), :] = jnp.minimum(kept, 1.0)
    lane, turn = iota((8, BZ), 1), iota((8, BZ), 0)
    extra = [jnp.zeros((8, BZ), F32) for zb in range(ZB)]
    for c in range(parts):
        for piece in range(PIECES):
            copies[c * PIECES + piece].wait()
        rows = remix(jnp.dot(table, vort[c], preferred_element_type=F32), mix)
        for zb in range(ZB):
            chunk = c * ZB + zb
            part = rows[:, zb * BZ : (zb + 1) * BZ]
            send[pl.ds(chunk, planes, stride=ROWS), :] = part[0:planes]
            line[chunk * BY : (chunk + 1) * BY, :] = part[planes : planes + BY]
            turned = jnp.broadcast_to(part[0:1], (8, BZ))
            turned = pltpu.roll(turned, c * SLICE, 1) if c else turned
            extra[zb] = jnp.where(lane >> 4 == (7 - turn + c) & 7, turned, extra[zb])
    for zb in range(ZB):
        turned = pltpu.roll(extra[zb], 0, 1, stride=SLICE, stride_axis=0)
        turned = pltpu.roll(turned, SLICE, 1)
        for row in range(8):
            at = (zb * 8 + 7 - row) * ROWS + EXTRA
            send[at : at + 1, :] = turned[row : row + 1]


def own_place():
    return lax.axis_index("gx"), lax.axis_index("yz")


def level_tables(length):
    square = (length, length)
    forward = weight_of(iota(square, 0), iota(square, 1), length).astype(BF16)
    inverse = sign_of(iota(square, 1), iota(square, 0), length).astype(BF16)
    return forward, inverse


def plane_kernel(recv, after, back, corner):
    place = own_place()
    del after
    planes = recv.shape[0] // ROWS
    forward, inverse = level_tables(planes)
    extra = recv[pl.ds(EXTRA, planes, stride=ROWS), :]
    lane = iota((PACKED, BZ), 1)
    row = iota((PACKED, BZ), 0)
    heads = recv[KEPT : KEPT + 1, :]
    first = 4 * row + (place[1] >> 3)
    low = jnp.sum(jnp.where(lane == first, heads, 0.0), axis=1, keepdims=True)
    high = jnp.sum(jnp.where(lane == first + HALF, heads, 0.0), axis=1, keepdims=True)
    levels = left_product(forward, extra)
    packed = levels[0:PACKED] + pltpu.roll(levels[PACKED:planes], HALF, 1)
    packed = jnp.where(lane == CORNER, low, packed)
    packed = jnp.where(lane == HALF + CORNER, high, packed)
    own = jnp.where(lane >> 2 == place[1], heads, 0.0).astype(BF16)
    source, target = iota((BZ, BZ), 0), iota((BZ, BZ), 1)
    slot = jnp.where(target == LINE_KEPT + (source & 3), 1.0, 0.0).astype(BF16)
    packed = packed + jnp.dot(own, slot, preferred_element_type=F32)
    for g in range(corner.shape[0]):
        corner[g] = packed
    pick = jnp.where(iota((BZ, ZB * BZ), 0) & 3 == iota((BZ, ZB * BZ), 1) >> 7, 1.0, 0.0)
    own = recv[pl.ds(place[1] * ROWS + KEPT, 1), :]
    spread = jnp.where(iota((planes, BZ), 1) >> 2 == iota((planes, BZ), 0), own, 0.0)
    mask = jnp.dot(spread.astype(BF16), pick.astype(BF16), preferred_element_type=F32)
    for c in range(3):
        data = jnp.concatenate(
            [recv[pl.ds(c * ZB + zb, planes, stride=ROWS), :] for zb in range(ZB)], axis=1
        )
        data = left_product(inverse, left_product(forward, data) * mask)
        for zb in range(ZB):
            back[pl.ds(c * ZB + zb, planes, stride=BACK), :] = data[:, zb * BZ : (zb + 1) * BZ]


def details_kernel(recv, vort, after, detail):
    place = own_place()
    del after
    parts, cells, wide = vort.shape
    planes = cells // BY
    row, column = iota((cells, planes), 0), iota((cells, planes), 1)
    span = jnp.maximum(2 * (column & -column), 1).astype(F32)
    tall = jnp.where((row >> 3 == column) & (column > 0), 1.0 / span, 0.0).astype(BF16)
    kept = recv[pl.ds(KEPT, planes, stride=ROWS), :].astype(BF16)
    kept = jnp.dot(tall, kept, preferred_element_type=F32).astype(BF16)
    mask = jnp.dot(kept, pick_table(ZB * place[1], wide), preferred_element_type=F32)
    row, column = iota((cells, cells), 0), iota((cells, cells), 1)
    same = row & (BY - 1) == column & (BY - 1)
    sign = sign_of(row >> 3, column >> 3, planes)
    forward = (sign * jnp.where(same, 1.0 - 1.0 / BY, -1.0 / BY)).astype(BF16)
    sign = sign_of(column >> 3, row >> 3, planes)
    inverse = jnp.where(same, sign, 0.0).astype(BF16)
    mix, unmix = mix_table(wide), unmix_table(wide)
    for c in range(parts):
        rows = remix(jnp.dot(forward, vort[c], preferred_element_type=F32), mix)
        detail[c] = remix(left_product(inverse, rows * mask), unmix)


def corner_kernel(gathered, back_in, mine, other, after, back, means):
    place = own_place()
    del after
    means[...] = (mine[...] + other[...]) * 0.5
    slabs = gathered.shape[0]
    planes = back.shape[0] // BACK
    lane = iota((PACKED, BZ), 1)
    back[...] = back_in[...]
    values = forward_levels([gathered[g] for g in range(slabs)])
    total = jnp.zeros((PACKED, BZ), F32)
    for p in range(slabs):
        low = gathered[p, :, CORNER : CORNER + 1]
        high = gathered[p, :, HALF + CORNER : HALF + CORNER + 1]
        sign = sign_of(jnp.int32(p), place[0], slabs)
        total = total + values[p] * jnp.where(lane < HALF, low, high) * sign
    total = jnp.concatenate([total, pltpu.roll(total, HALF, 1)], axis=0)
    total = jnp.where(iota((planes, BZ), 1) < CORNER, total, 0.0)
    back[pl.ds(EXTRA, planes, stride=BACK), :] = left_product(level_tables(planes)[1], total)


def line_kernel(gathered, after, mine, one, two, three, half, other, total, mask):
    place = own_place()
    del after
    wanted = [gathered[0, 0:1, :]]
    for level in range(4):
        slab = ((place[0] >> (level + 1)) << (level + 1)) + (1 << level)
        wanted.append(gathered[jnp.minimum(slab, gathered.shape[0] - 1), 0:1, :])
    wanted += [jnp.zeros((1, BZ), F32)] * (8 - len(wanted))
    wanted = jnp.concatenate(wanted, axis=0).astype(BF16)
    mask[...] = jnp.dot(wanted, pick_table(LINE_KEPT, mask.shape[1]), preferred_element_type=F32)
    for chunk in range(CHUNKS):
        span = slice(chunk * BY, (chunk + 1) * BY)
        lanes = slice(chunk % ZB * BZ, (chunk % ZB + 1) * BZ)
        near, far = mine[span, :] + one[span, :], two[span, :] + three[span, :]
        result = (mine[span, :] - one[span, :]) * 0.5 * mask[1:2, lanes]
        result = result + (near - far) * 0.25 * mask[2:3, lanes]
        result = result + (half[span, :] - other[span, :]) * 0.5 * mask[3:4, lanes]
        total[span, :] = result


def finish_kernel(got, mine, other, partial, mask, detail, velocity, out_hbm, rows, line, out, sems):
    planes = got.shape[0] // BACK
    parts, cells, wide = velocity.shape
    inverse = level_tables(planes)[1]
    extra = got[pl.ds(EXTRA, planes, stride=BACK), :]
    slot, lane = iota((8, BZ), 0), iota((8, BZ), 1)
    turned = [
        pltpu.roll(extra[zb * 8 : (zb + 1) * 8], 0, 1, stride=SLICE, stride_axis=0)
        for zb in range(ZB)
    ]
    for c in range(parts):
        columns = []
        for zb in range(ZB):
            span = slice((c * ZB + zb) * BY, (c * ZB + zb + 1) * BY)
            lanes = slice(zb * BZ, (zb + 1) * BZ)
            last = (mine[span, :] - other[span, :]) * 0.5
            mean = (mine[span, :] + other[span, :]) * 0.5
            total = partial[span, :] + last * mask[4:5, lanes] + mean * mask[0:1, lanes]
            line[c * BY : (c + 1) * BY, lanes] = total
            corner = jnp.where(lane >> 4 == (slot + c) & 7, turned[zb], 0.0)
            corner = jnp.sum(corner, axis=0, keepdims=True)
            corner = pltpu.roll(corner, BZ - c * SLICE, 1) if c else corner
            data = got[pl.ds(c * ZB + zb, planes, stride=BACK), :]
            columns.append(jnp.where(iota((planes, BZ), 0) == 0, corner, data))
        rows[c * planes : (c + 1) * planes, :] = left_product(
            inverse, jnp.concatenate(columns, axis=1)
        )
    unmix = unmix_table(wide)
    line[...] = remix(line[...], unmix)
    rows[...] = remix(rows[...], unmix)
    copies = []
    for x in range(planes):
        span = slice(x * BY, (x + 1) * BY)
        smooth = [
            detail[c, span, :]
            + rows[c * planes + x : c * planes + x + 1, :]
            + line[c * BY : (c + 1) * BY, :]
            for c in range(parts)
        ]
        speed = [velocity[c, span, :].astype(F32) for c in range(parts)]
        for c in range(parts):
            a, b = (c + 1) % parts, (c + 2) % parts
            out[c, span, :] = (smooth[a] * speed[b] - smooth[b] * speed[a]).astype(BF16)
        if (x + 1) % 8 == 0:
            done = pl.ds((x - 7) * BY, 8 * BY)
            for c in range(parts):
                copies.append(
                    pltpu.make_async_copy(
                        out.at[c, done, :], out_hbm.at[c, done, :], sems.at[len(copies)]
                    )
                )
                copies[-1].start()
    for copy in copies:
        copy.wait()


def exchange(value, axis):
    return lax.all_to_all(value, axis, split_axis=0, concat_axis=0, tiled=True)


def over_yz(rows, planes):
    moved = exchange(rows.reshape(planes, -1, 1, BZ), "yz")
    return moved.reshape(rows.shape)


def from_partner(value, distance):
    if distance >= lax.axis_size("gx"):
        return value
    pairs = [(source, source ^ distance) for source in range(lax.axis_size("gx"))]
    return lax.ppermute(value, "gx", pairs)


def body(vorticity, velocity, blocks, counts):
    parts, planes, tall, wide = vorticity.shape
    cells = planes * tall
    slabs = lax.axis_size("gx")
    vmem = pl.BlockSpec(memory_space=pltpu.VMEM)
    loose = pl.BlockSpec(memory_space=pl.ANY)
    params = pltpu.CompilerParams(vmem_limit_bytes=32 * 1024 * 1024)
    vort = vorticity.reshape(parts, cells, wide)
    line_shape = (CHUNKS * BY, BZ)

    def array(*shape):
        return jax.ShapeDtypeStruct(shape, F32)

    def call(kernel, name, out_shape, in_specs, scratch=(), cost=None, params=params, out=vmem):
        many = isinstance(out_shape, tuple)
        return pl.pallas_call(
            kernel,
            out_shape=out_shape,
            in_specs=in_specs,
            out_specs=tuple(out for _ in out_shape) if many else out,
            scratch_shapes=list(scratch),
            compiler_params=params,
            cost_estimate=cost,
            name=name,
        )

    def cost(products):
        return pl.CostEstimate(
            flops=products * 2 * parts * cells * cells * wide,
            bytes_accessed=10 * parts * cells * wide,
            transcendentals=0,
        )

    vort_scratch = pltpu.VMEM((parts, cells, wide), BF16)
    send, line = call(
        head_kernel,
        "head",
        (array(planes * ROWS, BZ), array(*line_shape)),
        [loose] * 3,
        [
            pltpu.SMEM(counts.shape, jnp.int32),
            pltpu.VMEM(blocks.shape, jnp.int32),
            vort_scratch,
            pltpu.SemaphoreType.DMA((parts * PIECES + 2,)),
        ],
        params=pltpu.CompilerParams(vmem_limit_bytes=60 * 1024 * 1024),
    )(counts, blocks, vort)
    recv = over_yz(send, planes)
    near = [from_partner(line, distance) for distance in (1, 2, 3)]
    half = (line + near[0] + (near[1] + near[2])) * 0.25
    back, corner = call(
        plane_kernel,
        "plane",
        (array(planes * BACK, BZ), array(slabs, PACKED, BZ)),
        [vmem, loose],
    )(recv, half)
    gathered = exchange(corner, "gx")
    opposite = from_partner(half, 4)
    detail = call(
        details_kernel,
        "details",
        array(parts, cells, wide),
        [vmem, vmem, loose],
        cost=cost(7),
    )(recv, vort, corner)
    back, means = call(
        corner_kernel,
        "corner",
        (array(planes * BACK, BZ), array(*line_shape)),
        [vmem] * 4 + [loose],
    )(gathered, back, half, opposite, detail)
    got = over_yz(back, planes)
    other = from_partner(means, 8)
    partial, mask = call(
        line_kernel,
        "line",
        (array(*line_shape), array(8, wide)),
        [vmem, loose] + [vmem] * 6,
    )(gathered, means, line, *near, half, opposite)
    out = call(
        finish_kernel,
        "finish",
        jax.ShapeDtypeStruct((parts, cells, wide), BF16),
        [vmem] * 7,
        [
            pltpu.VMEM((parts * planes, wide), F32),
            pltpu.VMEM((parts * tall, wide), F32),
            pltpu.VMEM((parts, cells, wide), BF16),
            pltpu.SemaphoreType.DMA((parts * planes // 8,)),
        ],
        out=loose,
    )(got, means, other, partial, mask, detail, velocity.reshape(parts, cells, wide))
    return out.reshape(parts, planes, tall, wide)


def solution(mesh):
    return jax.shard_map(
        body,
        mesh=mesh,
        in_specs=(
            P(None, "gx", "yz", None),
            P(None, "gx", "yz", None),
            P(("gx", "yz"), None),
            P(("gx", "yz")),
        ),
        out_specs=P(None, "gx", "yz", None),
        check_vma=False,
    )
```
